32 devices in a mesh: dp: 2 (over x), expert: 16 (over z, y, core).
Axes of the slice: x: 2, y: 2, z: 4, core: 2. Of those that a mesh axis runs over, the one named last changes fastest.
Arguments:
- tokens: bfloat16 [768, 2048], P(('dp', 'expert')), may hold values from -6 to 6
- out_grad: bfloat16 [768, 2048], P(('dp', 'expert')), may hold values from -0.59765625 to 0.59765625
- expert_ids: int32 [768, 8], P(('dp', 'expert')), may hold values from 0 to 15, all different within a row; in each aligned block of 24 rows (0 to 23, 24 to 47, ...) at most 16 rows name the same one
- router_weight: bfloat16 [2048, 16], replicated, may hold values from -0.1875 to 0.1875
- w_gate: bfloat16 [16, 2048, 768], P('expert'), may hold values from -0.125 to 0.125
- w_up: bfloat16 [16, 2048, 768], P('expert'), may hold values from -0.125 to 0.125
- w_down: bfloat16 [16, 768, 2048], P('expert'), may hold values from -0.21875 to 0.21875
Outputs:
- grad_tokens: bfloat16 [768, 2048], P(('dp', 'expert'))
- grad_router: float32 [2048, 16], replicated
- grad_gate: bfloat16 [16, 2048, 768], P('expert', 'dp')
- grad_up: bfloat16 [16, 2048, 768], P('expert', 'dp')
- grad_down: bfloat16 [16, 768, 2048], P('expert', 'dp')
The draws below stay inside these ranges and needn't reach their ends.
Inputs may be any that keep to these rules, and one draw needn't show every extreme that they name: `expert_ids`: each row names 8 different experts. Among the 24 tokens of one device (aligned blocks of rows), no expert is named by more than 16 tokens, and in some blocks one expert is named by exactly 16.
All inputs are finite; a program needn't handle non-finite values.
Results may differ from the reference program's by a relative error of at most 0.017.
Values may be sent and summed in bfloat16 or wider, within the bound.
No kernel may reach another device: no remote copies, remote signals or barrier semaphores. Data moves between devices by JAX's collectives and lax.ppermute only.
A program may use at most 128 MiB of HBM per device.

```python
import math
from functools import partial
import jax
import jax.numpy as jnp
import numpy as np
from jax import lax

D = 2048
FF = 768
TOP = 8
PASSES = 3
TOK_DEV = 24
EXPERTS = 16
CAP = 16
TOKENS = 768
N_DP = 2
N_EXPERT = 16


def level_of(rng, extent, split, least, top_value):
    def one(axis_at, parts):
        steps = jax.random.uniform(jax.random.fold_in(jax.random.fold_in(rng, 6), axis_at), (parts,), jnp.float32, least / len(split), top_value / len(split))
        return jnp.repeat(jnp.exp(steps), extent[axis_at] // parts).reshape((-1,) + (1,) * (len(extent) - axis_at - 1))

    level = one(*split[0])
    for cut in split[1:]:
        level = level * one(*cut)
    return level


def shared_out(stream_key, own, number, rows, number_of, top, reach, skew):
    sequence = jax.random.permutation(stream_key, number_of)
    packed, ordinary = shares(number_of, rows * top, reach, skew, True), shares(number_of, rows * top, reach, skew, False)
    places = jnp.arange(number_of)

    def named(lengths, offset_by):
        used = int((lengths > 0).sum())
        fixed = max(1, used // 4)
        shifted = fixed + (places - fixed + offset_by * (used - fixed)) % max(1, number_of - fixed)
        return jnp.zeros((number_of,), jnp.int32).at[sequence[jnp.where(places < fixed, places, shifted)]].set(jnp.asarray(lengths, jnp.int32))

    lengths = jnp.where(number % 4 == 0, named(packed, number // 4), named(ordinary, number - number // 4 - 1))
    mixed = jax.random.permutation(jax.random.fold_in(own, 3), number_of)
    giver, taker = mixed[0:number_of // 2 * 2:2], mixed[1:number_of // 2 * 2:2]
    slack = jnp.minimum(lengths[giver] - 1, reach - lengths[taker]) // 2
    slack = jnp.where((giver == sequence[0]) | (taker == sequence[0]) | (lengths[taker] == 0), 0, jnp.maximum(slack, 0))
    shifted = jax.random.randint(jax.random.fold_in(own, 4), (number_of // 2,), 0, 1 << 20) % (slack + 1)
    lengths = lengths.at[giver].add(-shifted).at[taker].add(shifted)
    labels = jnp.searchsorted(jnp.cumsum(lengths), jnp.arange(rows * top), side="right").astype(jnp.int32)
    listing = labels.reshape(top, rows).T
    listing = listing[jax.random.permutation(jax.random.fold_in(own, 1), rows)]
    offset_by = jax.random.randint(jax.random.fold_in(own, 2), (rows, 1), 0, top)
    return jnp.take_along_axis(listing, (jnp.arange(top)[None, :] + offset_by) % top, axis=1)


def shares(count, total, reach, skew, full):
    portions = [(1 << 20) // math.isqrt(grade ** skew) + 1 for grade in range(1, count + 1)]
    largest = reach if full else min(reach, max(-(-total // count), total * portions[0] // sum(portions)))
    least = 1 if total - largest >= count - 1 else 0
    holding, surplus = [largest] + [least] * (count - 1), total - largest - least * (count - 1)
    while surplus > 0:
        free = [i for i in range(1, count) if holding[i] < largest] or [i for i in range(1, count) if holding[i] < reach]
        mass, left = sum([portions[i] for i in free]), surplus
        for i in free:
            addition = min(reach - holding[i], max(1, left * portions[i] // mass), surplus)
            holding[i] = holding[i] + addition
            surplus = surplus - addition
    return np.array(holding)


def centred(key, extent, scale, most, pieces=(), held_as=jnp.bfloat16):
    drawn = scale * jax.random.normal(key, extent, jnp.float32)
    if pieces:
        drawn = drawn * level_of(key, extent, pieces, -0.22, 0.18)
    return jnp.clip(drawn, -most, most).astype(held_as)


def setup_inputs(seed: int = 0) -> dict:
    key_of = jax.random.split(jax.random.key(seed), 8)
    tokens = centred(key_of[0], (TOKENS, D), 1.0, 6.0, ((0, 32),))
    out_grad = centred(key_of[1], (TOKENS, D), 0.1, 0.59765625, ((0, 32),))
    expert_ids_keys = jax.random.split(jax.random.fold_in(key_of[2], 1), TOKENS // TOK_DEV)
    expert_ids_turns = jax.random.permutation(jax.random.fold_in(key_of[2], 3), TOKENS // TOK_DEV)
    expert_ids = jax.vmap(lambda own, number: shared_out(jax.random.fold_in(key_of[2], 2), own, number, TOK_DEV, EXPERTS, TOP, CAP, 2))(expert_ids_keys, expert_ids_turns).reshape((TOKENS, TOP))
    router_weight = centred(key_of[3], (D, EXPERTS), (D // 2) ** -0.5, 0.1875)
    w_gate = centred(key_of[4], (EXPERTS, D, FF), D ** -0.5, 0.125, ((0, 16),))
    w_up = centred(key_of[5], (EXPERTS, D, FF), D ** -0.5, 0.125, ((0, 16),))
    w_down = centred(key_of[6], (EXPERTS, FF, D), FF ** -0.5, 0.21875, ((0, 16),))
    return {"tokens": tokens, "out_grad": out_grad, "expert_ids": expert_ids, "router_weight": router_weight, "w_gate": w_gate, "w_up": w_up, "w_down": w_down}


def expert_rows(rows_in, rows_grad, weight_gate, weight_up, weight_down):
    gate_pre = jnp.dot(rows_in, weight_gate, preferred_element_type=jnp.float32)
    up_pre = jnp.dot(rows_in, weight_up, preferred_element_type=jnp.float32)
    sigmoid_gate = jax.nn.sigmoid(gate_pre)
    activation = gate_pre * sigmoid_gate
    hidden = activation * up_pre
    contract_cols = (((1,), (1,)), ((), ()))
    hidden_grad = lax.dot_general(rows_grad, weight_down, contract_cols, preferred_element_type=jnp.float32)
    score_grad = jnp.sum(hidden_grad * hidden, axis=1).astype(jnp.bfloat16)
    gate_grad = (hidden_grad * up_pre * sigmoid_gate * (1.0 + gate_pre * (1.0 - sigmoid_gate))).astype(jnp.bfloat16)
    up_grad = (hidden_grad * activation).astype(jnp.bfloat16)
    input_grad = lax.dot_general(gate_grad, weight_gate, contract_cols, preferred_element_type=jnp.float32)
    input_grad = input_grad + lax.dot_general(up_grad, weight_up, contract_cols, preferred_element_type=jnp.float32)
    return hidden.astype(jnp.bfloat16), gate_grad, up_grad, input_grad.astype(jnp.bfloat16), score_grad


def scaled_rows(gate_values, rows_grad, gate_grad, up_grad):
    gate_scale = gate_values.astype(jnp.float32)[:, None]
    return ((gate_scale * rows_grad).astype(jnp.bfloat16), (gate_scale * gate_grad).astype(jnp.bfloat16),
            (gate_scale * up_grad).astype(jnp.bfloat16))


def balancer_forward_pass(router_logit_rows):
    expert_density_rows = [jnp.exp(router_logit_rows)]
    division_ratios, column_totals, row_totals = [], [], []
    for repeat in range(PASSES):
        column_sum = jnp.sum(expert_density_rows[-1], axis=0)
        quotient = expert_density_rows[-1] / column_sum
        row_sum = jnp.sum(quotient, axis=1, keepdims=True)
        expert_density_rows.append(quotient / row_sum)
        division_ratios.append(quotient)
        column_totals.append(column_sum)
        row_totals.append(row_sum)
    return expert_density_rows, division_ratios, column_totals, row_totals


def balancer_adjoint_pass(density_gradient, expert_density_rows, division_ratios, column_totals, row_totals):
    for repeat in reversed(range(PASSES)):
        density = expert_density_rows[repeat + 1]
        quotient_grad = (density_gradient - jnp.sum(density_gradient * density, axis=1, keepdims=True)) / row_totals[repeat]
        shared = jnp.sum(quotient_grad * division_ratios[repeat], axis=0)
        density_gradient = (quotient_grad - shared) / column_totals[repeat]
    return density_gradient * expert_density_rows[0]


def one_group(expert, group_index, grouped_in, grouped_grad, picked_groups, gates_groups, sent_groups,
              w_gate, w_up, w_down):
    slot_total = N_EXPERT * CAP
    group_tokens = TOK_DEV * N_EXPERT
    route_mask = picked_groups[group_index][:, expert]
    route_count = jnp.sum(route_mask)
    positions = jnp.nonzero(route_mask, size=slot_total, fill_value=0)[0].astype(jnp.int32)
    live_slot = jnp.arange(slot_total, dtype=jnp.int32) < route_count
    zero_value = jnp.zeros((), jnp.bfloat16)
    rows_in = jnp.where(live_slot[:, None], grouped_in[group_index][positions], zero_value)
    rows_grad = jnp.where(live_slot[:, None], grouped_grad[group_index][positions], zero_value)
    gate_values = jnp.where(live_slot, sent_groups[group_index][positions, expert], zero_value)
    hidden, gate_grad, up_grad, input_grad, score_grad = expert_rows(
        rows_in, rows_grad, w_gate[expert], w_up[expert], w_down[expert])
    down_scaled, gate_scaled, up_scaled = scaled_rows(gate_values, rows_grad, gate_grad, up_grad)
    contract_rows = (((0,), (0,)), ((), ()))
    part_gate = lax.dot_general(rows_in, gate_scaled, contract_rows, preferred_element_type=jnp.float32)
    part_up = lax.dot_general(rows_in, up_scaled, contract_rows, preferred_element_type=jnp.float32)
    part_down = lax.dot_general(hidden, down_scaled, contract_rows, preferred_element_type=jnp.float32)
    gate_full = jnp.where(live_slot, gates_groups[group_index][positions, expert], 0.0)
    input_part = jnp.zeros((group_tokens, D), jnp.float32).at[positions].add(
        gate_full[:, None] * input_grad.astype(jnp.float32))
    score_part = jnp.zeros((group_tokens,), jnp.float32).at[positions].add(
        jnp.where(live_slot, score_grad.astype(jnp.float32), 0.0))
    return (input_part, score_part, part_gate.astype(jnp.bfloat16), part_up.astype(jnp.bfloat16),
            part_down.astype(jnp.bfloat16))


def reference(tokens, out_grad, expert_ids, router_weight, w_gate, w_up, w_down):
    router_logit_rows = jnp.dot(tokens, router_weight, preferred_element_type=jnp.float32)
    expert_density_rows, division_ratios, column_totals, row_totals = balancer_forward_pass(router_logit_rows)
    gate_matrix = EXPERTS * expert_density_rows[-1]
    expert_range = jnp.arange(EXPERTS, dtype=jnp.int32)
    picked = jnp.sum((expert_ids[:, :, None] == expert_range[None, None, :]).astype(jnp.int32), axis=1)
    group_tokens = TOK_DEV * N_EXPERT
    grouped_in = tokens.reshape(N_DP, group_tokens, D)
    grouped_grad = out_grad.reshape(N_DP, group_tokens, D)
    picked_groups = picked.reshape(N_DP, group_tokens, EXPERTS)
    gates_groups = gate_matrix.reshape(N_DP, group_tokens, EXPERTS)
    sent_groups = gate_matrix.astype(jnp.bfloat16).reshape(N_DP, group_tokens, EXPERTS)

    def one_expert(input_acc, expert):
        group_fn = partial(one_group, expert, grouped_in=grouped_in, grouped_grad=grouped_grad,
                           picked_groups=picked_groups, gates_groups=gates_groups, sent_groups=sent_groups,
                           w_gate=w_gate, w_up=w_up, w_down=w_down)
        input_part, score_part, part_gate, part_up, part_down = lax.map(
            group_fn, jnp.arange(N_DP, dtype=jnp.int32))
        grad_gate_one = jnp.sum(part_gate.astype(jnp.float32), axis=0).astype(jnp.bfloat16)
        grad_up_one = jnp.sum(part_up.astype(jnp.float32), axis=0).astype(jnp.bfloat16)
        grad_down_one = jnp.sum(part_down.astype(jnp.float32), axis=0).astype(jnp.bfloat16)
        return input_acc + input_part, (score_part.reshape(TOKENS), grad_gate_one, grad_up_one, grad_down_one)

    input_start = jnp.zeros((N_DP, group_tokens, D), jnp.float32)
    input_acc, (score_cols, grad_gate, grad_up, grad_down) = lax.scan(one_expert, input_start, expert_range)
    density_gradient = EXPERTS * score_cols.T
    logit_gradient = balancer_adjoint_pass(density_gradient, expert_density_rows, division_ratios, column_totals, row_totals).astype(jnp.bfloat16)
    grad_router = lax.dot_general(tokens, logit_gradient, (((0,), (0,)), ((), ())), preferred_element_type=jnp.float32)
    router_input = lax.dot_general(logit_gradient, router_weight, (((1,), (1,)), ((), ())),
                                   preferred_element_type=jnp.float32)
    grad_tokens = (input_acc.reshape(TOKENS, D) + router_input).astype(jnp.bfloat16)
    return grad_tokens, grad_router, grad_gate, grad_up, grad_down
```

```python
import jax
import jax.numpy as jnp
from jax import lax
from jax.sharding import PartitionSpec as P

PASSES = 3
LANES = 128


def swap_expert(array, offset):
    size = lax.axis_size("expert")
    return lax.ppermute(array, "expert", [(i, i ^ offset) for i in range(size)])


def swap_group(array, offset):
    size = lax.axis_size("dp")
    return lax.ppermute(array, "dp", [(i, i ^ offset) for i in range(size)])


def contract(left, right, left_dim, right_dim):
    return lax.dot_general(
        left, right, (((left_dim,), (right_dim,)), ((), ())), preferred_element_type=jnp.float32
    )


def expert_rows(rows_in, rows_grad, weight_gate, weight_up, weight_down):
    gate_pre = contract(rows_in, weight_gate, 1, 0)
    up_pre = contract(rows_in, weight_up, 1, 0)
    sigmoid_gate = jax.nn.sigmoid(gate_pre)
    activation = gate_pre * sigmoid_gate
    hidden = activation * up_pre
    hidden_grad = contract(rows_grad, weight_down, 1, 1)
    score = jnp.sum(hidden_grad * hidden, axis=1)
    gate_grad = hidden_grad * up_pre * sigmoid_gate * (1.0 + gate_pre * (1.0 - sigmoid_gate))
    up_grad = hidden_grad * activation
    return (
        hidden.astype(jnp.bfloat16),
        gate_grad.astype(jnp.bfloat16),
        up_grad.astype(jnp.bfloat16),
        score,
    )


def balancer_forward_pass(logits):
    densities = [jnp.exp(logits)]
    quotients, column_totals, row_totals = ([], [], [])
    for _ in range(PASSES):
        column_sum = jnp.sum(densities[-1], axis=1, keepdims=True)
        quotient = densities[-1] / column_sum
        row_sum = jnp.sum(quotient, axis=0, keepdims=True)
        densities.append(quotient / row_sum)
        quotients.append(quotient)
        column_totals.append(column_sum)
        row_totals.append(row_sum)
    return (densities, quotients, column_totals, row_totals)


def balancer_adjoint_pass(density_gradient, densities, quotients, column_totals, row_totals):
    for repeat in reversed(range(PASSES)):
        inner = jnp.sum(density_gradient * densities[repeat + 1], axis=0, keepdims=True)
        quotient_grad = (density_gradient - inner) / row_totals[repeat]
        shared = jnp.sum(quotient_grad * quotients[repeat], axis=1, keepdims=True)
        density_gradient = (quotient_grad - shared) / column_totals[repeat]
    return density_gradient * densities[0]


def per_device(tokens, out_grad, expert_ids, router_weight, w_gate, w_up, w_down):
    tok_rows, model_width = tokens.shape
    experts = router_weight.shape[1]
    groups = lax.axis_size("dp")
    far = lax.axis_size("expert") // 4
    chunk = 2 * far * tok_rows
    me = lax.axis_index("expert")
    my_group = lax.axis_index("dp")
    weight_gate, weight_up, weight_down = (w_gate[0], w_up[0], w_down[0])
    ff_width = weight_gate.shape[1]

    lane = jnp.arange(LANES, dtype=jnp.int32)
    picked = jnp.any(expert_ids[:, :, None] == lane[None, None, :], axis=1)
    packed = jnp.concatenate([tokens, out_grad, picked.astype(jnp.bfloat16)], axis=1)

    line = jnp.concatenate([packed] + [swap_expert(packed, k * 4) for k in range(1, far)], axis=0)
    line_next = swap_expert(line, 2)
    own = [
        jnp.concatenate([line, swap_expert(line, 1)], axis=0),
        jnp.concatenate([line_next, swap_expert(line_next, 1)], axis=0),
    ]
    logits_own = jnp.concatenate(
        [contract(router_weight, rows[:, :model_width], 0, 1) for rows in own], axis=1
    )
    logits = jnp.concatenate(
        [logits_own] + [swap_group(logits_own, offset) for offset in range(1, groups)], axis=1
    )
    state = balancer_forward_pass(logits)
    gates = experts * state[0][-1]
    my_gate = lax.dynamic_slice_in_dim(gates, me, 1, axis=0)[0]

    sums, scores, token_rows = ([], [], [])
    half = model_width // groups
    half_ff = ff_width // groups
    tie = None
    for index in range(2 * groups):
        if index < 2:
            rows = own[index]
        else:
            source = (line, line_next)[index % 2]
            if groups > 2 and tie is not None:
                source, tie = lax.optimization_barrier((source, tie))
            moved = swap_group(source, index // 2)
            rows = jnp.concatenate([moved, swap_expert(moved, 1)], axis=0)
        rows_in = rows[:, :model_width]
        rows_grad = rows[:, model_width : 2 * model_width]
        mask = jnp.sum(
            jnp.where(lane[None, :] == me, rows[:, 2 * model_width :].astype(jnp.float32), 0.0), axis=1
        )
        hidden, gate_grad, up_grad, score = expert_rows(
            rows_in, rows_grad, weight_gate, weight_up, weight_down
        )
        gate = (mask * my_gate[index * chunk : (index + 1) * chunk])[:, None]
        if index < 2:
            scores.append((score * mask).astype(jnp.bfloat16))
            part = contract(gate_grad, weight_gate, 1, 1) + contract(up_grad, weight_up, 1, 1)
            part = (gate * part).astype(jnp.bfloat16).reshape(2, far, tok_rows, model_width)
            near = part[0].astype(jnp.float32) + swap_expert(part[1], 1).astype(jnp.float32)
            total = near[0]
            near = near.astype(jnp.bfloat16)
            for k in range(1, far):
                total = total + swap_expert(near[k], k * 4).astype(jnp.float32)
            sums.append(total)
        sent = gate.astype(jnp.bfloat16).astype(jnp.float32)
        rows_half = lax.dynamic_slice_in_dim(rows_in, my_group * half, half, axis=1)
        hidden_half = lax.dynamic_slice_in_dim(hidden, my_group * half_ff, half_ff, axis=1)
        terms = (
            contract(rows_half, (sent * gate_grad).astype(jnp.bfloat16), 0, 0),
            contract(rows_half, (sent * up_grad).astype(jnp.bfloat16), 0, 0),
            contract(hidden_half, (sent * rows_grad).astype(jnp.bfloat16), 0, 0),
        )
        totals = terms if index == 0 else tuple(t + u for t, u in zip(totals, terms))
        token_rows.append(rows_in)
        tie = totals[0]
    row_sum = sums[0] + swap_expert(sums[1].astype(jnp.bfloat16), 2).astype(jnp.float32)

    grad_gate, grad_up, grad_down = (t.astype(jnp.bfloat16)[None] for t in totals)

    score = jnp.stack(scores).reshape(2, 2, far, tok_rows)
    from_far = [score]
    for k in range(1, far):
        got = swap_expert(score, k * 4)
        from_far.append(jnp.stack([got[:, :, j ^ k] for j in range(far)], axis=2))
    score = jnp.stack(from_far)
    score = jnp.stack([score, jnp.flip(swap_expert(score, 2), axis=1)], axis=1)
    score = jnp.stack([score, jnp.flip(swap_expert(score, 1), axis=3)], axis=2)
    score = score.reshape(experts, 2 * chunk)
    score = jnp.concatenate(
        [score] + [swap_group(score, offset) for offset in range(1, groups)], axis=1
    )
    order = jnp.arange(experts, dtype=jnp.int32)
    unswap = ((order[:, None] ^ me) == order[None, :]).astype(jnp.bfloat16)
    score = contract(unswap, score, 1, 0)
    logit_grad = balancer_adjoint_pass(experts * score, *state).astype(jnp.bfloat16)
    grad_router = sum(
        contract(rows, logit_grad[:, i * chunk : (i + 1) * chunk], 0, 1)
        for i, rows in enumerate(token_rows)
    )
    mine = logit_grad[:, :tok_rows]
    grad_tokens = (row_sum + contract(mine, router_weight, 0, 1)).astype(jnp.bfloat16)
    return (grad_tokens, grad_router, grad_gate, grad_up, grad_down)


def solution(mesh):
    in_specs = (
        P(("dp", "expert"), None),
        P(("dp", "expert"), None),
        P(("dp", "expert"), None),
        P(),
        P("expert", None, None),
        P("expert", None, None),
        P("expert", None, None),
    )
    out_specs = (
        P(("dp", "expert"), None),
        P(),
        P("expert", "dp", None),
        P("expert", "dp", None),
        P("expert", "dp", None),
    )
    return jax.shard_map(
        per_device, mesh=mesh, in_specs=in_specs, out_specs=out_specs, check_vma=False
    )
```

```python
import functools

import jax
import jax.numpy as jnp
from jax import lax
from jax.experimental import pallas as pl
from jax.experimental.pallas import tpu as pltpu
from jax.sharding import PartitionSpec as P

PASSES = 3
LANES = 128
SUBLANES = 8
FF_TILE = 256
MIB = 1 << 20
ROWS_AT_ONCE = 1024


def swap_expert(array, offset):
    size = lax.axis_size("expert")
    return lax.ppermute(array, "expert", [(i, i ^ offset) for i in range(size)])


def swap_group(array, offset):
    size = lax.axis_size("dp")
    return lax.ppermute(array, "dp", [(i, i ^ offset) for i in range(size)])


def contract(left, right, left_dim, right_dim):
    return lax.dot_general(
        left, right, (((left_dim,), (right_dim,)), ((), ())), preferred_element_type=jnp.float32
    )


def balancer_forward_pass(logits):
    densities = [jnp.exp(logits)]
    quotients, column_totals, row_totals = ([], [], [])
    for _ in range(PASSES):
        column_sum = jnp.sum(densities[-1], axis=1, keepdims=True)
        quotient = densities[-1] / column_sum
        row_sum = jnp.sum(quotient, axis=0, keepdims=True)
        densities.append(quotient / row_sum)
        quotients.append(quotient)
        column_totals.append(column_sum)
        row_totals.append(row_sum)
    return (densities, quotients, column_totals, row_totals)


def balancer_adjoint_pass(density_gradient, densities, quotients, column_totals, row_totals):
    for repeat in reversed(range(PASSES)):
        inner = jnp.sum(density_gradient * densities[repeat + 1], axis=0, keepdims=True)
        quotient_grad = (density_gradient - inner) / row_totals[repeat]
        shared = jnp.sum(quotient_grad * quotients[repeat], axis=1, keepdims=True)
        density_gradient = (quotient_grad - shared) / column_totals[repeat]
    return density_gradient * densities[0]


def gate_kernel(me_ref, logits_ref, gate_ref):
    logits = logits_ref[...]
    experts, count = logits.shape
    gates = experts * balancer_forward_pass(logits)[0][-1]
    row = lax.broadcasted_iota(jnp.int32, gates.shape, 0)
    mine = jnp.sum(jnp.where(row == me_ref[0], gates, 0.0), axis=0, keepdims=True)
    gate_ref[...] = jnp.transpose(jnp.broadcast_to(mine, (LANES, count)))


def adjoint_kernel(me_ref, logits_ref, score_ref, grad_ref):
    logits = logits_ref[...]
    experts = logits.shape[0]
    row = lax.broadcasted_iota(jnp.int32, (experts, experts), 0)
    column = lax.broadcasted_iota(jnp.int32, (experts, experts), 1)
    unswap = jnp.where((row ^ me_ref[0]) == column, 1.0, 0.0).astype(jnp.bfloat16)
    score = contract(unswap, score_ref[...], 1, 0)
    state = balancer_forward_pass(logits)
    grad_ref[...] = balancer_adjoint_pass(experts * score, *state).astype(jnp.bfloat16)


def small_call(kernel, me, operands, out_shape):
    whole = pl.BlockSpec(memory_space=pltpu.VMEM)
    return pl.pallas_call(
        kernel,
        in_specs=[pl.BlockSpec(memory_space=pltpu.SMEM)] + [whole] * len(operands),
        out_specs=whole,
        out_shape=out_shape,
        compiler_params=pltpu.CompilerParams(vmem_limit_bytes=32 * MIB),
        cost_estimate=pl.CostEstimate(flops=10**6, bytes_accessed=10**6, transcendentals=10**4),
    )(me, *operands)


def rows_kernel(parts, own, me_ref, *refs):
    tok_refs, grad_refs = (refs[:parts], refs[parts : 2 * parts])
    gate_ref, wg_ref, wu_ref, wd_ref = refs[2 * parts : 2 * parts + 4]
    tok_ref, grad_ref, hidden_ref, gs_ref, us_ref = refs[2 * parts + 4 : 2 * parts + 9]
    width = tok_ref.shape[1]
    if own:
        keep_ref, send_ref, score_ref, total_ref, mask_ref = refs[2 * parts + 9 :]
    else:
        (mask_ref,) = refs[2 * parts + 9 :]
    step = pl.program_id(0)

    @pl.when(step == 0)
    def _():
        at = 0
        for tok_part, grad_part in zip(tok_refs, grad_refs):
            rows = tok_part.shape[0]
            tok_ref[at : at + rows, :] = tok_part[...]
            grad_ref[at : at + rows, :] = grad_part[:, :width]
            picked = grad_part[:, width:].astype(jnp.float32)
            lane = lax.broadcasted_iota(jnp.int32, picked.shape, 1)
            mask = jnp.sum(jnp.where(lane == me_ref[0], picked, 0.0), axis=1, keepdims=True)
            mask_ref[at : at + rows, :] = jnp.broadcast_to(mask, (rows, LANES))
            at += rows

    rows_in, rows_grad = (tok_ref[...], grad_ref[...])
    wg, wu, wd = (wg_ref[0], wu_ref[0], wd_ref[0])
    gate_pre = contract(rows_in, wg, 1, 0)
    up_pre = contract(rows_in, wu, 1, 0)
    hidden_grad = contract(rows_grad, wd, 1, 1)
    sigmoid_gate = jax.nn.sigmoid(gate_pre)
    activation = gate_pre * sigmoid_gate
    hidden = activation * up_pre
    gate_grad = (
        hidden_grad * up_pre * sigmoid_gate * (1.0 + gate_pre * (1.0 - sigmoid_gate))
    ).astype(jnp.bfloat16)
    up_grad = (hidden_grad * activation).astype(jnp.bfloat16)
    mask = mask_ref[:, :1]
    gate = mask * gate_ref[:, :1]
    sent = gate.astype(jnp.bfloat16).astype(jnp.float32)
    hidden_ref[...] = (sent * hidden).astype(jnp.bfloat16)
    gs_ref[...] = (sent * gate_grad).astype(jnp.bfloat16)
    us_ref[...] = (sent * up_grad).astype(jnp.bfloat16)
    if own:
        product = hidden_grad * hidden * mask
        high = product.astype(jnp.bfloat16)
        low = (product - high).astype(jnp.bfloat16)
        ones = jnp.ones((SUBLANES, product.shape[1]), jnp.bfloat16)
        score = contract(ones, high, 1, 1) + contract(ones, low, 1, 1)
        part = contract(gate_grad, wg, 1, 1) + contract(up_grad, wu, 1, 1)

        @pl.when(step == 0)
        def _():
            total_ref[...] = part
            score_ref[...] = score

        @pl.when(step > 0)
        def _():
            total_ref[...] += part
            score_ref[...] += score

        @pl.when(step == pl.num_programs(0) - 1)
        def _():
            half = keep_ref.shape[0]
            scaled = (gate * total_ref[...]).astype(jnp.bfloat16)
            keep_ref[...] = scaled[:half]
            send_ref[...] = scaled[half:]


def rows_call(me, tok_parts, grad_parts, gate, w_gate, w_up, w_down, own):
    parts = len(tok_parts)
    width = tok_parts[0].shape[1]
    ff_width = w_gate.shape[2]
    tile = FF_TILE if ff_width % FF_TILE == 0 else ff_width
    rows = sum(part.shape[0] for part in tok_parts)
    half = jnp.bfloat16

    def whole(array):
        return pl.BlockSpec(array.shape, lambda j: (0, 0))

    def fixed(shape):
        return pl.BlockSpec(shape, lambda j: (0, 0))

    out_shape = [
        jax.ShapeDtypeStruct((rows, width), half),
        jax.ShapeDtypeStruct((rows, width), half),
    ] + [jax.ShapeDtypeStruct((rows, ff_width), half)] * 3
    out_specs = [fixed((rows, width))] * 2 + [pl.BlockSpec((rows, tile), lambda j: (0, j))] * 3
    scratch = []
    if own:
        out_shape += [jax.ShapeDtypeStruct((rows // 2, width), half)] * 2
        out_shape += [jax.ShapeDtypeStruct((SUBLANES, rows), jnp.float32)]
        out_specs += [fixed((rows // 2, width))] * 2 + [fixed((SUBLANES, rows))]
        scratch = [pltpu.VMEM((rows, width), jnp.float32)]
    scratch += [pltpu.VMEM((rows, LANES), jnp.float32)]
    products = 5 if own else 3
    return pl.pallas_call(
        functools.partial(rows_kernel, parts, own),
        grid=(ff_width // tile,),
        in_specs=[pl.BlockSpec(memory_space=pltpu.SMEM)]
        + [whole(part) for part in tok_parts]
        + [whole(part) for part in grad_parts]
        + [
            fixed((rows, LANES)),
            pl.BlockSpec((1, width, tile), lambda j: (0, 0, j)),
            pl.BlockSpec((1, width, tile), lambda j: (0, 0, j)),
            pl.BlockSpec((1, tile, width), lambda j: (0, j, 0)),
        ],
        out_specs=out_specs,
        out_shape=out_shape,
        scratch_shapes=scratch,
        compiler_params=pltpu.CompilerParams(vmem_limit_bytes=56 * MIB),
        cost_estimate=pl.CostEstimate(
            flops=2 * products * rows * width * ff_width,
            bytes_accessed=6 * width * ff_width,
            transcendentals=rows * ff_width,
        ),
    )(me, *tok_parts, *grad_parts, gate, w_gate, w_up, w_down)


def weights_kernel(blocks, group_ref, *refs):
    tok, grad, hidden, gates, ups = (refs[i * blocks : (i + 1) * blocks] for i in range(5))
    out_gate, out_up, out_down = refs[5 * blocks :]
    for out, lefts, rights in ((out_gate, tok, gates), (out_up, tok, ups), (out_down, hidden, grad)):
        total = contract(lefts[0][...], rights[0][...], 0, 0)
        for left, right in zip(lefts[1:], rights[1:]):
            total += contract(left[...], right[...], 0, 0)
        out[0] = total.astype(out.dtype)


def weights_call(group, groups, tok, grad, hidden, gates, ups, dtype):
    width, ff_width = (tok[0].shape[1], gates[0].shape[1])
    half, half_ff = (width // groups, ff_width // groups)
    steps = max(s for s in (4, 2, 1) if half % (s * LANES) == 0)
    if half_ff % LANES:
        hidden = [lax.dynamic_slice_in_dim(h, group[0] * half_ff, half_ff, axis=1) for h in hidden]

    def rows(array):
        return array.shape[0]

    def hidden_block(j, group_ref):
        return (0, 0 if half_ff % LANES else group_ref[0])

    in_specs = (
        [pl.BlockSpec((rows(a), half // steps), lambda j, g: (0, g[0] * steps + j)) for a in tok]
        + [pl.BlockSpec((rows(a), width // steps), lambda j, g: (0, j)) for a in grad]
        + [pl.BlockSpec((rows(a), half_ff), hidden_block) for a in hidden]
        + [pl.BlockSpec((rows(a), ff_width), lambda j, g: (0, 0)) for a in gates + ups]
    )
    return pl.pallas_call(
        functools.partial(weights_kernel, len(tok)),
        grid_spec=pltpu.PrefetchScalarGridSpec(
            num_scalar_prefetch=1,
            grid=(steps,),
            in_specs=in_specs,
            out_specs=[
                pl.BlockSpec((1, half // steps, ff_width), lambda j, g: (0, j, 0)),
                pl.BlockSpec((1, half // steps, ff_width), lambda j, g: (0, j, 0)),
                pl.BlockSpec((1, half_ff, width // steps), lambda j, g: (0, 0, j)),
            ],
        ),
        out_shape=[
            jax.ShapeDtypeStruct((1, half, ff_width), dtype),
            jax.ShapeDtypeStruct((1, half, ff_width), dtype),
            jax.ShapeDtypeStruct((1, half_ff, width), dtype),
        ],
        compiler_params=pltpu.CompilerParams(vmem_limit_bytes=48 * MIB),
        cost_estimate=pl.CostEstimate(
            flops=6 * sum(rows(a) for a in tok) * half * ff_width,
            bytes_accessed=6 * half * ff_width,
            transcendentals=0,
        ),
    )(group, *tok, *grad, *hidden, *gates, *ups)


def per_device(tokens, out_grad, expert_ids, router_weight, w_gate, w_up, w_down):
    tok_rows, width = tokens.shape
    experts = router_weight.shape[1]
    groups = lax.axis_size("dp")
    far = lax.axis_size("expert") // 4
    chunk = 2 * far * tok_rows
    me = lax.axis_index("expert").astype(jnp.int32)[None]
    group = lax.axis_index("dp").astype(jnp.int32)[None]

    def along(array):
        return jnp.concatenate([array] + [swap_expert(array, 4 * k) for k in range(1, far)], axis=0)

    tok_line = along(tokens)
    lane = jnp.arange(LANES, dtype=jnp.int32)
    picked = jnp.any(expert_ids[:, :, None] == lane[None, None, :], axis=1)
    grad_line = along(jnp.concatenate([out_grad, picked.astype(jnp.bfloat16)], axis=1))
    tok_next = swap_expert(tok_line, 2)
    grad_next = swap_expert(grad_line, 2)
    tok_own = [(tok_line, swap_expert(tok_line, 1)), (tok_next, swap_expert(tok_next, 1))]
    grad_own = [(grad_line, swap_expert(grad_line, 1)), (grad_next, swap_expert(grad_next, 1))]

    logits_own = jnp.concatenate(
        [contract(router_weight, rows, 0, 1) for pair in tok_own for rows in pair], axis=1
    )
    logits = jnp.concatenate(
        [logits_own] + [swap_group(logits_own, offset) for offset in range(1, groups)], axis=1
    )
    gate = small_call(
        gate_kernel, me, (logits,), jax.ShapeDtypeStruct((logits.shape[1], LANES), jnp.float32)
    )

    done, sums, scores = ([], [], [])
    row_sum = 0.0
    for index in range(2):
        *rows, keep, send, score = rows_call(
            me, tok_own[index], grad_own[index], gate[index * chunk : (index + 1) * chunk],
            w_gate, w_up, w_down, True,
        )
        done.append(rows)
        scores.append(score[0].astype(jnp.bfloat16))
        got = swap_expert(send, 1)
        for k in range(far):
            cut = slice(k * tok_rows, (k + 1) * tok_rows)
            near = keep[cut].astype(jnp.float32) + got[cut].astype(jnp.float32)
            if index or k:
                near = swap_expert(near.astype(jnp.bfloat16), 4 * k + 2 * index).astype(jnp.float32)
            row_sum = row_sum + near

    score = jnp.stack(scores).reshape(2, 2, far, tok_rows)
    from_far = [score]
    for k in range(1, far):
        got = swap_expert(score, k * 4)
        from_far.append(jnp.stack([got[:, :, j ^ k] for j in range(far)], axis=2))
    score = jnp.stack(from_far)
    score = jnp.stack([score, jnp.flip(swap_expert(score, 2), axis=1)], axis=1)
    score = jnp.stack([score, jnp.flip(swap_expert(score, 1), axis=3)], axis=2)
    score = score.reshape(experts, 2 * chunk)
    score = jnp.concatenate(
        [score] + [swap_group(score, offset) for offset in range(1, groups)], axis=1
    )
    logit_grad = small_call(
        adjoint_kernel, me, (logits, score), jax.ShapeDtypeStruct(logits.shape, jnp.bfloat16)
    )

    token_rows = [rows[0] for rows in done]
    at_once = 2 * groups * chunk <= ROWS_AT_ONCE
    totals = None
    tie = None
    for offset in range(1, groups):
        sources = (tok_line, grad_line, tok_next, grad_next)
        if not at_once:
            terms = weights_call(group, groups, *map(list, zip(*done)), jnp.float32)
            totals = terms if totals is None else [t + u for t, u in zip(totals, terms)]
            done = []
            sources, totals = lax.optimization_barrier((sources, totals))
        moved = [swap_group(part, offset) for part in sources]
        parts = []
        for part in moved:
            parts += [part, swap_expert(part, 1)]
        rows = rows_call(
            me, parts[0:2] + parts[4:6], parts[2:4] + parts[6:8],
            gate[2 * chunk * offset : 2 * chunk * (offset + 1)], w_gate, w_up, w_down, False,
        )
        done.append(rows)
        token_rows.append(rows[0])
    final = weights_call(
        group, groups, *map(list, zip(*done)), jnp.bfloat16 if totals is None else jnp.float32
    )
    if totals is not None:
        final = [(t + u).astype(jnp.bfloat16) for t, u in zip(totals, final)]

    grad_router = 0.0
    at = 0
    for rows in token_rows:
        grad_router += contract(rows, logit_grad[:, at : at + rows.shape[0]], 0, 1)
        at += rows.shape[0]
    row_sum = row_sum + contract(logit_grad[:, :tok_rows], router_weight, 0, 1)
    return (row_sum.astype(jnp.bfloat16), grad_router, *final)


def solution(mesh):
    in_specs = (
        P(("dp", "expert"), None),
        P(("dp", "expert"), None),
        P(("dp", "expert"), None),
        P(),
        P("expert", None, None),
        P("expert", None, None),
        P("expert", None, None),
    )
    out_specs = (
        P(("dp", "expert"), None),
        P(),
        P("expert", "dp", None),
        P("expert", "dp", None),
        P("expert", "dp", None),
    )
    return jax.shard_map(
        per_device, mesh=mesh, in_specs=in_specs, out_specs=out_specs, check_vma=False
    )
```

```python
import functools

import jax
import jax.numpy as jnp
from jax import lax
from jax.experimental import pallas as pl
from jax.experimental.pallas import tpu as pltpu
from jax.sharding import PartitionSpec as P

PASSES = 3
LANES = 128
SUBLANES = 8
FF_TILE = 256
GRANT = 56 << 20
ROWS_AT_ONCE = 1024


def swap_expert(array, offset):
    size = lax.axis_size("expert")
    return lax.ppermute(array, "expert", [(i, i ^ offset) for i in range(size)])


def swap_group(array, offset):
    size = lax.axis_size("dp")
    return lax.ppermute(array, "dp", [(i, i ^ offset) for i in range(size)])


def contract(left, right, left_dim, right_dim):
    return lax.dot_general(
        left, right, (((left_dim,), (right_dim,)), ((), ())), preferred_element_type=jnp.float32
    )


def balancer_forward_pass(logits):
    densities = [jnp.exp(logits)]
    quotients, column_totals, row_totals = ([], [], [])
    for _ in range(PASSES):
        column_sum = jnp.sum(densities[-1], axis=1, keepdims=True)
        quotient = densities[-1] / column_sum
        row_sum = jnp.sum(quotient, axis=0, keepdims=True)
        densities.append(quotient / row_sum)
        quotients.append(quotient)
        column_totals.append(column_sum)
        row_totals.append(row_sum)
    return (densities, quotients, column_totals, row_totals)


def balancer_adjoint_pass(density_gradient, densities, quotients, column_totals, row_totals):
    for repeat in reversed(range(PASSES)):
        inner = jnp.sum(density_gradient * densities[repeat + 1], axis=0, keepdims=True)
        quotient_grad = (density_gradient - inner) / row_totals[repeat]
        shared = jnp.sum(quotient_grad * quotients[repeat], axis=1, keepdims=True)
        density_gradient = (quotient_grad - shared) / column_totals[repeat]
    return density_gradient * densities[0]


def gate_kernel(me_ref, logits_ref, gate_ref):
    logits = logits_ref[...]
    experts, count = logits.shape
    gates = experts * balancer_forward_pass(logits)[0][-1]
    row = lax.broadcasted_iota(jnp.int32, gates.shape, 0)
    mine = jnp.sum(jnp.where(row == me_ref[0], gates, 0.0), axis=0, keepdims=True)
    gate_ref[...] = jnp.transpose(jnp.broadcast_to(mine, (LANES, count)))


def kernel_call(
    kernel, scalars, small, large, out_shape, scratch, copies, large_outs=0, after=(), macs=10**6
):
    whole = pl.BlockSpec(memory_space=pltpu.VMEM)
    outside = pl.BlockSpec(memory_space=pltpu.HBM)
    inputs = len(scalars) + len(small) + len(large)

    def body(*refs):
        kernel(*refs[:inputs], *refs[inputs + len(after) :])

    return pl.pallas_call(
        body,
        in_specs=[pl.BlockSpec(memory_space=pltpu.SMEM)] * len(scalars)
        + [whole] * len(small)
        + [outside] * (len(large) + len(after)),
        out_specs=[outside] * large_outs + [whole] * (len(out_shape) - large_outs),
        out_shape=out_shape,
        scratch_shapes=[*scratch] + [pltpu.SemaphoreType.DMA((copies,))] * (copies > 0),
        compiler_params=pltpu.CompilerParams(vmem_limit_bytes=GRANT),
        cost_estimate=pl.CostEstimate(
            flops=2 * macs, bytes_accessed=macs // 200, transcendentals=macs // 10000
        ),
    )(*scalars, *small, *large, *after)


def shape(rows, columns, dtype=jnp.bfloat16):
    return jax.ShapeDtypeStruct((rows, columns), dtype)


def tiles(extent, tile):
    tile = tile if extent % tile == 0 else extent
    return [slice(at, at + tile) for at in range(0, extent, tile)]


class Copies:
    def __init__(self, sems):
        self.sems, self.count = (sems, 0)

    def start(self, source, target):
        copy = pltpu.make_async_copy(source, target, self.sems.at[self.count])
        self.count += 1
        copy.start()
        return copy

    def stack(self, parts, target, columns=slice(None)):
        started, at = ([], 0)
        for part in parts:
            rows = part.shape[0]
            started.append(self.start(part.at[:, columns], target.at[pl.ds(at, rows), :]))
            at += rows
        return started


def wait(copies):
    for copy in copies:
        copy.wait()


def column_of(me_ref, picked):
    picked = picked.astype(jnp.float32)
    lane = lax.broadcasted_iota(jnp.int32, picked.shape, 1)
    return jnp.sum(jnp.where(lane == me_ref[0], picked, 0.0), axis=1, keepdims=True)


def hidden_tile(rows_in, rows_grad, wg, wu, wd):
    gate_pre = contract(rows_in, wg, 1, 0)
    up_pre = contract(rows_in, wu, 1, 0)
    hidden_grad = contract(rows_grad, wd, 1, 1)
    sigmoid_gate = jax.nn.sigmoid(gate_pre)
    activation = gate_pre * sigmoid_gate
    hidden = activation * up_pre
    gate_grad = hidden_grad * up_pre * sigmoid_gate * (1.0 + gate_pre * (1.0 - sigmoid_gate))
    up_grad = hidden_grad * activation
    half = jnp.bfloat16
    return hidden, gate_grad.astype(half), up_grad.astype(half), hidden_grad * hidden


def start_weights(copies, sources, targets):
    (wg, wu, wd), (wg_to, wu_to, wd_to) = (sources, targets)
    started = []
    for cut in tiles(wg.shape[2], FF_TILE):
        here = pl.ds(cut.start, cut.stop - cut.start)
        started.append(
            [
                copies.start(wg.at[0, :, here], wg_to.at[:, here]),
                copies.start(wu.at[0, :, here], wu_to.at[:, here]),
                copies.start(wd.at[0, here, :], wd_to.at[here, :]),
            ]
        )
    return started


def logits_kernel(parts, *refs):
    router, *tok, out, rows, sems = refs
    copies = Copies(sems)
    wait(copies.stack(tok, rows))
    out[...] = contract(router[...], rows[...], 1, 1)


def expert_kernel(parts, me_ref, gate_ref, *refs):
    tok, grad, sources = (refs[:parts], refs[parts : 2 * parts], refs[2 * parts : 2 * parts + 3])
    refs = refs[2 * parts + 3 :]
    sum_outs, scaled_outs, score_ref, refs = (refs[:parts], refs[parts : parts + 3], refs[parts + 3], refs[parts + 4 :])
    rows_in, rows_grad, wg, wu, wd, gate_grad, up_grad, hs, gs, us, sums, sems = refs
    copies = Copies(sems)
    width = rows_in.shape[1]
    tok_here = copies.stack(tok, rows_in)
    weights_here = start_weights(copies, sources, (wg, wu, wd))
    grad_here = copies.stack(grad, rows_grad)
    wait(tok_here)
    wait(grad_here)
    mask = column_of(me_ref, rows_grad[:, width:])
    gate = mask * gate_ref[: rows_in.shape[0], :1]
    sent = gate.astype(jnp.bfloat16).astype(jnp.float32)
    score = jnp.zeros(score_ref.shape, jnp.float32)
    results = []
    for cut, here in zip(tiles(wg.shape[1], FF_TILE), weights_here):
        wait(here)
        hidden, gate_part, up_part, product = hidden_tile(
            rows_in[...], rows_grad[:, :width], wg[:, cut], wu[:, cut], wd[cut, :]
        )
        gate_grad[:, cut] = gate_part
        up_grad[:, cut] = up_part
        here = pl.ds(cut.start, cut.stop - cut.start)
        for value, target, out in zip((hidden, gate_part, up_part), (hs, gs, us), scaled_outs):
            target[:, cut] = (sent * value).astype(jnp.bfloat16)
            results.append(copies.start(target.at[:, here], out.at[:, here]))
        product = product * mask
        high = product.astype(jnp.bfloat16)
        low = (product - high).astype(jnp.bfloat16)
        ones = jnp.ones((SUBLANES, product.shape[1]), jnp.bfloat16)
        score += contract(ones, high, 1, 1) + contract(ones, low, 1, 1)
    score_ref[...] = score
    for cut in tiles(width, 2 * FF_TILE):
        part = contract(gate_grad[...], wg[cut, :], 1, 1)
        part += contract(up_grad[...], wu[cut, :], 1, 1)
        sums[:, cut] = (gate * part).astype(jnp.bfloat16)
        at = 0
        here = pl.ds(cut.start, cut.stop - cut.start)
        for out in sum_outs:
            source = sums.at[pl.ds(at, out.shape[0]), here]
            results.append(copies.start(source, out.at[:, here]))
            at += out.shape[0]
    wait(results)


def expert_call(me, gate, tok, grad, weights, after):
    rows = sum(part.shape[0] for part in tok)
    width, ff_width = weights[0].shape[1:]
    half = jnp.bfloat16
    wide, narrow = (pltpu.VMEM((rows, width), half), pltpu.VMEM((rows, ff_width), half))
    return kernel_call(
        functools.partial(expert_kernel, len(tok)), (me,), (gate,), (*tok, *grad, *weights),
        [shape(part.shape[0], width) for part in tok]
        + [shape(rows, ff_width)] * 3 + [shape(SUBLANES, rows, jnp.float32)],
        [wide, pltpu.VMEM((rows, grad[0].shape[1]), half)]
        + [pltpu.VMEM((width, ff_width), half)] * 2 + [pltpu.VMEM((ff_width, width), half)]
        + [narrow] * 5 + [wide],
        2 * len(tok) + 6 * len(tiles(ff_width, FF_TILE))
        + len(tok) * len(tiles(width, 2 * FF_TILE)),
        len(tok) + 3, after, 5 * rows * width * ff_width,
    )


def add_kernel(left, right, out, left_here, right_here, total, sems):
    copies = Copies(sems)
    wait([copies.start(left, left_here), copies.start(right, right_here)])
    total[...] = (
        left_here[...].astype(jnp.float32) + right_here[...].astype(jnp.float32)
    ).astype(total.dtype)
    wait([copies.start(total, out)])


def weights_kernel(parts, fresh, given, start, steps, me_ref, group_ref, *refs):
    gate_ref, refs = (refs[0], refs[1:])
    tok, grad, sources = (refs[:parts], refs[parts : 2 * parts], refs[2 * parts : 2 * parts + 3])
    refs = refs[2 * parts + 3 :]
    given_refs, outs, refs = (refs[: 3 * given], refs[3 * given :][:3], refs[3 * given + 3 :])
    hs, gs, us, tok_half, grad_all, hidden_half, *refs = refs
    tile_out, rows_in, picked, wg, wu, wd, sems = (refs[:3], *refs[3:])
    copies = Copies(sems)
    width = tok[0].shape[1]
    half = outs[0].shape[1]
    half_ff = outs[2].shape[1]
    plain = pl.ds(0, width)
    known = sum(ref.shape[0] for ref in given_refs[:given])
    fresh_here = weights_here = []
    if fresh:
        fresh_here = copies.stack(tok[parts - fresh :], rows_in)
        fresh_here += copies.stack(grad[parts - fresh :], picked, pl.ds(width, LANES))
    first = sum(ref.shape[0] for ref in grad[: parts - fresh])
    new_here = []
    if fresh:
        fresh_rows = pl.ds(first, grad_all.shape[0] - first)
        new_here = copies.stack(grad[parts - fresh :], grad_all.at[fresh_rows, :], plain)
        weights_here = start_weights(copies, sources, (wg, wu, wd))
    grad_here = copies.stack(grad[: parts - fresh], grad_all, plain)
    mine = pl.ds(pl.multiple_of(group_ref[0] * half, LANES), half)
    rest_here = copies.stack(tok, tok_half, mine)
    for kind, target in enumerate((hs, gs, us)):
        if given:
            rest_here += copies.stack(
                given_refs[kind * given : (kind + 1) * given], target
            )
    wait(fresh_here)
    wait(new_here)
    if fresh:
        count = rows_in.shape[0]
        gate = column_of(me_ref, picked[...]) * gate_ref[start : start + count, :1]
        sent = gate.astype(jnp.bfloat16).astype(jnp.float32)
        new = slice(known, known + count)
        for cut, here in zip(tiles(wg.shape[1], FF_TILE), weights_here):
            wait(here)
            hidden, gate_grad, up_grad, _ = hidden_tile(
                rows_in[...], grad_all[new, :], wg[:, cut], wu[:, cut], wd[cut, :]
            )
            hs[new, cut] = (sent * hidden).astype(jnp.bfloat16)
            gs[new, cut] = (sent * gate_grad).astype(jnp.bfloat16)
            us[new, cut] = (sent * up_grad).astype(jnp.bfloat16)
    wait(rest_here)
    wait(grad_here)
    if half_ff % LANES == 0:
        hidden_half[...] = hs[:, pl.ds(pl.multiple_of(group_ref[0] * half_ff, LANES), half_ff)]
    else:
        for index in range(hs.shape[1] // half_ff):

            @pl.when(group_ref[0] == index)
            def _():
                hidden_half[...] = hs[:, index * half_ff : (index + 1) * half_ff]

    results = []
    for which, left, right in ((0, tok_half, gs), (1, tok_half, us), (2, hidden_half, grad_all)):
        for step in range(steps):
            if which < 2:
                size = half // steps
                cut = slice(step * size, (step + 1) * size)
                value = contract(left[:, cut], right[...], 0, 0)
                target = outs[which].at[0, pl.ds(step * size, size), :]
            else:
                size = width // steps
                cut = slice(step * size, (step + 1) * size)
                value = contract(left[...], right[:, cut], 0, 0)
                target = outs[which].at[0, :, pl.ds(step * size, size)]
            tile_out[which][step] = value.astype(tile_out[which].dtype)
            results.append(copies.start(tile_out[which].at[step], target))
    wait(results)


def weights_call(me, group, groups, tok, grad, gate, weights, given, fresh, start, dtype):
    width, ff_width = weights[0].shape[1:]
    half, half_ff = (width // groups, ff_width // groups)
    rows = sum(part.shape[0] for part in tok)
    new_rows = sum(part.shape[0] for part in tok[len(tok) - fresh :]) if fresh else SUBLANES * 2
    steps = max(s for s in (4, 2, 1) if half % (s * LANES) == 0)
    low = jnp.bfloat16
    scratch = [pltpu.VMEM((rows, ff_width), low)] * 3
    scratch += [
        pltpu.VMEM((rows, half), low),
        pltpu.VMEM((rows, width), low),
        pltpu.VMEM((rows, half_ff), low),
        pltpu.VMEM((steps, half // steps, ff_width), dtype),
        pltpu.VMEM((steps, half // steps, ff_width), dtype),
        pltpu.VMEM((steps, half_ff, width // steps), dtype),
        pltpu.VMEM((new_rows, width), low),
        pltpu.VMEM((new_rows, LANES), low),
        pltpu.VMEM((width, ff_width), low),
        pltpu.VMEM((width, ff_width), low),
        pltpu.VMEM((ff_width, width), low),
    ]
    count = 2 * len(tok) + 2 * fresh + 3 * len(given) + 3 * steps
    count += 3 * len(tiles(ff_width, FF_TILE)) if fresh else 0
    return kernel_call(
        functools.partial(weights_kernel, len(tok), fresh, len(given), start, steps),
        (me, group), (gate,),
        (*tok, *grad, *weights, *(block[kind] for kind in range(3) for block in given)),
        [
            jax.ShapeDtypeStruct((1, half, ff_width), dtype),
            jax.ShapeDtypeStruct((1, half, ff_width), dtype),
            jax.ShapeDtypeStruct((1, half_ff, width), dtype),
        ],
        scratch, count, 3, (), 3 * (rows * half + new_rows * width) * ff_width,
    )


def router_kernel(parts, me_ref, *refs):
    logits_ref, score_ref, *tok = refs[: 2 + parts]
    grad_ref, router_ref, rows, sems = refs[2 + parts :]
    copies = Copies(sems)
    rows_here = copies.stack(tok, rows)
    logits = logits_ref[...]
    experts = logits.shape[0]
    row = lax.broadcasted_iota(jnp.int32, (experts, experts), 0)
    column = lax.broadcasted_iota(jnp.int32, (experts, experts), 1)
    unswap = jnp.where((row ^ me_ref[0]) == column, 1.0, 0.0).astype(jnp.bfloat16)
    score = contract(unswap, score_ref[...], 1, 0)
    state = balancer_forward_pass(logits)
    grad = balancer_adjoint_pass(experts * score, *state).astype(jnp.bfloat16)
    grad_ref[...] = grad
    wait(rows_here)
    router_ref[...] = contract(grad, rows[...], 1, 0)


def per_device(tokens, out_grad, expert_ids, router_weight, w_gate, w_up, w_down):
    tok_rows, width = tokens.shape
    experts = router_weight.shape[1]
    groups = lax.axis_size("dp")
    far = lax.axis_size("expert") // 4
    chunk = 2 * far * tok_rows
    me = lax.axis_index("expert").astype(jnp.int32)[None]
    group = lax.axis_index("dp").astype(jnp.int32)[None]

    def along(array):
        return jnp.concatenate([array] + [swap_expert(array, 4 * k) for k in range(1, far)], axis=0)

    tok_line = along(tokens)
    lane = jnp.arange(LANES, dtype=jnp.int32)
    picked = jnp.any(expert_ids[:, :, None] == lane[None, None, :], axis=1)
    grad_line = along(jnp.concatenate([out_grad, picked.astype(jnp.bfloat16)], axis=1))
    tok_next = swap_expert(tok_line, 2)
    grad_next = swap_expert(grad_line, 2)
    tok_own = [(tok_line, swap_expert(tok_line, 1)), (tok_next, swap_expert(tok_next, 1))]
    grad_own = [(grad_line, swap_expert(grad_line, 1)), (grad_next, swap_expert(grad_next, 1))]

    tok_parts = [rows for pair in tok_own for rows in pair]
    grad_parts = [rows for pair in grad_own for rows in pair]
    weights = (w_gate, w_up, w_down)
    ff_width = w_gate.shape[2]

    at_once = 2 * groups * chunk <= ROWS_AT_ONCE

    def moved(parts, offset):
        out = []
        for part in parts:
            part = swap_group(part, offset)
            out += [part, swap_expert(part, 1)]
        return out

    moved_tok = moved((tok_line, tok_next), 1) if at_once else []
    (logits_own,) = kernel_call(
        functools.partial(logits_kernel, len(tok_parts)), (), (router_weight.T,), tok_parts,
        [shape(experts, 2 * chunk, jnp.float32)],
        [pltpu.VMEM((2 * chunk, width), jnp.bfloat16)], len(tok_parts), 0, moved_tok[:1],
    )
    moved_grad = moved((grad_line, grad_next), 1) if at_once else []
    logits = jnp.concatenate(
        [logits_own] + [swap_group(logits_own, offset) for offset in range(1, groups)], axis=1
    )
    (gate,) = kernel_call(
        gate_kernel, (me,), (logits,), (), [shape(logits.shape[1], LANES, jnp.float32)], (), 0
    )

    keep0, send0, keep1, send1, *scaled, score = expert_call(
        me, gate, tok_parts, grad_parts, weights, moved_tok[2:3]
    )
    given = [scaled]
    got1, got0 = (swap_expert(send1, 1), swap_expert(send0, 1))
    (near,) = kernel_call(
        add_kernel, (), (), (keep1, got1), [shape(*keep1.shape)],
        [pltpu.VMEM(keep1.shape, keep1.dtype)] * 3, 3, 1, moved_grad,
    )
    near = swap_expert(near, 2)
    row_sum = 0.0
    for k in range(far):
        cut = slice(k * tok_rows, (k + 1) * tok_rows)
        total = sum(array[cut].astype(jnp.float32) for array in (keep0, got0, near))
        if k:
            total = swap_expert(total.astype(jnp.bfloat16), 4 * k).astype(jnp.float32)
        row_sum = row_sum + total

    score = score[0].astype(jnp.bfloat16).reshape(2, 2, far, tok_rows)
    from_far = [score]
    for k in range(1, far):
        got = swap_expert(score, k * 4)
        from_far.append(jnp.stack([got[:, :, j ^ k] for j in range(far)], axis=2))
    score = jnp.stack(from_far)
    score = jnp.stack([score, jnp.flip(swap_expert(score, 2), axis=1)], axis=1)
    score = jnp.stack([score, jnp.flip(swap_expert(score, 1), axis=3)], axis=2)
    score = score.reshape(experts, 2 * chunk)
    score = jnp.concatenate(
        [score] + [swap_group(score, offset) for offset in range(1, groups)], axis=1
    )
    token_rows = list(tok_parts)
    totals = None
    if not at_once:
        totals = weights_call(
            me, group, groups, tok_parts, grad_parts, gate, weights, given, 0, 0, jnp.float32
        )
        tok_parts, grad_parts, given = ([], [], [])
    for offset in range(1, groups):
        if not at_once:
            (tok_line, tok_next, grad_line, grad_next), totals = lax.optimization_barrier(
                ((tok_line, tok_next, grad_line, grad_next), totals)
            )
            moved_tok = moved((tok_line, tok_next), offset)
            moved_grad = moved((grad_line, grad_next), offset)
        token_rows += moved_tok
        terms = weights_call(
            me, group, groups, tok_parts + moved_tok, grad_parts + moved_grad, gate, weights, given,
            4, 2 * chunk * offset, jnp.bfloat16 if at_once else jnp.float32,
        )
        totals = terms if totals is None else [t + u for t, u in zip(totals, terms)]
    final = [t.astype(jnp.bfloat16) for t in totals]

    logit_grad, grad_router = kernel_call(
        functools.partial(router_kernel, len(token_rows)), (me,), (logits, score), token_rows,
        [shape(*logits.shape), shape(experts, width, jnp.float32)],
        [pltpu.VMEM((logits.shape[1], width), jnp.bfloat16)], len(token_rows),
    )
    row_sum = row_sum + contract(logit_grad[:, :tok_rows], router_weight, 0, 1)
    return (row_sum.astype(jnp.bfloat16), grad_router.T, *final)


def solution(mesh):
    in_specs = (
        P(("dp", "expert"), None),
        P(("dp", "expert"), None),
        P(("dp", "expert"), None),
        P(),
        P("expert", None, None),
        P("expert", None, None),
        P("expert", None, None),
    )
    out_specs = (
        P(("dp", "expert"), None),
        P(),
        P("expert", "dp", None),
        P("expert", "dp", None),
        P("expert", "dp", None),
    )
    return jax.shard_map(
        per_device, mesh=mesh, in_specs=in_specs, out_specs=out_specs, check_vma=False
    )
```

```python
import functools

import jax
import jax.numpy as jnp
from jax import lax
from jax.experimental import pallas as pl
from jax.experimental.pallas import tpu as pltpu
from jax.sharding import PartitionSpec as P

PASSES = 3
LANES = 128
SUBLANES = 8
FF_TILE = 256
ROW_TILE = 32
GRANT = 56 << 20
ROWS_AT_ONCE = 1024


def swap_expert(array, offset):
    size = lax.axis_size("expert")
    return lax.ppermute(array, "expert", [(i, i ^ offset) for i in range(size)])


def swap_group(array, offset):
    size = lax.axis_size("dp")
    return lax.ppermute(array, "dp", [(i, i ^ offset) for i in range(size)])


def contract(left, right, left_dim, right_dim):
    return lax.dot_general(
        left, right, (((left_dim,), (right_dim,)), ((), ())), preferred_element_type=jnp.float32
    )


def balancer_forward_pass(logits):
    densities = [jnp.exp(logits)]
    quotients, column_totals, row_totals = ([], [], [])
    for _ in range(PASSES):
        column_sum = jnp.sum(densities[-1], axis=1, keepdims=True)
        quotient = densities[-1] / column_sum
        row_sum = jnp.sum(quotient, axis=0, keepdims=True)
        densities.append(quotient / row_sum)
        quotients.append(quotient)
        column_totals.append(column_sum)
        row_totals.append(row_sum)
    return (densities, quotients, column_totals, row_totals)


def balancer_adjoint_pass(density_gradient, densities, quotients, column_totals, row_totals):
    for repeat in reversed(range(PASSES)):
        inner = jnp.sum(density_gradient * densities[repeat + 1], axis=0, keepdims=True)
        quotient_grad = (density_gradient - inner) / row_totals[repeat]
        shared = jnp.sum(quotient_grad * quotients[repeat], axis=1, keepdims=True)
        density_gradient = (quotient_grad - shared) / column_totals[repeat]
    return density_gradient * densities[0]


def round_up(value, unit):
    return -(-value // unit) * unit


def pack_kernel(ids_ref, tok_ref, router_ref, out):
    experts = router_ref.shape[0]
    rest = contract(tok_ref[...], router_ref[...], 1, 1)
    lane = lax.broadcasted_iota(jnp.int32, out.shape, 1)
    packed = jnp.zeros(out.shape, jnp.float32)
    for pick in range(ids_ref.shape[1]):
        packed += jnp.where(lane == ids_ref[:, pick : pick + 1], 1.0, 0.0)
    row = lax.broadcasted_iota(jnp.int32, (experts, out.shape[1]), 0)
    column = lax.broadcasted_iota(jnp.int32, (experts, out.shape[1]), 1)
    for term in range(1, 4):
        part = rest.astype(jnp.bfloat16)
        rest = rest - part.astype(jnp.float32)
        place = jnp.where(column == row + term * experts, 1.0, 0.0).astype(jnp.bfloat16)
        packed += contract(part, place, 1, 0)
    out[...] = packed.astype(jnp.bfloat16)


def gate_kernel(parts, experts, me_ref, *refs):
    grad, gate_ref, logits_ref, packed, sems = (refs[:parts], *refs[parts:])
    copies = Copies(sems)
    extra = packed.shape[1]
    wait(copies.stack(grad, packed, pl.ds(grad[0].shape[1] - extra, extra)))
    turned = jnp.transpose(packed[...].astype(jnp.float32))
    columns = []
    for group in range(logits_ref.shape[1] // packed.shape[0]):
        at = (3 * group + 1) * experts
        terms = [turned[at + i * experts : at + (i + 1) * experts] for i in range(3)]
        columns.append(terms[0] + terms[1] + terms[2])
    logits = jnp.concatenate(columns, axis=1)
    logits_ref[...] = logits
    gates = experts * balancer_forward_pass(logits)[0][-1]
    row = lax.broadcasted_iota(jnp.int32, gates.shape, 0)
    mine = jnp.sum(jnp.where(row == me_ref[0], gates, 0.0), axis=0, keepdims=True)
    gate_ref[...] = jnp.transpose(jnp.broadcast_to(mine, (LANES, gates.shape[1])))


def kernel_call(
    kernel, scalars, small, large, out_shape, scratch, copies, large_outs=0, after=(), macs=10**6
):
    whole = pl.BlockSpec(memory_space=pltpu.VMEM)
    outside = pl.BlockSpec(memory_space=pltpu.HBM)
    inputs = len(scalars) + len(small) + len(large)

    def body(*refs):
        kernel(*refs[:inputs], *refs[inputs + len(after) :])

    return pl.pallas_call(
        body,
        in_specs=[pl.BlockSpec(memory_space=pltpu.SMEM)] * len(scalars)
        + [whole] * len(small)
        + [outside] * (len(large) + len(after)),
        out_specs=[outside] * large_outs + [whole] * (len(out_shape) - large_outs),
        out_shape=out_shape,
        scratch_shapes=[*scratch] + [pltpu.SemaphoreType.DMA((copies,))] * (copies > 0),
        compiler_params=pltpu.CompilerParams(vmem_limit_bytes=GRANT),
        cost_estimate=pl.CostEstimate(
            flops=2 * macs, bytes_accessed=macs // 200, transcendentals=macs // 10000
        ),
    )(*scalars, *small, *large, *after)


def shape(rows, columns, dtype=jnp.bfloat16):
    return jax.ShapeDtypeStruct((rows, columns), dtype)


def tiles(extent, tile):
    tile = tile if extent % tile == 0 else extent
    return [slice(at, at + tile) for at in range(0, extent, tile)]


class Copies:
    def __init__(self, sems):
        self.sems, self.count = (sems, 0)

    def start(self, source, target):
        copy = pltpu.make_async_copy(source, target, self.sems.at[self.count])
        self.count += 1
        copy.start()
        return copy

    def stack(self, parts, target, columns=slice(None)):
        started, at = ([], 0)
        for part in parts:
            rows = part.shape[0]
            started.append(self.start(part.at[:, columns], target.at[pl.ds(at, rows), :]))
            at += rows
        return started


def wait(copies):
    for copy in copies:
        copy.wait()


def loop(count, body, rolled=True):
    if not rolled:
        for index in range(count):
            body(index)
        return

    def step(index, carry):
        body(index)
        return carry

    lax.fori_loop(0, count, step, 0)


class Tiles:
    def __init__(self, copies, source, target, dim, tile):
        extent = target.shape[dim]
        self.tile = tile if extent % tile == 0 else extent
        self.count = extent // self.tile
        self.source, self.target, self.dim = (source, target, dim)
        self.sems, self.base = (copies.sems, copies.count)
        copies.count += self.count
        for index in range(self.count):
            self.copy(index).start()

    def here(self, index):
        start = index * self.tile
        if not isinstance(index, int):
            start = pl.multiple_of(start, self.tile)
        cut = pl.ds(start, self.tile)
        return (cut, slice(None)) if self.dim == 0 else (slice(None), cut)

    def copy(self, index):
        here = self.here(index)
        return pltpu.make_async_copy(
            self.source.at[here], self.target.at[here], self.sems.at[self.base + index]
        )


def mask_of(me_ref, picked):
    row = lax.broadcasted_iota(jnp.int32, (LANES, LANES), 0)
    mine = jnp.where(row == me_ref[0], 1.0, 0.0).astype(jnp.bfloat16)
    return contract(picked, mine, 1, 0)


def spread(lanes, width):
    return jnp.concatenate([lanes] * (width // LANES), axis=1)


def rounded(array):
    return array.astype(jnp.bfloat16).astype(jnp.float32)


def inner_terms(gate_pre, up_pre, hidden_grad):
    sigmoid_gate = jax.nn.sigmoid(gate_pre)
    activation = gate_pre * sigmoid_gate
    hidden = activation * up_pre
    gate_grad = hidden_grad * up_pre * sigmoid_gate * (1.0 + gate_pre * (1.0 - sigmoid_gate))
    up_grad = hidden_grad * activation
    half = jnp.bfloat16
    return hidden, gate_grad.astype(half), up_grad.astype(half)


def project_start(copies, tok, rows_in, sources, weights):
    width = rows_in.shape[1]
    tile = 2 * FF_TILE if width % (2 * FF_TILE) == 0 else width
    blocks = []
    for start in range(0, width, tile):
        cut = pl.ds(start, tile)
        here, at = ([], 0)
        for part in tok:
            rows = pl.ds(at, part.shape[0])
            here.append(copies.start(part.at[:, cut], rows_in.at[rows, cut]))
            at += part.shape[0]
        for source, weight in zip(sources, weights):
            here.append(copies.start(source.at[0, cut, :], weight.at[cut, :]))
        blocks.append((slice(start, start + tile), here))
    return blocks


def project(blocks, rows_in, targets, weights):
    for cut, here in blocks:
        wait(here)
        for target, weight in zip(targets, weights):
            value = contract(rows_in[:, cut], weight[cut, :], 1, 0)
            if cut.start == 0:
                target[...] = value
            else:
                target[...] += value


def backward(grad_here, rows_grad, hidden_grad, weight):
    wait(grad_here)

    def body(index):
        weight.copy(index).wait()
        cut = weight.here(index)[0]
        rows = rows_grad[:, : weight.target.shape[1]]
        hidden_grad[:, cut] = contract(rows, weight.target[cut, :], 1, 1)

    loop(weight.count, body)


def row_cut(index):
    start = index * ROW_TILE
    return pl.ds(start if isinstance(index, int) else pl.multiple_of(start, ROW_TILE), ROW_TILE)


def expert_kernel(parts, me_ref, gate_ref, place_ref, *refs):
    tok, grad, sources = (refs[:parts], refs[parts : 2 * parts], refs[2 * parts : 2 * parts + 3])
    refs = refs[2 * parts + 3 :]
    sum_outs, scaled_outs = (refs[:parts], refs[parts : parts + 3])
    rows_in, rows_grad, gate_pre, up_pre, hidden_grad, *refs = refs[parts + 3 :]
    wg, wu, wd, gate_grad, up_grad, hs, gs, us, sums, column, gate, sems = refs
    copies = Copies(sems)
    width = wg.shape[0]
    rows = gate_pre.shape[0]
    ff_width = wd.shape[0]
    blocks = project_start(copies, tok, rows_in, sources, (wg, wu))
    grad_here = copies.stack(grad, rows_grad)
    down = Tiles(copies, sources[2].at[0], wd, 0, FF_TILE)
    project(blocks, rows_in, (gate_pre, up_pre), (wg, wu))
    backward(grad_here, rows_grad, hidden_grad, down)
    gate[...] = mask_of(me_ref, rows_grad[:, width : width + LANES])
    column[...] = gate[...]
    gate[...] *= gate_ref[:rows, :]

    def terms(index):
        cut = row_cut(index)
        values = inner_terms(gate_pre[cut, :], up_pre[cut, :], hidden_grad[cut, :])
        gate_grad[cut, :] = values[1]
        up_grad[cut, :] = values[2]
        sent = spread(rounded(gate[cut, :]), ff_width)
        for value, target in zip(values, (hs, gs, us)):
            target[cut, :] = (sent * value).astype(jnp.bfloat16)
        product = hidden_grad[cut, :] * values[0]
        column[cut, :] *= sum(product[:, at] for at in tiles(ff_width, LANES))

    loop(rows // ROW_TILE, terms)
    results = [copies.start(source, out) for source, out in zip((hs, gs, us), scaled_outs)]
    ones = jnp.ones((SUBLANES, LANES), jnp.bfloat16)
    high = column[...].astype(jnp.bfloat16)
    low = (column[...] - high.astype(jnp.float32)).astype(jnp.bfloat16)
    score = (contract(ones, high, 1, 1) + contract(ones, low, 1, 1)).astype(jnp.bfloat16)
    score = contract(score, order_matrix(place_ref, round_up(rows, LANES)), 1, 1)
    block = placed([score[:1, at] for at in tiles(score.shape[1], LANES)], sums.shape[0])
    sums[:, width:] = block.astype(sums.dtype)
    chunk = sum_outs[0].shape[0]
    for at in range(0, rows, chunk):
        sums[at : at + chunk, width:] = sums[:chunk, width:]

    tile = 2 * FF_TILE if width % (2 * FF_TILE) == 0 else width

    def products(index):
        cut = pl.ds(pl.multiple_of(index * tile, tile), tile)
        part = contract(gate_grad[...], wg[cut, :], 1, 1)
        part += contract(up_grad[...], wu[cut, :], 1, 1)
        sums[:, cut] = (spread(gate[...], tile) * part).astype(jnp.bfloat16)

    loop(width // tile, products)
    at = 0
    for out in sum_outs:
        here = sums.at[pl.ds(at, out.shape[0]), pl.ds(0, out.shape[1])]
        results.append(copies.start(here, out))
        at += out.shape[0]
    wait(results)


def expert_call(me, gate, place, tok, grad, weights, after):
    rows = sum(part.shape[0] for part in tok)
    width, ff_width = weights[0].shape[1:]
    half = jnp.bfloat16
    narrow = pltpu.VMEM((rows, ff_width), half)
    return kernel_call(
        functools.partial(expert_kernel, len(tok)), (me,), (gate, place),
        (*tok, *grad, *weights),
        [shape(part.shape[0], width + LANES * (at > 1)) for at, part in enumerate(tok)]
        + [shape(rows, ff_width)] * 3,
        [pltpu.VMEM((rows, width), half), pltpu.VMEM((rows, grad[0].shape[1]), half)]
        + [pltpu.VMEM((rows, ff_width), jnp.float32)] * 3
        + [pltpu.VMEM((width, ff_width), half)] * 2 + [pltpu.VMEM((ff_width, width), half)]
        + [narrow] * 5 + [pltpu.VMEM((rows, width + LANES), half)]
        + [pltpu.VMEM((rows, LANES), jnp.float32)] * 2,
        2 * len(tok) + (len(tok) + 2) * len(tiles(width, 2 * FF_TILE))
        + len(tiles(ff_width, FF_TILE)) + 3,
        len(tok) + 3, after, 5 * rows * width * ff_width,
    )


def placed(rows, height):
    index = lax.broadcasted_iota(jnp.int32, (height, LANES), 0)
    block = jnp.zeros((height, LANES), jnp.float32)
    for at, row in enumerate(rows):
        block = jnp.where(index == at, jnp.broadcast_to(row, block.shape), block)
    return block


def first_rows(block, count):
    block = block.astype(jnp.float32)
    return [block[at : at + 1, :] for at in range(count)]


def order_matrix(place_ref, height):
    count = place_ref.shape[1]
    row = lax.broadcasted_iota(jnp.int32, (height, count), 0)
    return jnp.where(row == place_ref[...], 1.0, 0.0).astype(jnp.bfloat16)


def near_kernel(pieces, keep, got, out, keep_here, got_here, total, sems):
    copies = Copies(sems)
    wait([copies.start(keep, keep_here), copies.start(got, got_here)])
    width = total.shape[1] - LANES
    total[:, :width] = (
        keep_here[:, :width].astype(jnp.float32) + got_here[:, :width].astype(jnp.float32)
    ).astype(total.dtype)
    scores = first_rows(keep_here[: 2 * SUBLANES, width:], pieces)
    scores += first_rows(got_here[: 2 * SUBLANES, width:], pieces)
    total[:, width:] = placed(scores, total.shape[0]).astype(total.dtype)
    wait([copies.start(total, out)])


def ready_kernel(pieces, keep, got, near, across, *refs):
    outs, refs = (refs[: len(refs) - 6], refs[len(refs) - 6 :])
    keep_here, got_here, near_here, across_here, made, sems = refs
    copies = Copies(sems)
    wait(
        [
            copies.start(keep, keep_here), copies.start(got, got_here),
            copies.start(near, near_here), copies.start(across, across_here),
        ]
    )
    far = made.shape[0]
    rows = made.shape[1]
    width = keep_here.shape[1]
    scores = first_rows(near_here[: 4 * SUBLANES, width:], 2 * pieces)
    scores += first_rows(across_here[: 4 * SUBLANES, width:], 2 * pieces)
    block = placed(scores, rows)
    total = keep_here[...].astype(jnp.float32) + got_here[...].astype(jnp.float32)
    total += across_here[:, :width].astype(jnp.float32)
    results = []
    for k in range(far):
        made[k, :, :width] = total[k * rows : (k + 1) * rows, :].astype(made.dtype)
        made[k, :, width:] = block.astype(made.dtype)
        results.append(copies.start(made.at[k], outs[k]))
    wait(results)


def others_kernel(parts, start, me_ref, gate_ref, *refs):
    tok, grad, sources = (refs[:parts], refs[parts : 2 * parts], refs[2 * parts : 2 * parts + 3])
    outs, refs = (refs[2 * parts + 3 : 2 * parts + 6], refs[2 * parts + 6 :])
    rows_in, rows_grad, gate_pre, up_pre, hidden_grad, wg, wu, wd, hs, gs, us, gate, sems = refs
    copies = Copies(sems)
    rows, width = rows_in.shape
    ff_width = wd.shape[0]
    blocks = project_start(copies, tok, rows_in, sources, (wg, wu))
    grad_here = copies.stack(grad, rows_grad)
    down = Tiles(copies, sources[2].at[0], wd, 0, FF_TILE)
    project(blocks, rows_in, (gate_pre, up_pre), (wg, wu))
    backward(grad_here, rows_grad, hidden_grad, down)
    gate[...] = mask_of(me_ref, rows_grad[:, width : width + LANES])
    gate[...] *= gate_ref[start : start + rows, :]

    def terms(index):
        cut = row_cut(index)
        values = inner_terms(gate_pre[cut, :], up_pre[cut, :], hidden_grad[cut, :])
        sent = spread(rounded(gate[cut, :]), ff_width)
        for value, target in zip(values, (hs, gs, us)):
            target[cut, :] = (sent * value).astype(jnp.bfloat16)

    loop(rows // ROW_TILE, terms)
    wait([copies.start(source, out) for source, out in zip((hs, gs, us), outs)])


def others_call(me, gate, tok, grad, weights, start, after=()):
    rows = sum(part.shape[0] for part in tok)
    width, ff_width = weights[0].shape[1:]
    half = jnp.bfloat16
    return kernel_call(
        functools.partial(others_kernel, len(tok), start), (me,), (gate,), (*tok, *grad, *weights),
        [shape(rows, ff_width)] * 3,
        [pltpu.VMEM((rows, width), half), pltpu.VMEM((rows, grad[0].shape[1]), half)]
        + [pltpu.VMEM((rows, ff_width), jnp.float32)] * 3
        + [pltpu.VMEM((width, ff_width), half)] * 2 + [pltpu.VMEM((ff_width, width), half)]
        + [pltpu.VMEM((rows, ff_width), half)] * 3 + [pltpu.VMEM((rows, LANES), jnp.float32)],
        len(tok) + (len(tok) + 2) * len(tiles(width, 2 * FF_TILE))
        + len(tiles(ff_width, FF_TILE)) + 3,
        3, after, 3 * rows * width * ff_width,
    )


def weights_kernel(parts, given, steps, group_ref, *refs):
    tok, grad, given_refs = (refs[:parts], refs[parts : 2 * parts], refs[2 * parts :][: 3 * given])
    outs, refs = (refs[2 * parts + 3 * given :][:3], refs[2 * parts + 3 * given + 3 :])
    hs, gs, us, tok_half, grad_all, hidden_half, *tile_out, sems = refs
    copies = Copies(sems)
    width = grad_all.shape[1]
    half = outs[0].shape[1]
    half_ff = outs[2].shape[1]
    blocks = [given_refs[kind * given : (kind + 1) * given] for kind in range(3)]
    mine = pl.ds(pl.multiple_of(group_ref[0] * half, LANES), half)
    gate_here = copies.stack(tok, tok_half, mine) + copies.stack(blocks[1], gs)
    up_here = copies.stack(blocks[2], us)
    down_here = copies.stack(blocks[0], hs) + copies.stack(grad, grad_all, pl.ds(0, width))
    base = copies.count

    def result(which, step):
        tile = tile_out[which].shape[1 if which < 2 else 2]
        at = step * tile if isinstance(step, int) else pl.multiple_of(step * tile, tile)
        cut = pl.ds(at, tile)
        target = outs[which].at[0, cut, :] if which < 2 else outs[which].at[0, :, cut]
        return cut, pltpu.make_async_copy(
            tile_out[which].at[step], target, sems.at[base + which * steps + step]
        )

    def form(which, left, right):
        def body(step):
            cut, copy = result(which, step)
            sides = (left[:, cut], right[...]) if which < 2 else (left[...], right[:, cut])
            tile_out[which][step] = contract(*sides, 0, 0).astype(tile_out[which].dtype)
            copy.start()

        loop(steps, body, rolled=False)

    wait(gate_here)
    form(0, tok_half, gs)
    wait(up_here)
    form(1, tok_half, us)
    wait(down_here)
    if half_ff % LANES == 0:
        place = pl.ds(pl.multiple_of(group_ref[0] * half_ff, LANES), half_ff)
        hidden_half[...] = hs[:, place]
    else:
        for index in range(hs.shape[1] // half_ff):

            @pl.when(group_ref[0] == index)
            def _():
                hidden_half[...] = hs[:, index * half_ff : (index + 1) * half_ff]

    form(2, hidden_half, grad_all)
    wait([result(which, step)[1] for which in range(3) for step in range(steps)])


def weights_call(group, groups, tok, grad, given, dtype, after=()):
    width, ff_width = (tok[0].shape[1], given[0][0].shape[1])
    half, half_ff = (width // groups, ff_width // groups)
    rows = sum(part.shape[0] for part in tok)
    steps = max(s for s in (4, 2, 1) if half % (s * LANES) == 0)
    low = jnp.bfloat16
    scratch = [pltpu.VMEM((rows, ff_width), low)] * 3
    scratch += [
        pltpu.VMEM((rows, half), low),
        pltpu.VMEM((rows, width), low),
        pltpu.VMEM((rows, half_ff), low),
        pltpu.VMEM((steps, half // steps, ff_width), dtype),
        pltpu.VMEM((steps, half // steps, ff_width), dtype),
        pltpu.VMEM((steps, half_ff, width // steps), dtype),
    ]
    return kernel_call(
        functools.partial(weights_kernel, len(tok), len(given), steps), (group,), (),
        (*tok, *grad, *(block[kind] for kind in range(3) for block in given)),
        [
            jax.ShapeDtypeStruct((1, half, ff_width), dtype),
            jax.ShapeDtypeStruct((1, half, ff_width), dtype),
            jax.ShapeDtypeStruct((1, half_ff, width), dtype),
        ],
        scratch, 2 * len(tok) + 3 * len(given) + 3 * steps, 3, after, 3 * rows * half * ff_width,
    )


def router_kernel(parts, me_ref, *refs):
    logits_ref, score_ref, place_ref, *tok = refs[: 3 + parts]
    grad_ref, router_ref, rows, sems = refs[3 + parts :]
    copies = Copies(sems)
    rows_here = copies.stack(tok, rows)
    logits = logits_ref[...]
    experts = logits.shape[0]
    row = lax.broadcasted_iota(jnp.int32, (experts, experts), 0)
    column = lax.broadcasted_iota(jnp.int32, (experts, experts), 1)
    unswap = jnp.where((row ^ me_ref[0]) == column, 1.0, 0.0).astype(jnp.bfloat16)
    group = score_ref.shape[2]
    order = order_matrix(place_ref, group)
    score = jnp.concatenate(
        [contract(score_ref[at], order, 1, 0) for at in range(score_ref.shape[0])], axis=1
    )
    score = contract(unswap, score.astype(jnp.bfloat16), 1, 0)
    state = balancer_forward_pass(logits)
    grad = balancer_adjoint_pass(experts * score, *state).astype(jnp.bfloat16)
    grad_ref[...] = grad
    wait(rows_here)
    router_ref[...] = contract(grad, rows[...], 1, 0)


def per_device(tokens, out_grad, expert_ids, router_weight, w_gate, w_up, w_down):
    tok_rows, width = tokens.shape
    experts = router_weight.shape[1]
    groups = lax.axis_size("dp")
    far = lax.axis_size("expert") // 4
    chunk = 2 * far * tok_rows
    me = lax.axis_index("expert").astype(jnp.int32)[None]
    group = lax.axis_index("dp").astype(jnp.int32)[None]

    def along(array):
        return jnp.concatenate([array] + [swap_expert(array, 4 * k) for k in range(1, far)], axis=0)

    tok_line = along(tokens)
    (packed,) = kernel_call(
        pack_kernel, (), (expert_ids, tokens, router_weight.T), (),
        [shape(tok_rows, round_up(4 * experts, LANES))], (), 0,
    )
    columns = [out_grad, packed[:, : 4 * experts]]
    for offset in range(1, groups):
        columns.append(swap_group(packed, offset)[:, experts : 4 * experts])
    extra = (3 * groups + 1) * experts
    columns.append(jnp.zeros((tok_rows, round_up(extra, LANES) - extra), jnp.bfloat16))
    grad_line = along(jnp.concatenate(columns, axis=1))
    tok_next = swap_expert(tok_line, 2)
    grad_next = swap_expert(grad_line, 2)
    tok_own = [(tok_line, swap_expert(tok_line, 1)), (tok_next, swap_expert(tok_next, 1))]
    grad_own = [(grad_line, swap_expert(grad_line, 1)), (grad_next, swap_expert(grad_next, 1))]

    tok_parts = [rows for pair in tok_own for rows in pair]
    grad_parts = [rows for pair in grad_own for rows in pair]
    weights = (w_gate, w_up, w_down)

    at_once = 2 * groups * chunk <= ROWS_AT_ONCE

    def moved(parts, offset):
        out = []
        for part in parts:
            part = swap_group(part, offset)
            out += [part, swap_expert(part, 1)]
        return out

    moved_tok = moved((tok_line, tok_next), 1) if at_once else []
    moved_grad = moved((grad_line, grad_next), 1) if at_once else []
    early = []
    if at_once:
        for part, hops in ((moved_tok[1], 2), (tok_parts[3], 3)):
            corner = part[: 2 * SUBLANES, :LANES]
            for _ in range(hops):
                corner = swap_expert(corner, 1)
            early.append(corner)
    extra = grad_line.shape[1] - width
    gate, logits = kernel_call(
        functools.partial(gate_kernel, len(grad_parts), experts), (me,), (), grad_parts,
        [shape(2 * chunk * groups, LANES, jnp.float32), shape(experts, 2 * chunk * groups, jnp.float32)],
        [pltpu.VMEM((2 * chunk, extra), jnp.bfloat16)], len(grad_parts), 0, early,
    )
    slots = [4 * j + 2 * i + k for i in range(2) for k in range(2) for j in range(far)]
    slots = jnp.array(slots, jnp.int32) ^ me
    place = slots[:, None] * tok_rows + jnp.arange(tok_rows, dtype=jnp.int32)[None, :]
    place = place.reshape(1, 2 * chunk)
    pieces = round_up(2 * chunk, LANES) // LANES

    keep0, send0, keep1, send1, *scaled = expert_call(
        me, gate, place, tok_parts, grad_parts, weights, moved_tok[2:3]
    )
    given = [scaled]
    got1, got0 = (swap_expert(send1, 1), swap_expert(send0, 1))
    (near,) = kernel_call(
        functools.partial(near_kernel, pieces), (), (), (keep1, got1), [shape(*keep1.shape)],
        [pltpu.VMEM(keep1.shape, keep1.dtype)] * 3, 3, 1, moved_grad[0::2],
    )
    across = swap_expert(near, 2)
    ready = kernel_call(
        functools.partial(ready_kernel, pieces), (), (), (keep0, got0, near, across),
        [shape(tok_rows, width + LANES)] * far,
        [pltpu.VMEM(keep0.shape, keep0.dtype)] * 2 + [pltpu.VMEM(near.shape, near.dtype)] * 2
        + [pltpu.VMEM((far, tok_rows, width + LANES), near.dtype)], 4 + far, far,
    )
    arrived = [ready[0]] + [swap_expert(ready[k], 4 * k) for k in range(1, far)]
    row_sum = sum(part[:, :width].astype(jnp.float32) for part in arrived)
    score = jnp.stack([part[: 4 * pieces, width:] for part in arrived])
    score = score.reshape(experts, pieces * LANES)
    score = jnp.stack([score] + [swap_group(score, offset) for offset in range(1, groups)])
    to_send = ready[1:]

    token_rows = list(tok_parts)
    totals = None
    if not at_once:
        totals = weights_call(group, groups, tok_parts, grad_parts, given, jnp.float32)
        tok_parts, grad_parts, given = ([], [], [])
    for offset in range(1, groups):
        if not at_once:
            (tok_line, tok_next, grad_line, grad_next), totals = lax.optimization_barrier(
                ((tok_line, tok_next, grad_line, grad_next), totals)
            )
            moved_tok = moved((tok_line, tok_next), offset)
            moved_grad = moved((grad_line, grad_next), offset)
        token_rows += moved_tok
        fresh = others_call(me, gate, moved_tok, moved_grad, weights, 2 * chunk * offset)
        terms = weights_call(
            group, groups, tok_parts + moved_tok, grad_parts + moved_grad, given + [fresh],
            jnp.bfloat16 if at_once else jnp.float32, to_send,
        )
        totals = terms if totals is None else [t + u for t, u in zip(totals, terms)]
    final = [t.astype(jnp.bfloat16) for t in totals]

    logit_grad, grad_router = kernel_call(
        functools.partial(router_kernel, len(token_rows)), (me,), (logits, score, place), token_rows,
        [shape(*logits.shape), shape(experts, width, jnp.float32)],
        [pltpu.VMEM((logits.shape[1], width), jnp.bfloat16)], len(token_rows),
    )
    row_sum = row_sum + contract(logit_grad[:, :tok_rows], router_weight, 0, 1)
    return (row_sum.astype(jnp.bfloat16), grad_router.T, *final)


def solution(mesh):
    in_specs = (
        P(("dp", "expert"), None),
        P(("dp", "expert"), None),
        P(("dp", "expert"), None),
        P(),
        P("expert", None, None),
        P("expert", None, None),
        P("expert", None, None),
    )
    out_specs = (
        P(("dp", "expert"), None),
        P(),
        P("expert", "dp", None),
        P("expert", "dp", None),
        P("expert", "dp", None),
    )
    return jax.shard_map(
        per_device, mesh=mesh, in_specs=in_specs, out_specs=out_specs, check_vma=False
    )
```

```python
import functools

import jax
import jax.numpy as jnp
from jax import lax
from jax.experimental import pallas as pl
from jax.experimental.pallas import tpu as pltpu
from jax.sharding import PartitionSpec as P

PASSES = 3
LANES = 128
SUBLANES = 8
FF_TILE = 256
ROW_TILE = 32
GRANT = 56 << 20
ROWS_AT_ONCE = 1024


def swap_expert(array, offset):
    size = lax.axis_size("expert")
    return lax.ppermute(array, "expert", [(i, i ^ offset) for i in range(size)])


def swap_group(array, offset):
    size = lax.axis_size("dp")
    return lax.ppermute(array, "dp", [(i, i ^ offset) for i in range(size)])


def contract(left, right, left_dim, right_dim):
    return lax.dot_general(
        left, right, (((left_dim,), (right_dim,)), ((), ())), preferred_element_type=jnp.float32
    )


def balancer_forward_pass(logits):
    densities = [jnp.exp(logits)]
    quotients, column_totals, row_totals = ([], [], [])
    for _ in range(PASSES):
        column_sum = jnp.sum(densities[-1], axis=1, keepdims=True)
        quotient = densities[-1] / column_sum
        row_sum = jnp.sum(quotient, axis=0, keepdims=True)
        densities.append(quotient / row_sum)
        quotients.append(quotient)
        column_totals.append(column_sum)
        row_totals.append(row_sum)
    return (densities, quotients, column_totals, row_totals)


def balancer_adjoint_pass(density_gradient, densities, quotients, column_totals, row_totals):
    for repeat in reversed(range(PASSES)):
        inner = jnp.sum(density_gradient * densities[repeat + 1], axis=0, keepdims=True)
        quotient_grad = (density_gradient - inner) / row_totals[repeat]
        shared = jnp.sum(quotient_grad * quotients[repeat], axis=1, keepdims=True)
        density_gradient = (quotient_grad - shared) / column_totals[repeat]
    return density_gradient * densities[0]


def round_up(value, unit):
    return -(-value // unit) * unit


def pack_kernel(slots, me_ref, ids_ref, tok_ref, router_ref, out, place_ref):
    experts = router_ref.shape[0]
    rows = tok_ref.shape[0]
    at = lax.broadcasted_iota(jnp.int32, place_ref.shape, 1)
    place = jnp.zeros(place_ref.shape, jnp.int32)
    for index, offset in enumerate(slots):
        first = index * rows
        here = (at >= first) & (at < first + rows)
        place = jnp.where(here, (me_ref[0] ^ offset) * rows + at - first, place)
    place_ref[...] = place
    rest = contract(tok_ref[...], router_ref[...], 1, 1)
    lane = lax.broadcasted_iota(jnp.int32, out.shape, 1)
    packed = jnp.zeros(out.shape, jnp.float32)
    for pick in range(ids_ref.shape[1]):
        packed += jnp.where(lane == ids_ref[:, pick : pick + 1], 1.0, 0.0)
    row = lax.broadcasted_iota(jnp.int32, (experts, out.shape[1]), 0)
    column = lax.broadcasted_iota(jnp.int32, (experts, out.shape[1]), 1)
    for term in range(1, 4):
        part = rest.astype(jnp.bfloat16)
        rest = rest - part.astype(jnp.float32)
        place = jnp.where(column == row + term * experts, 1.0, 0.0).astype(jnp.bfloat16)
        packed += contract(part, place, 1, 0)
    out[...] = packed.astype(jnp.bfloat16)


def gate_kernel(parts, experts, me_ref, *refs):
    grad, gate_out, logits_out = (refs[:parts], *refs[parts : parts + 2])
    packed, gate_ref, logits_ref, sems = refs[parts + 2 :]
    copies = Copies(sems)
    extra = packed.shape[1]
    wait(copies.stack(grad, packed, pl.ds(grad[0].shape[1] - extra, extra)))
    turned = jnp.transpose(packed[...].astype(jnp.float32))
    columns = []
    for group in range(logits_ref.shape[1] // packed.shape[0]):
        at = (3 * group + 1) * experts
        terms = [turned[at + i * experts : at + (i + 1) * experts] for i in range(3)]
        columns.append(terms[0] + terms[1] + terms[2])
    logits = jnp.concatenate(columns, axis=1)
    logits_ref[...] = logits
    results = [copies.start(logits_ref, logits_out)]
    gates = experts * balancer_forward_pass(logits)[0][-1]
    row = lax.broadcasted_iota(jnp.int32, gates.shape, 0)
    mine = jnp.sum(jnp.where(row == me_ref[0], gates, 0.0), axis=0, keepdims=True)
    gate_ref[...] = jnp.transpose(jnp.broadcast_to(mine, (LANES, gates.shape[1])))
    wait([*results, copies.start(gate_ref, gate_out)])


def kernel_call(
    kernel, scalars, small, large, out_shape, scratch, copies, large_outs=0, after=(), macs=10**6
):
    whole = pl.BlockSpec(memory_space=pltpu.VMEM)
    outside = pl.BlockSpec(memory_space=pltpu.HBM)
    inputs = len(scalars) + len(small) + len(large)

    def body(*refs):
        kernel(*refs[:inputs], *refs[inputs + len(after) :])

    return pl.pallas_call(
        body,
        in_specs=[pl.BlockSpec(memory_space=pltpu.SMEM)] * len(scalars)
        + [whole] * len(small)
        + [outside] * (len(large) + len(after)),
        out_specs=[outside] * large_outs + [whole] * (len(out_shape) - large_outs),
        out_shape=out_shape,
        scratch_shapes=[*scratch] + [pltpu.SemaphoreType.DMA((copies,))] * (copies > 0),
        compiler_params=pltpu.CompilerParams(vmem_limit_bytes=GRANT),
        cost_estimate=pl.CostEstimate(
            flops=2 * macs, bytes_accessed=macs // 200, transcendentals=macs // 10000
        ),
    )(*scalars, *small, *large, *after)


def shape(rows, columns, dtype=jnp.bfloat16):
    return jax.ShapeDtypeStruct((rows, columns), dtype)


def tiles(extent, tile):
    tile = tile if extent % tile == 0 else extent
    return [slice(at, at + tile) for at in range(0, extent, tile)]


class Copies:
    def __init__(self, sems):
        self.sems, self.count = (sems, 0)

    def start(self, source, target):
        copy = pltpu.make_async_copy(source, target, self.sems.at[self.count])
        self.count += 1
        copy.start()
        return copy

    def stack(self, parts, target, columns=slice(None)):
        started, at = ([], 0)
        for part in parts:
            rows = part.shape[0]
            started.append(self.start(part.at[:, columns], target.at[pl.ds(at, rows), :]))
            at += rows
        return started


def wait(copies):
    for copy in copies:
        copy.wait()


def loop(count, body, rolled=True):
    if not rolled:
        for index in range(count):
            body(index)
        return

    def step(index, carry):
        body(index)
        return carry

    lax.fori_loop(0, count, step, 0)


class Tiles:
    def __init__(self, copies, source, target, dim, tile):
        extent = target.shape[dim]
        self.tile = tile if extent % tile == 0 else extent
        self.count = extent // self.tile
        self.source, self.target, self.dim = (source, target, dim)
        self.sems, self.base = (copies.sems, copies.count)
        copies.count += self.count
        for index in range(self.count):
            self.copy(index).start()

    def here(self, index):
        start = index * self.tile
        if not isinstance(index, int):
            start = pl.multiple_of(start, self.tile)
        cut = pl.ds(start, self.tile)
        return (cut, slice(None)) if self.dim == 0 else (slice(None), cut)

    def copy(self, index):
        here = self.here(index)
        return pltpu.make_async_copy(
            self.source.at[here], self.target.at[here], self.sems.at[self.base + index]
        )


def mask_of(me_ref, picked):
    row = lax.broadcasted_iota(jnp.int32, (LANES, LANES), 0)
    mine = jnp.where(row == me_ref[0], 1.0, 0.0).astype(jnp.bfloat16)
    return contract(picked, mine, 1, 0)


def spread(lanes, width):
    return jnp.concatenate([lanes] * (width // LANES), axis=1)


def rounded(array):
    return array.astype(jnp.bfloat16).astype(jnp.float32)


def inner_terms(gate_pre, up_pre, hidden_grad):
    sigmoid_gate = jax.nn.sigmoid(gate_pre)
    activation = gate_pre * sigmoid_gate
    hidden = activation * up_pre
    gate_grad = hidden_grad * up_pre * sigmoid_gate * (1.0 + gate_pre * (1.0 - sigmoid_gate))
    up_grad = hidden_grad * activation
    half = jnp.bfloat16
    return hidden, gate_grad.astype(half), up_grad.astype(half)


def project_start(copies, tok, rows_in, sources, weights):
    width = rows_in.shape[1]
    tile = 2 * FF_TILE if width % (2 * FF_TILE) == 0 else width
    blocks = []
    for start in range(0, width, tile):
        cut = pl.ds(start, tile)
        here, at = ([], 0)
        for part in tok:
            rows = pl.ds(at, part.shape[0])
            here.append(copies.start(part.at[:, cut], rows_in.at[rows, cut]))
            at += part.shape[0]
        for source, weight in zip(sources, weights):
            here.append(copies.start(source.at[0, cut, :], weight.at[cut, :]))
        blocks.append((slice(start, start + tile), here))
    return blocks


def project(blocks, rows_in, targets, weights):
    for cut, here in blocks:
        wait(here)
        for target, weight in zip(targets, weights):
            value = contract(rows_in[:, cut], weight[cut, :], 1, 0)
            if cut.start == 0:
                target[...] = value
            else:
                target[...] += value


def backward(grad_here, rows_grad, hidden_grad, weight):
    wait(grad_here)

    def body(index):
        weight.copy(index).wait()
        cut = weight.here(index)[0]
        rows = rows_grad[:, : weight.target.shape[1]]
        hidden_grad[:, cut] = contract(rows, weight.target[cut, :], 1, 1)

    loop(weight.count, body)


def row_cut(index):
    start = index * ROW_TILE
    return pl.ds(start if isinstance(index, int) else pl.multiple_of(start, ROW_TILE), ROW_TILE)


def expert_kernel(parts, me_ref, place_ref, gate_all, *refs):
    tok, grad, sources = (refs[:parts], refs[parts : 2 * parts], refs[2 * parts : 2 * parts + 3])
    refs = refs[2 * parts + 3 :]
    sum_outs, scaled_outs = (refs[:parts], refs[parts : parts + 3])
    rows_in, rows_grad, gate_pre, up_pre, hidden_grad, *refs = refs[parts + 3 :]
    wg, wu, wd, gate_grad, up_grad, hs, gs, us, sums, column, gate, sems = refs
    copies = Copies(sems)
    width = wg.shape[0]
    rows = gate_pre.shape[0]
    ff_width = wd.shape[0]
    blocks = project_start(copies, tok, rows_in, sources, (wg, wu))
    grad_here = copies.stack(grad, rows_grad)
    grad_here.append(copies.start(gate_all.at[pl.ds(0, rows), :], gate))
    down = Tiles(copies, sources[2].at[0], wd, 0, FF_TILE)
    project(blocks, rows_in, (gate_pre, up_pre), (wg, wu))
    backward(grad_here, rows_grad, hidden_grad, down)
    column[...] = mask_of(me_ref, rows_grad[:, width : width + LANES])
    gate[...] *= column[...]

    def terms(index):
        cut = row_cut(index)
        values = inner_terms(gate_pre[cut, :], up_pre[cut, :], hidden_grad[cut, :])
        gate_grad[cut, :] = values[1]
        up_grad[cut, :] = values[2]
        sent = spread(rounded(gate[cut, :]), ff_width)
        for value, target in zip(values, (hs, gs, us)):
            target[cut, :] = (sent * value).astype(jnp.bfloat16)
        product = hidden_grad[cut, :] * values[0]
        column[cut, :] *= sum(product[:, at] for at in tiles(ff_width, LANES))

    loop(rows // ROW_TILE, terms)
    results = [copies.start(source, out) for source, out in zip((hs, gs, us), scaled_outs)]
    ones = jnp.ones((SUBLANES, LANES), jnp.bfloat16)
    high = column[...].astype(jnp.bfloat16)
    low = (column[...] - high.astype(jnp.float32)).astype(jnp.bfloat16)
    score = (contract(ones, high, 1, 1) + contract(ones, low, 1, 1)).astype(jnp.bfloat16)
    score = contract(score, order_matrix(place_ref, round_up(rows, LANES)), 1, 1)
    block = placed([score[:1, at] for at in tiles(score.shape[1], LANES)], sums.shape[0])
    sums[:, width:] = block.astype(sums.dtype)
    chunk = sum_outs[0].shape[0]
    for at in range(0, rows, chunk):
        sums[at : at + chunk, width:] = sums[:chunk, width:]

    tile = 2 * FF_TILE if width % (2 * FF_TILE) == 0 else width

    def products(index):
        cut = pl.ds(pl.multiple_of(index * tile, tile), tile)
        part = contract(gate_grad[...], wg[cut, :], 1, 1)
        part += contract(up_grad[...], wu[cut, :], 1, 1)
        sums[:, cut] = (spread(gate[...], tile) * part).astype(jnp.bfloat16)

    loop(width // tile, products)
    at = 0
    for out in sum_outs:
        here = sums.at[pl.ds(at, out.shape[0]), pl.ds(0, out.shape[1])]
        results.append(copies.start(here, out))
        at += out.shape[0]
    wait(results)


def expert_call(me, gate, place, tok, grad, weights, after):
    rows = sum(part.shape[0] for part in tok)
    width, ff_width = weights[0].shape[1:]
    half = jnp.bfloat16
    narrow = pltpu.VMEM((rows, ff_width), half)
    return kernel_call(
        functools.partial(expert_kernel, len(tok)), (me,), (place,),
        (gate, *tok, *grad, *weights),
        [shape(part.shape[0], width + LANES * (at > 1)) for at, part in enumerate(tok)]
        + [shape(rows, ff_width)] * 3,
        [pltpu.VMEM((rows, width), half), pltpu.VMEM((rows, grad[0].shape[1]), half)]
        + [pltpu.VMEM((rows, ff_width), jnp.float32)] * 3
        + [pltpu.VMEM((width, ff_width), half)] * 2 + [pltpu.VMEM((ff_width, width), half)]
        + [narrow] * 5 + [pltpu.VMEM((rows, width + LANES), half)]
        + [pltpu.VMEM((rows, LANES), jnp.float32)] * 2,
        2 * len(tok) + (len(tok) + 2) * len(tiles(width, 2 * FF_TILE))
        + len(tiles(ff_width, FF_TILE)) + 4,
        len(tok) + 3, after, 5 * rows * width * ff_width,
    )


def placed(rows, height):
    index = lax.broadcasted_iota(jnp.int32, (height, LANES), 0)
    block = jnp.zeros((height, LANES), jnp.float32)
    for at, row in enumerate(rows):
        block = jnp.where(index == at, jnp.broadcast_to(row, block.shape), block)
    return block


def first_rows(block, count):
    block = block.astype(jnp.float32)
    return [block[at : at + 1, :] for at in range(count)]


def order_matrix(place_ref, height):
    count = place_ref.shape[1]
    row = lax.broadcasted_iota(jnp.int32, (height, count), 0)
    return jnp.where(row == place_ref[...], 1.0, 0.0).astype(jnp.bfloat16)


def near_kernel(pieces, keep, got, out, score_out, keep_here, got_here, total, sems):
    copies = Copies(sems)
    wait([copies.start(keep, keep_here), copies.start(got, got_here)])
    width = total.shape[1] - LANES
    total[:, :width] = (
        keep_here[:, :width].astype(jnp.float32) + got_here[:, :width].astype(jnp.float32)
    ).astype(total.dtype)
    scores = first_rows(keep_here[: 2 * SUBLANES, width:], pieces)
    scores += first_rows(got_here[: 2 * SUBLANES, width:], pieces)
    block = placed(scores, total.shape[0]).astype(total.dtype)
    total[:, width:] = block
    score_out[...] = block[: score_out.shape[0]]
    wait([copies.start(total, out)])


def ready_kernel(pieces, others, *refs):
    other_scores, (keep, got, near, across, *refs) = (refs[:others], refs[others:])
    outs, refs = (refs[: len(refs) - 6], refs[len(refs) - 6 :])
    keep_here, got_here, near_here, across_here, made, sems = refs
    copies = Copies(sems)
    wait(
        [
            copies.start(keep, keep_here), copies.start(got, got_here),
            copies.start(near, near_here), copies.start(across, across_here),
        ]
    )
    far = made.shape[0]
    rows = made.shape[1]
    width = keep_here.shape[1]
    scores = first_rows(near_here[: 4 * SUBLANES, width:], 2 * pieces)
    scores += first_rows(across_here[: 4 * SUBLANES, width:], 2 * pieces)
    for other in other_scores:
        scores += first_rows(other[...], 2 * pieces)
    blocks = [placed(scores[at : at + rows], rows) for at in range(0, len(scores), rows)]
    block = jnp.concatenate(blocks, axis=1)
    total = keep_here[...].astype(jnp.float32) + got_here[...].astype(jnp.float32)
    total += across_here[:, :width].astype(jnp.float32)
    results = []
    for k in range(far):
        made[k, :, :width] = total[k * rows : (k + 1) * rows, :].astype(made.dtype)
        made[k, :, width:] = block.astype(made.dtype)
        results.append(copies.start(made.at[k], outs[k]))
    wait(results)


def others_kernel(parts, start, me_ref, gate_all, *refs):
    tok, grad, sources = (refs[:parts], refs[parts : 2 * parts], refs[2 * parts : 2 * parts + 3])
    outs, refs = (refs[2 * parts + 3 : 2 * parts + 6], refs[2 * parts + 6 :])
    rows_in, rows_grad, gate_pre, up_pre, hidden_grad, wg, wu, wd, hs, gs, us, gate, sems = refs
    copies = Copies(sems)
    rows, width = rows_in.shape
    ff_width = wd.shape[0]
    blocks = project_start(copies, tok, rows_in, sources, (wg, wu))
    grad_here = copies.stack(grad, rows_grad)
    grad_here.append(copies.start(gate_all.at[pl.ds(start, rows), :], gate))
    down = Tiles(copies, sources[2].at[0], wd, 0, FF_TILE)
    project(blocks, rows_in, (gate_pre, up_pre), (wg, wu))
    backward(grad_here, rows_grad, hidden_grad, down)
    gate[...] *= mask_of(me_ref, rows_grad[:, width : width + LANES])

    def terms(index):
        cut = row_cut(index)
        values = inner_terms(gate_pre[cut, :], up_pre[cut, :], hidden_grad[cut, :])
        sent = spread(rounded(gate[cut, :]), ff_width)
        for value, target in zip(values, (hs, gs, us)):
            target[cut, :] = (sent * value).astype(jnp.bfloat16)

    loop(rows // ROW_TILE, terms)
    wait([copies.start(source, out) for source, out in zip((hs, gs, us), outs)])


def others_call(me, gate, tok, grad, weights, start, after=()):
    rows = sum(part.shape[0] for part in tok)
    width, ff_width = weights[0].shape[1:]
    half = jnp.bfloat16
    return kernel_call(
        functools.partial(others_kernel, len(tok), start), (me,), (),
        (gate, *tok, *grad, *weights),
        [shape(rows, ff_width)] * 3,
        [pltpu.VMEM((rows, width), half), pltpu.VMEM((rows, grad[0].shape[1]), half)]
        + [pltpu.VMEM((rows, ff_width), jnp.float32)] * 3
        + [pltpu.VMEM((width, ff_width), half)] * 2 + [pltpu.VMEM((ff_width, width), half)]
        + [pltpu.VMEM((rows, ff_width), half)] * 3 + [pltpu.VMEM((rows, LANES), jnp.float32)],
        len(tok) + (len(tok) + 2) * len(tiles(width, 2 * FF_TILE))
        + len(tiles(ff_width, FF_TILE)) + 4,
        3, after, 3 * rows * width * ff_width,
    )


def weights_kernel(parts, given, steps, group_ref, *refs):
    tok, grad, given_refs = (refs[:parts], refs[parts : 2 * parts], refs[2 * parts :][: 3 * given])
    outs, refs = (refs[2 * parts + 3 * given :][:3], refs[2 * parts + 3 * given + 3 :])
    hs, gs, us, tok_half, grad_all, hidden_half, *tile_out, sems = refs
    copies = Copies(sems)
    width = grad_all.shape[1]
    half = outs[0].shape[1]
    half_ff = outs[2].shape[1]
    blocks = [given_refs[kind * given : (kind + 1) * given] for kind in range(3)]
    mine = pl.ds(pl.multiple_of(group_ref[0] * half, LANES), half)
    gate_here = copies.stack(tok, tok_half, mine) + copies.stack(blocks[1], gs)
    up_here = copies.stack(blocks[2], us)
    down_here = copies.stack(blocks[0], hs) + copies.stack(grad, grad_all, pl.ds(0, width))
    base = copies.count

    def result(which, step):
        tile = tile_out[which].shape[1 if which < 2 else 2]
        at = step * tile if isinstance(step, int) else pl.multiple_of(step * tile, tile)
        cut = pl.ds(at, tile)
        target = outs[which].at[0, cut, :] if which < 2 else outs[which].at[0, :, cut]
        return cut, pltpu.make_async_copy(
            tile_out[which].at[step], target, sems.at[base + which * steps + step]
        )

    def form(which, left, right):
        def body(step):
            cut, copy = result(which, step)
            sides = (left[:, cut], right[...]) if which < 2 else (left[...], right[:, cut])
            tile_out[which][step] = contract(*sides, 0, 0).astype(tile_out[which].dtype)
            copy.start()

        loop(steps, body, rolled=False)

    wait(gate_here)
    form(0, tok_half, gs)
    wait(up_here)
    form(1, tok_half, us)
    wait(down_here)
    if half_ff % LANES == 0:
        place = pl.ds(pl.multiple_of(group_ref[0] * half_ff, LANES), half_ff)
        hidden_half[...] = hs[:, place]
    else:
        for index in range(hs.shape[1] // half_ff):

            @pl.when(group_ref[0] == index)
            def _():
                hidden_half[...] = hs[:, index * half_ff : (index + 1) * half_ff]

    form(2, hidden_half, grad_all)
    wait([result(which, step)[1] for which in range(3) for step in range(steps)])


def weights_call(group, groups, tok, grad, given, dtype, after=()):
    width, ff_width = (tok[0].shape[1], given[0][0].shape[1])
    half, half_ff = (width // groups, ff_width // groups)
    rows = sum(part.shape[0] for part in tok)
    steps = max(s for s in (4, 2, 1) if half % (s * LANES) == 0)
    low = jnp.bfloat16
    scratch = [pltpu.VMEM((rows, ff_width), low)] * 3
    scratch += [
        pltpu.VMEM((rows, half), low),
        pltpu.VMEM((rows, width), low),
        pltpu.VMEM((rows, half_ff), low),
        pltpu.VMEM((steps, half // steps, ff_width), dtype),
        pltpu.VMEM((steps, half // steps, ff_width), dtype),
        pltpu.VMEM((steps, half_ff, width // steps), dtype),
    ]
    return kernel_call(
        functools.partial(weights_kernel, len(tok), len(given), steps), (group,), (),
        (*tok, *grad, *(block[kind] for kind in range(3) for block in given)),
        [
            jax.ShapeDtypeStruct((1, half, ff_width), dtype),
            jax.ShapeDtypeStruct((1, half, ff_width), dtype),
            jax.ShapeDtypeStruct((1, half_ff, width), dtype),
        ],
        scratch, 2 * len(tok) + 3 * len(given) + 3 * steps, 3, after, 3 * rows * half * ff_width,
    )


def router_kernel(parts, me_ref, *refs):
    score_ref, place_ref, logits_all, *tok = refs[: 3 + parts]
    grad_ref, router_ref, rows, logits_ref, sems = refs[3 + parts :]
    copies = Copies(sems)
    logits_here = copies.start(logits_all, logits_ref)
    rows_here = copies.stack(tok, rows)
    logits_here.wait()
    logits = logits_ref[...]
    experts = logits.shape[0]
    row = lax.broadcasted_iota(jnp.int32, (experts, experts), 0)
    column = lax.broadcasted_iota(jnp.int32, (experts, experts), 1)
    unswap = jnp.where((row ^ me_ref[0]) == column, 1.0, 0.0).astype(jnp.bfloat16)
    group = score_ref.shape[2]
    order = order_matrix(place_ref, group)
    score = jnp.concatenate(
        [contract(score_ref[at], order, 1, 0) for at in range(score_ref.shape[0])], axis=1
    )
    score = contract(unswap, score.astype(jnp.bfloat16), 1, 0)
    state = balancer_forward_pass(logits)
    grad = balancer_adjoint_pass(experts * score, *state).astype(jnp.bfloat16)
    grad_ref[...] = grad
    wait(rows_here)
    router_ref[...] = contract(grad, rows[...], 1, 0)


def per_device(tokens, out_grad, expert_ids, router_weight, w_gate, w_up, w_down):
    tok_rows, width = tokens.shape
    experts = router_weight.shape[1]
    groups = lax.axis_size("dp")
    far = lax.axis_size("expert") // 4
    chunk = 2 * far * tok_rows
    me = lax.axis_index("expert").astype(jnp.int32)[None]
    group = lax.axis_index("dp").astype(jnp.int32)[None]

    def along(array):
        return jnp.concatenate([array] + [swap_expert(array, 4 * k) for k in range(1, far)], axis=0)

    tok_line = along(tokens)
    slots = [4 * j + 2 * i + k for i in range(2) for k in range(2) for j in range(far)]
    packed, place = kernel_call(
        functools.partial(pack_kernel, slots), (me,), (expert_ids, tokens, router_weight.T), (),
        [shape(tok_rows, round_up(4 * experts, LANES)), shape(1, 2 * chunk, jnp.int32)], (), 0,
    )
    columns = [out_grad, packed[:, : 4 * experts]]
    for offset in range(1, groups):
        columns.append(swap_group(packed, offset)[:, experts : 4 * experts])
    extra = (3 * groups + 1) * experts
    columns.append(jnp.zeros((tok_rows, round_up(extra, LANES) - extra), jnp.bfloat16))
    grad_line = along(jnp.concatenate(columns, axis=1))
    tok_next = swap_expert(tok_line, 2)
    grad_next = swap_expert(grad_line, 2)
    tok_own = [(tok_line, swap_expert(tok_line, 1)), (tok_next, swap_expert(tok_next, 1))]
    grad_own = [(grad_line, swap_expert(grad_line, 1)), (grad_next, swap_expert(grad_next, 1))]

    tok_parts = [rows for pair in tok_own for rows in pair]
    grad_parts = [rows for pair in grad_own for rows in pair]
    weights = (w_gate, w_up, w_down)

    at_once = 2 * groups * chunk <= ROWS_AT_ONCE

    def moved(parts, offset):
        out = []
        for part in parts:
            part = swap_group(part, offset)
            out += [part, swap_expert(part, 1)]
        return out

    moved_tok = moved((tok_line, tok_next), 1) if at_once else []
    moved_grad = moved((grad_line, grad_next), 1) if at_once else []
    early = [part[: 2 * SUBLANES, :LANES] for part in moved_tok[1:2]]
    extra = grad_line.shape[1] - width
    wide = jnp.float32
    all_rows = 2 * chunk * groups
    gate, logits = kernel_call(
        functools.partial(gate_kernel, len(grad_parts), experts), (me,), (), grad_parts,
        [shape(all_rows, LANES, wide), shape(experts, all_rows, wide)],
        [
            pltpu.VMEM((2 * chunk, extra), jnp.bfloat16), pltpu.VMEM((all_rows, LANES), wide),
            pltpu.VMEM((experts, all_rows), wide),
        ],
        len(grad_parts) + 2, 2, early,
    )
    pieces = round_up(2 * chunk, LANES) // LANES

    keep0, send0, keep1, send1, *scaled = expert_call(
        me, gate, place, tok_parts, grad_parts, weights, moved_tok[3:4]
    )
    given = [scaled]
    got1, got0 = (swap_expert(send1, 1), swap_expert(send0, 1))
    near, near_score = kernel_call(
        functools.partial(near_kernel, pieces), (), (), (keep1, got1),
        [shape(*keep1.shape), shape(round_up(2 * pieces, 2 * SUBLANES), LANES)],
        [pltpu.VMEM(keep1.shape, keep1.dtype)] * 3, 3, 1, moved_grad[0::2],
    )
    other_scores = []
    for offset in range(1, groups):
        moved_score = swap_group(near_score, offset)
        other_scores += [moved_score, swap_expert(moved_score, 2)]
    across = swap_expert(near, 2)
    count = 4 * pieces * groups
    behind = round_up(count, tok_rows) // tok_rows * LANES
    ready = kernel_call(
        functools.partial(ready_kernel, pieces, len(other_scores)), (), other_scores,
        (keep0, got0, near, across), [shape(tok_rows, width + behind)] * far,
        [pltpu.VMEM(keep0.shape, keep0.dtype)] * 2 + [pltpu.VMEM(near.shape, near.dtype)] * 2
        + [pltpu.VMEM((far, tok_rows, width + behind), near.dtype)], 4 + far, far,
    )
    arrived = [ready[0]] + [swap_expert(ready[k], 4 * k) for k in range(1, far)]
    row_sum = sum(part[:, :width].astype(jnp.float32) for part in arrived)
    score = [
        jnp.concatenate([part[:, at : at + LANES] for at in range(width, width + behind, LANES)])
        for part in arrived
    ]
    score = jnp.stack([part[:count].reshape(groups, 4, pieces * LANES) for part in score], axis=1)
    score = score.reshape(groups, experts, pieces * LANES)
    to_send = ready[1:]

    token_rows = list(tok_parts)
    totals = None
    if not at_once:
        totals = weights_call(group, groups, tok_parts, grad_parts, given, jnp.float32)
        tok_parts, grad_parts, given = ([], [], [])
    for offset in range(1, groups):
        if not at_once:
            (tok_line, tok_next, grad_line, grad_next), totals = lax.optimization_barrier(
                ((tok_line, tok_next, grad_line, grad_next), totals)
            )
            moved_tok = moved((tok_line, tok_next), offset)
            moved_grad = moved((grad_line, grad_next), offset)
        token_rows += moved_tok
        fresh = others_call(me, gate, moved_tok, moved_grad, weights, 2 * chunk * offset)
        terms = weights_call(
            group, groups, tok_parts + moved_tok, grad_parts + moved_grad, given + [fresh],
            jnp.bfloat16 if at_once else jnp.float32, to_send,
        )
        totals = terms if totals is None else [t + u for t, u in zip(totals, terms)]
    final = [t.astype(jnp.bfloat16) for t in totals]

    logit_grad, grad_router = kernel_call(
        functools.partial(router_kernel, len(token_rows)), (me,), (score, place),
        (logits, *token_rows),
        [shape(*logits.shape), shape(experts, width, jnp.float32)],
        [pltpu.VMEM((logits.shape[1], width), jnp.bfloat16), pltpu.VMEM(logits.shape, wide)],
        len(token_rows) + 1,
    )
    row_sum = row_sum + contract(logit_grad[:, :tok_rows], router_weight, 0, 1)
    return (row_sum.astype(jnp.bfloat16), grad_router.T, *final)


def solution(mesh):
    in_specs = (
        P(("dp", "expert"), None),
        P(("dp", "expert"), None),
        P(("dp", "expert"), None),
        P(),
        P("expert", None, None),
        P("expert", None, None),
        P("expert", None, None),
    )
    out_specs = (
        P(("dp", "expert"), None),
        P(),
        P("expert", "dp", None),
        P("expert", "dp", None),
        P("expert", "dp", None),
    )
    return jax.shard_map(
        per_device, mesh=mesh, in_specs=in_specs, out_specs=out_specs, check_vma=False
    )
```

```python
import functools

import jax
import jax.numpy as jnp
from jax import lax
from jax.experimental import pallas as pl
from jax.experimental.pallas import tpu as pltpu
from jax.sharding import PartitionSpec as P

PASSES = 3
LANES = 128
SUBLANES = 8
FF_TILE = 256
ROW_TILE = 32
GRANT = 53 << 20
SMALL_GRANT = 24 << 20
ROWS_AT_ONCE = 1024


def swap_expert(array, offset):
    size = lax.axis_size("expert")
    return lax.ppermute(array, "expert", [(i, i ^ offset) for i in range(size)])


def swap_group(array, offset):
    size = lax.axis_size("dp")
    return lax.ppermute(array, "dp", [(i, i ^ offset) for i in range(size)])


def contract(left, right, left_dim, right_dim):
    return lax.dot_general(
        left, right, (((left_dim,), (right_dim,)), ((), ())), preferred_element_type=jnp.float32
    )


def balancer_forward_pass(logits):
    densities = [jnp.exp(logits)]
    quotients, column_totals, row_totals = ([], [], [])
    for _ in range(PASSES):
        column_sum = jnp.sum(densities[-1], axis=1, keepdims=True)
        quotient = densities[-1] / column_sum
        row_sum = jnp.sum(quotient, axis=0, keepdims=True)
        densities.append(quotient / row_sum)
        quotients.append(quotient)
        column_totals.append(column_sum)
        row_totals.append(row_sum)
    return (densities, quotients, column_totals, row_totals)


def balancer_adjoint_pass(density_gradient, densities, quotients, column_totals, row_totals):
    for repeat in reversed(range(PASSES)):
        inner = jnp.sum(density_gradient * densities[repeat + 1], axis=0, keepdims=True)
        quotient_grad = (density_gradient - inner) / row_totals[repeat]
        shared = jnp.sum(quotient_grad * quotients[repeat], axis=1, keepdims=True)
        density_gradient = (quotient_grad - shared) / column_totals[repeat]
    return density_gradient * densities[0]


def round_up(value, unit):
    return -(-value // unit) * unit


def pack_kernel(slots, me_ref, ids_ref, tok_ref, router_ref, out, place_ref):
    experts = router_ref.shape[0]
    rows = tok_ref.shape[0]
    at = lax.broadcasted_iota(jnp.int32, place_ref.shape, 1)
    place = jnp.zeros(place_ref.shape, jnp.int32)
    for index, offset in enumerate(slots):
        first = index * rows
        here = (at >= first) & (at < first + rows)
        place = jnp.where(here, (me_ref[0] ^ offset) * rows + at - first, place)
    place_ref[...] = place
    rest = contract(tok_ref[...], router_ref[...], 1, 1)
    lane = lax.broadcasted_iota(jnp.int32, out.shape, 1)
    packed = jnp.zeros(out.shape, jnp.float32)
    for pick in range(ids_ref.shape[1]):
        packed += jnp.where(lane == ids_ref[:, pick : pick + 1], 1.0, 0.0)
    row = lax.broadcasted_iota(jnp.int32, (experts, out.shape[1]), 0)
    column = lax.broadcasted_iota(jnp.int32, (experts, out.shape[1]), 1)
    for term in range(1, 4):
        part = rest.astype(jnp.bfloat16)
        rest = rest - part.astype(jnp.float32)
        place = jnp.where(column == row + term * experts, 1.0, 0.0).astype(jnp.bfloat16)
        packed += contract(part, place, 1, 0)
    out[...] = packed.astype(jnp.bfloat16)


def gate_kernel(parts, experts, me_ref, *refs):
    grad, gate_out, logits_out = (refs[:parts], *refs[parts : parts + 2])
    packed, gate_ref, logits_ref, sems = refs[parts + 2 :]
    copies = Copies(sems)
    extra = packed.shape[1]
    wait(copies.stack(grad, packed, pl.ds(grad[0].shape[1] - extra, extra)))
    turned = jnp.transpose(packed[...].astype(jnp.float32))
    columns = []
    for group in range(logits_ref.shape[1] // packed.shape[0]):
        at = (3 * group + 1) * experts
        terms = [turned[at + i * experts : at + (i + 1) * experts] for i in range(3)]
        columns.append(terms[0] + terms[1] + terms[2])
    logits = jnp.concatenate(columns, axis=1)
    logits_ref[...] = logits
    results = [copies.start(logits_ref, logits_out)]
    gates = experts * balancer_forward_pass(logits)[0][-1]
    row = lax.broadcasted_iota(jnp.int32, gates.shape, 0)
    mine = jnp.sum(jnp.where(row == me_ref[0], gates, 0.0), axis=0, keepdims=True)
    gate_ref[...] = jnp.transpose(jnp.broadcast_to(mine, (LANES, gates.shape[1])))
    wait([*results, copies.start(gate_ref, gate_out)])


def kernel_call(
    kernel, scalars, small, large, out_shape, scratch, copies, large_outs=0, after=(), macs=10**6, grant=GRANT
):
    whole = pl.BlockSpec(memory_space=pltpu.VMEM)
    outside = pl.BlockSpec(memory_space=pltpu.HBM)
    inputs = len(scalars) + len(small) + len(large)

    def body(*refs):
        kernel(*refs[:inputs], *refs[inputs + len(after) :])

    return pl.pallas_call(
        body,
        in_specs=[pl.BlockSpec(memory_space=pltpu.SMEM)] * len(scalars)
        + [whole] * len(small)
        + [outside] * (len(large) + len(after)),
        out_specs=[outside] * large_outs + [whole] * (len(out_shape) - large_outs),
        out_shape=out_shape,
        scratch_shapes=[*scratch] + [pltpu.SemaphoreType.DMA((copies,))] * (copies > 0),
        compiler_params=pltpu.CompilerParams(vmem_limit_bytes=grant),
        cost_estimate=pl.CostEstimate(
            flops=2 * macs, bytes_accessed=macs // 200, transcendentals=macs // 10000
        ),
    )(*scalars, *small, *large, *after)


def shape(rows, columns, dtype=jnp.bfloat16):
    return jax.ShapeDtypeStruct((rows, columns), dtype)


def tiles(extent, tile):
    tile = tile if extent % tile == 0 else extent
    return [slice(at, at + tile) for at in range(0, extent, tile)]


class Copies:
    def __init__(self, sems):
        self.sems, self.count = (sems, 0)

    def start(self, source, target):
        copy = pltpu.make_async_copy(source, target, self.sems.at[self.count])
        self.count += 1
        copy.start()
        return copy

    def stack(self, parts, target, columns=slice(None)):
        started, at = ([], 0)
        for part in parts:
            rows = part.shape[0]
            started.append(self.start(part.at[:, columns], target.at[pl.ds(at, rows), :]))
            at += rows
        return started


def wait(copies):
    for copy in copies:
        copy.wait()


def loop(count, body, rolled=True):
    if not rolled:
        for index in range(count):
            body(index)
        return

    def step(index, carry):
        body(index)
        return carry

    lax.fori_loop(0, count, step, 0)


class Tiles:
    def __init__(self, copies, source, target, dim, tile):
        extent = target.shape[dim]
        self.tile = tile if extent % tile == 0 else extent
        self.count = extent // self.tile
        self.source, self.target, self.dim = (source, target, dim)
        self.sems, self.base = (copies.sems, copies.count)
        copies.count += self.count
        for index in range(self.count):
            self.copy(index).start()

    def here(self, index):
        start = index * self.tile
        if not isinstance(index, int):
            start = pl.multiple_of(start, self.tile)
        cut = pl.ds(start, self.tile)
        return (cut, slice(None)) if self.dim == 0 else (slice(None), cut)

    def copy(self, index):
        here = self.here(index)
        return pltpu.make_async_copy(
            self.source.at[here], self.target.at[here], self.sems.at[self.base + index]
        )


def mask_of(me_ref, picked):
    row = lax.broadcasted_iota(jnp.int32, (LANES, LANES), 0)
    mine = jnp.where(row == me_ref[0], 1.0, 0.0).astype(jnp.bfloat16)
    return contract(picked, mine, 1, 0)


def spread(lanes, width):
    return jnp.concatenate([lanes] * (width // LANES), axis=1)


def rounded(array):
    return array.astype(jnp.bfloat16).astype(jnp.float32)


def inner_terms(gate_pre, up_pre, hidden_grad):
    sigmoid_gate = jax.nn.sigmoid(gate_pre)
    activation = gate_pre * sigmoid_gate
    hidden = activation * up_pre
    gate_grad = hidden_grad * up_pre * sigmoid_gate * (1.0 + gate_pre * (1.0 - sigmoid_gate))
    up_grad = hidden_grad * activation
    half = jnp.bfloat16
    return hidden, gate_grad.astype(half), up_grad.astype(half)


def project_start(copies, tok, rows_in, sources, weights):
    width = rows_in.shape[1]
    tile = 2 * FF_TILE if width % (2 * FF_TILE) == 0 else width
    blocks = []
    for start in range(0, width, tile):
        cut = pl.ds(start, tile)
        here, at = ([], 0)
        for part in tok:
            rows = pl.ds(at, part.shape[0])
            here.append(copies.start(part.at[:, cut], rows_in.at[rows, cut]))
            at += part.shape[0]
        for source, weight in zip(sources, weights):
            here.append(copies.start(source.at[0, cut, :], weight.at[cut, :]))
        blocks.append((slice(start, start + tile), here))
    return blocks


def project(blocks, rows_in, targets, weights):
    for cut, here in blocks:
        wait(here)
        for target, weight in zip(targets, weights):
            value = contract(rows_in[:, cut], weight[cut, :], 1, 0)
            if cut.start == 0:
                target[...] = value
            else:
                target[...] += value


def backward(grad_here, rows_grad, hidden_grad, weight):
    wait(grad_here)

    def body(index):
        weight.copy(index).wait()
        cut = weight.here(index)[0]
        rows = rows_grad[:, : weight.target.shape[1]]
        hidden_grad[:, cut] = contract(rows, weight.target[cut, :], 1, 1)

    loop(weight.count, body)


def row_cut(index):
    start = index * ROW_TILE
    return pl.ds(start if isinstance(index, int) else pl.multiple_of(start, ROW_TILE), ROW_TILE)


def expert_kernel(parts, me_ref, place_ref, gate_all, *refs):
    tok, grad, sources = (refs[:parts], refs[parts : 2 * parts], refs[2 * parts : 2 * parts + 3])
    refs = refs[2 * parts + 3 :]
    sum_outs, scaled_outs = (refs[:parts], refs[parts : parts + 3])
    rows_in, rows_grad, gate_pre, up_pre, hidden_grad, *refs = refs[parts + 3 :]
    wg, wu, wd, gate_grad, up_grad, hs, gs, us, sums, column, gate, sems = refs
    copies = Copies(sems)
    width = wg.shape[0]
    rows = gate_pre.shape[0]
    ff_width = wd.shape[0]
    blocks = project_start(copies, tok, rows_in, sources, (wg, wu))
    grad_here = copies.stack(grad, rows_grad)
    grad_here.append(copies.start(gate_all.at[pl.ds(0, rows), :], gate))
    down = Tiles(copies, sources[2].at[0], wd, 0, FF_TILE)
    project(blocks, rows_in, (gate_pre, up_pre), (wg, wu))
    backward(grad_here, rows_grad, hidden_grad, down)
    column[...] = mask_of(me_ref, rows_grad[:, width : width + LANES])
    gate[...] *= column[...]

    def terms(index):
        cut = row_cut(index)
        values = inner_terms(gate_pre[cut, :], up_pre[cut, :], hidden_grad[cut, :])
        gate_grad[cut, :] = values[1]
        up_grad[cut, :] = values[2]
        sent = spread(rounded(gate[cut, :]), ff_width)
        for value, target in zip(values, (hs, gs, us)):
            target[cut, :] = (sent * value).astype(jnp.bfloat16)
        product = hidden_grad[cut, :] * values[0]
        column[cut, :] *= sum(product[:, at] for at in tiles(ff_width, LANES))

    loop(rows // ROW_TILE, terms)
    results = [copies.start(source, out) for source, out in zip((hs, gs, us), scaled_outs)]
    ones = jnp.ones((SUBLANES, LANES), jnp.bfloat16)
    high = column[...].astype(jnp.bfloat16)
    low = (column[...] - high.astype(jnp.float32)).astype(jnp.bfloat16)
    score = (contract(ones, high, 1, 1) + contract(ones, low, 1, 1)).astype(jnp.bfloat16)
    score = contract(score, order_matrix(place_ref, round_up(rows, LANES)), 1, 1)
    block = placed([score[:1, at] for at in tiles(score.shape[1], LANES)], sums.shape[0])
    sums[:, width:] = block.astype(sums.dtype)
    chunk = sum_outs[0].shape[0]
    for at in range(0, rows, chunk):
        sums[at : at + chunk, width:] = sums[:chunk, width:]

    tile = 2 * FF_TILE if width % (2 * FF_TILE) == 0 else width

    def products(index):
        cut = pl.ds(pl.multiple_of(index * tile, tile), tile)
        part = contract(gate_grad[...], wg[cut, :], 1, 1)
        part += contract(up_grad[...], wu[cut, :], 1, 1)
        sums[:, cut] = (spread(gate[...], tile) * part).astype(jnp.bfloat16)

    loop(width // tile, products)
    at = 0
    for out in sum_outs:
        here = sums.at[pl.ds(at, out.shape[0]), pl.ds(0, out.shape[1])]
        results.append(copies.start(here, out))
        at += out.shape[0]
    wait(results)


def expert_call(me, gate, place, tok, grad, weights, after):
    rows = sum(part.shape[0] for part in tok)
    width, ff_width = weights[0].shape[1:]
    half = jnp.bfloat16
    narrow = pltpu.VMEM((rows, ff_width), half)
    return kernel_call(
        functools.partial(expert_kernel, len(tok)), (me,), (place,),
        (gate, *tok, *grad, *weights),
        [shape(part.shape[0], width + LANES * (at > 1)) for at, part in enumerate(tok)]
        + [shape(rows, ff_width)] * 3,
        [pltpu.VMEM((rows, width), half), pltpu.VMEM((rows, grad[0].shape[1]), half)]
        + [pltpu.VMEM((rows, ff_width), jnp.float32)] * 3
        + [pltpu.VMEM((width, ff_width), half)] * 2 + [pltpu.VMEM((ff_width, width), half)]
        + [narrow] * 5 + [pltpu.VMEM((rows, width + LANES), half)]
        + [pltpu.VMEM((rows, LANES), jnp.float32)] * 2,
        2 * len(tok) + (len(tok) + 2) * len(tiles(width, 2 * FF_TILE))
        + len(tiles(ff_width, FF_TILE)) + 4,
        len(tok) + 3, after, 5 * rows * width * ff_width,
    )


def placed(rows, height):
    index = lax.broadcasted_iota(jnp.int32, (height, LANES), 0)
    block = jnp.zeros((height, LANES), jnp.float32)
    for at, row in enumerate(rows):
        block = jnp.where(index == at, jnp.broadcast_to(row, block.shape), block)
    return block


def first_rows(block, count):
    block = block.astype(jnp.float32)
    return [block[at : at + 1, :] for at in range(count)]


def order_matrix(place_ref, height):
    count = place_ref.shape[1]
    row = lax.broadcasted_iota(jnp.int32, (height, count), 0)
    return jnp.where(row == place_ref[...], 1.0, 0.0).astype(jnp.bfloat16)


def near_kernel(pieces, keep, got, out, score_out, keep_here, got_here, total, sems):
    copies = Copies(sems)
    wait([copies.start(keep, keep_here), copies.start(got, got_here)])
    width = total.shape[1] - LANES
    total[:, :width] = (
        keep_here[:, :width].astype(jnp.float32) + got_here[:, :width].astype(jnp.float32)
    ).astype(total.dtype)
    scores = first_rows(keep_here[: 2 * SUBLANES, width:], pieces)
    scores += first_rows(got_here[: 2 * SUBLANES, width:], pieces)
    block = placed(scores, total.shape[0]).astype(total.dtype)
    total[:, width:] = block
    score_out[...] = block[: score_out.shape[0]]
    wait([copies.start(total, out)])


def ready_kernel(pieces, others, *refs):
    other_scores, (keep, got, near, across, *refs) = (refs[:others], refs[others:])
    outs, refs = (refs[: len(refs) - 6], refs[len(refs) - 6 :])
    keep_here, got_here, near_here, across_here, made, sems = refs
    copies = Copies(sems)
    wait(
        [
            copies.start(keep, keep_here), copies.start(got, got_here),
            copies.start(near, near_here), copies.start(across, across_here),
        ]
    )
    far = made.shape[0]
    rows = made.shape[1]
    width = keep_here.shape[1]
    scores = first_rows(near_here[: 4 * SUBLANES, width:], 2 * pieces)
    scores += first_rows(across_here[: 4 * SUBLANES, width:], 2 * pieces)
    for other in other_scores:
        scores += first_rows(other[...], 2 * pieces)
    blocks = [placed(scores[at : at + rows], rows) for at in range(0, len(scores), rows)]
    block = jnp.concatenate(blocks, axis=1)
    total = keep_here[...].astype(jnp.float32) + got_here[...].astype(jnp.float32)
    total += across_here[:, :width].astype(jnp.float32)
    results = []
    for k in range(far):
        made[k, :, :width] = total[k * rows : (k + 1) * rows, :].astype(made.dtype)
        made[k, :, width:] = block.astype(made.dtype)
        results.append(copies.start(made.at[k], outs[k]))
    wait(results)


def others_kernel(parts, start, me_ref, gate_all, *refs):
    tok, grad, sources = (refs[:parts], refs[parts : 2 * parts], refs[2 * parts : 2 * parts + 3])
    outs, refs = (refs[2 * parts + 3 : 2 * parts + 6], refs[2 * parts + 6 :])
    rows_in, rows_grad, gate_pre, up_pre, hidden_grad, wg, wu, wd, hs, gs, us, gate, sems = refs
    copies = Copies(sems)
    rows, width = rows_in.shape
    ff_width = wd.shape[0]
    blocks = project_start(copies, tok, rows_in, sources, (wg, wu))
    grad_here = copies.stack(grad, rows_grad)
    grad_here.append(copies.start(gate_all.at[pl.ds(start, rows), :], gate))
    down = Tiles(copies, sources[2].at[0], wd, 0, FF_TILE)
    project(blocks, rows_in, (gate_pre, up_pre), (wg, wu))
    backward(grad_here, rows_grad, hidden_grad, down)
    gate[...] *= mask_of(me_ref, rows_grad[:, width : width + LANES])

    def terms(index):
        cut = row_cut(index)
        values = inner_terms(gate_pre[cut, :], up_pre[cut, :], hidden_grad[cut, :])
        sent = spread(rounded(gate[cut, :]), ff_width)
        for value, target in zip(values, (hs, gs, us)):
            target[cut, :] = (sent * value).astype(jnp.bfloat16)

    loop(rows // ROW_TILE, terms)
    wait([copies.start(source, out) for source, out in zip((hs, gs, us), outs)])


def others_call(me, gate, tok, grad, weights, start, after=()):
    rows = sum(part.shape[0] for part in tok)
    width, ff_width = weights[0].shape[1:]
    half = jnp.bfloat16
    return kernel_call(
        functools.partial(others_kernel, len(tok), start), (me,), (),
        (gate, *tok, *grad, *weights),
        [shape(rows, ff_width)] * 3,
        [pltpu.VMEM((rows, width), half), pltpu.VMEM((rows, grad[0].shape[1]), half)]
        + [pltpu.VMEM((rows, ff_width), jnp.float32)] * 3
        + [pltpu.VMEM((width, ff_width), half)] * 2 + [pltpu.VMEM((ff_width, width), half)]
        + [pltpu.VMEM((rows, ff_width), half)] * 3 + [pltpu.VMEM((rows, LANES), jnp.float32)],
        len(tok) + (len(tok) + 2) * len(tiles(width, 2 * FF_TILE))
        + len(tiles(ff_width, FF_TILE)) + 4,
        3, after, 3 * rows * width * ff_width,
    )


def weights_kernel(parts, given, steps, group_ref, *refs):
    tok, grad, given_refs = (refs[:parts], refs[parts : 2 * parts], refs[2 * parts :][: 3 * given])
    outs, refs = (refs[2 * parts + 3 * given :][:3], refs[2 * parts + 3 * given + 3 :])
    hs, gs, us, tok_half, grad_all, hidden_half, *tile_out, sems = refs
    copies = Copies(sems)
    width = grad_all.shape[1]
    half = outs[0].shape[1]
    half_ff = outs[2].shape[1]
    blocks = [given_refs[kind * given : (kind + 1) * given] for kind in range(3)]
    mine = pl.ds(pl.multiple_of(group_ref[0] * half, LANES), half)
    gate_here = copies.stack(tok, tok_half, mine) + copies.stack(blocks[1], gs)
    up_here = copies.stack(blocks[2], us)
    down_here = copies.stack(blocks[0], hs) + copies.stack(grad, grad_all, pl.ds(0, width))
    base = copies.count

    def result(which, step):
        tile = tile_out[which].shape[1 if which < 2 else 2]
        at = step * tile if isinstance(step, int) else pl.multiple_of(step * tile, tile)
        cut = pl.ds(at, tile)
        target = outs[which].at[0, cut, :] if which < 2 else outs[which].at[0, :, cut]
        return cut, pltpu.make_async_copy(
            tile_out[which].at[step], target, sems.at[base + which * steps + step]
        )

    def form(which, left, right):
        def body(step):
            cut, copy = result(which, step)
            sides = (left[:, cut], right[...]) if which < 2 else (left[...], right[:, cut])
            tile_out[which][step] = contract(*sides, 0, 0).astype(tile_out[which].dtype)
            copy.start()

        loop(steps, body, rolled=False)

    wait(gate_here)
    form(0, tok_half, gs)
    wait(up_here)
    form(1, tok_half, us)
    wait(down_here)
    if half_ff % LANES == 0:
        place = pl.ds(pl.multiple_of(group_ref[0] * half_ff, LANES), half_ff)
        hidden_half[...] = hs[:, place]
    else:
        for index in range(hs.shape[1] // half_ff):

            @pl.when(group_ref[0] == index)
            def _():
                hidden_half[...] = hs[:, index * half_ff : (index + 1) * half_ff]

    form(2, hidden_half, grad_all)
    wait([result(which, step)[1] for which in range(3) for step in range(steps)])


def weights_call(group, groups, tok, grad, given, dtype, after=()):
    width, ff_width = (tok[0].shape[1], given[0][0].shape[1])
    half, half_ff = (width // groups, ff_width // groups)
    rows = sum(part.shape[0] for part in tok)
    steps = max(s for s in (4, 2, 1) if half % (s * LANES) == 0)
    low = jnp.bfloat16
    scratch = [pltpu.VMEM((rows, ff_width), low)] * 3
    scratch += [
        pltpu.VMEM((rows, half), low),
        pltpu.VMEM((rows, width), low),
        pltpu.VMEM((rows, half_ff), low),
        pltpu.VMEM((steps, half // steps, ff_width), dtype),
        pltpu.VMEM((steps, half // steps, ff_width), dtype),
        pltpu.VMEM((steps, half_ff, width // steps), dtype),
    ]
    return kernel_call(
        functools.partial(weights_kernel, len(tok), len(given), steps), (group,), (),
        (*tok, *grad, *(block[kind] for kind in range(3) for block in given)),
        [
            jax.ShapeDtypeStruct((1, half, ff_width), dtype),
            jax.ShapeDtypeStruct((1, half, ff_width), dtype),
            jax.ShapeDtypeStruct((1, half_ff, width), dtype),
        ],
        scratch, 2 * len(tok) + 3 * len(given) + 3 * steps, 3, after, 3 * rows * half * ff_width,
    )


def router_kernel(parts, me_ref, *refs):
    score_ref, place_ref, logits_all, *tok = refs[: 3 + parts]
    grad_ref, router_ref, rows, logits_ref, sems = refs[3 + parts :]
    copies = Copies(sems)
    logits_here = copies.start(logits_all, logits_ref)
    rows_here = copies.stack(tok, rows)
    logits_here.wait()
    logits = logits_ref[...]
    experts = logits.shape[0]
    row = lax.broadcasted_iota(jnp.int32, (experts, experts), 0)
    column = lax.broadcasted_iota(jnp.int32, (experts, experts), 1)
    unswap = jnp.where((row ^ me_ref[0]) == column, 1.0, 0.0).astype(jnp.bfloat16)
    group = score_ref.shape[2]
    order = order_matrix(place_ref, group)
    score = jnp.concatenate(
        [contract(score_ref[at], order, 1, 0) for at in range(score_ref.shape[0])], axis=1
    )
    score = contract(unswap, score.astype(jnp.bfloat16), 1, 0)
    state = balancer_forward_pass(logits)
    grad = balancer_adjoint_pass(experts * score, *state).astype(jnp.bfloat16)
    grad_ref[...] = grad
    wait(rows_here)
    router_ref[...] = contract(grad, rows[...], 1, 0)


def per_device(tokens, out_grad, expert_ids, router_weight, w_gate, w_up, w_down):
    tok_rows, width = tokens.shape
    experts = router_weight.shape[1]
    groups = lax.axis_size("dp")
    far = lax.axis_size("expert") // 4
    chunk = 2 * far * tok_rows
    me = lax.axis_index("expert").astype(jnp.int32)[None]
    group = lax.axis_index("dp").astype(jnp.int32)[None]

    def along(array):
        return jnp.concatenate([array] + [swap_expert(array, 4 * k) for k in range(1, far)], axis=0)

    tok_line = along(tokens)
    slots = [4 * j + 2 * i + k for i in range(2) for k in range(2) for j in range(far)]
    packed, place = kernel_call(
        functools.partial(pack_kernel, slots), (me,), (expert_ids, tokens, router_weight.T), (),
        [shape(tok_rows, round_up(4 * experts, LANES)), shape(1, 2 * chunk, jnp.int32)], (), 0,
    )
    columns = [out_grad, packed[:, : 4 * experts]]
    for offset in range(1, groups):
        columns.append(swap_group(packed, offset)[:, experts : 4 * experts])
    extra = (3 * groups + 1) * experts
    columns.append(jnp.zeros((tok_rows, round_up(extra, LANES) - extra), jnp.bfloat16))
    grad_line = along(jnp.concatenate(columns, axis=1))
    tok_next = swap_expert(tok_line, 2)
    grad_next = swap_expert(grad_line, 2)
    tok_own = [(tok_line, swap_expert(tok_line, 1)), (tok_next, swap_expert(tok_next, 1))]
    grad_own = [(grad_line, swap_expert(grad_line, 1)), (grad_next, swap_expert(grad_next, 1))]

    tok_parts = [rows for pair in tok_own for rows in pair]
    grad_parts = [rows for pair in grad_own for rows in pair]
    weights = (w_gate, w_up, w_down)

    at_once = 2 * groups * chunk <= ROWS_AT_ONCE

    def moved(parts, offset):
        out = []
        for part in parts:
            part = swap_group(part, offset)
            out += [part, swap_expert(part, 1)]
        return out

    moved_tok = moved((tok_line, tok_next), 1) if at_once else []
    moved_grad = moved((grad_line, grad_next), 1) if at_once else []
    early = [part[: 2 * SUBLANES, :LANES] for part in moved_tok[1:2]]
    extra = grad_line.shape[1] - width
    wide = jnp.float32
    all_rows = 2 * chunk * groups
    gate, logits = kernel_call(
        functools.partial(gate_kernel, len(grad_parts), experts), (me,), (), grad_parts,
        [shape(all_rows, LANES, wide), shape(experts, all_rows, wide)],
        [
            pltpu.VMEM((2 * chunk, extra), jnp.bfloat16), pltpu.VMEM((all_rows, LANES), wide),
            pltpu.VMEM((experts, all_rows), wide),
        ],
        len(grad_parts) + 2, 2, early,
    )
    pieces = round_up(2 * chunk, LANES) // LANES

    keep0, send0, keep1, send1, *scaled = expert_call(
        me, gate, place, tok_parts, grad_parts, weights, moved_tok[3:4]
    )
    given = [scaled]
    got1, got0 = (swap_expert(send1, 1), swap_expert(send0, 1))
    near, near_score = kernel_call(
        functools.partial(near_kernel, pieces), (), (), (keep1, got1),
        [shape(*keep1.shape), shape(round_up(2 * pieces, 2 * SUBLANES), LANES)],
        [pltpu.VMEM(keep1.shape, keep1.dtype)] * 3, 3, 1, moved_grad[0::2], grant=SMALL_GRANT,
    )
    other_scores = []
    for offset in range(1, groups):
        moved_score = swap_group(near_score, offset)
        other_scores += [moved_score, swap_expert(moved_score, 2)]
    across = swap_expert(near, 2)
    count = 4 * pieces * groups
    behind = round_up(count, tok_rows) // tok_rows * LANES
    ready = kernel_call(
        functools.partial(ready_kernel, pieces, len(other_scores)), (), other_scores,
        (keep0, got0, near, across), [shape(tok_rows, width + behind)] * far,
        [pltpu.VMEM(keep0.shape, keep0.dtype)] * 2 + [pltpu.VMEM(near.shape, near.dtype)] * 2
        + [pltpu.VMEM((far, tok_rows, width + behind), near.dtype)], 4 + far, far, grant=SMALL_GRANT,
    )
    arrived = [ready[0]] + [swap_expert(ready[k], 4 * k) for k in range(1, far)]
    row_sum = sum(part[:, :width].astype(jnp.float32) for part in arrived)
    score = [
        jnp.concatenate([part[:, at : at + LANES] for at in range(width, width + behind, LANES)])
        for part in arrived
    ]
    score = jnp.stack([part[:count].reshape(groups, 4, pieces * LANES) for part in score], axis=1)
    score = score.reshape(groups, experts, pieces * LANES)
    to_send = ready[1:]

    token_rows = list(tok_parts)
    totals = None
    if not at_once:
        totals = weights_call(group, groups, tok_parts, grad_parts, given, jnp.float32)
        tok_parts, grad_parts, given = ([], [], [])
    for offset in range(1, groups):
        if not at_once:
            (tok_line, tok_next, grad_line, grad_next), totals = lax.optimization_barrier(
                ((tok_line, tok_next, grad_line, grad_next), totals)
            )
            moved_tok = moved((tok_line, tok_next), offset)
            moved_grad = moved((grad_line, grad_next), offset)
        token_rows += moved_tok
        fresh = others_call(me, gate, moved_tok, moved_grad, weights, 2 * chunk * offset)
        terms = weights_call(
            group, groups, tok_parts + moved_tok, grad_parts + moved_grad, given + [fresh],
            jnp.bfloat16 if at_once else jnp.float32, to_send,
        )
        totals = terms if totals is None else [t + u for t, u in zip(totals, terms)]
    final = [t.astype(jnp.bfloat16) for t in totals]

    logit_grad, grad_router = kernel_call(
        functools.partial(router_kernel, len(token_rows)), (me,), (score, place),
        (logits, *token_rows),
        [shape(*logits.shape), shape(experts, width, jnp.float32)],
        [pltpu.VMEM((logits.shape[1], width), jnp.bfloat16), pltpu.VMEM(logits.shape, wide)],
        len(token_rows) + 1,
    )
    row_sum = row_sum + contract(logit_grad[:, :tok_rows], router_weight, 0, 1)
    return (row_sum.astype(jnp.bfloat16), grad_router.T, *final)


def solution(mesh):
    in_specs = (
        P(("dp", "expert"), None),
        P(("dp", "expert"), None),
        P(("dp", "expert"), None),
        P(),
        P("expert", None, None),
        P("expert", None, None),
        P("expert", None, None),
    )
    out_specs = (
        P(("dp", "expert"), None),
        P(),
        P("expert", "dp", None),
        P("expert", "dp", None),
        P("expert", "dp", None),
    )
    return jax.shard_map(
        per_device, mesh=mesh, in_specs=in_specs, out_specs=out_specs, check_vma=False
    )
```

```python
import functools

import jax
import jax.numpy as jnp
from jax import lax
from jax.experimental import pallas as pl
from jax.experimental.pallas import tpu as pltpu
from jax.sharding import PartitionSpec as P

PASSES = 3
LANES = 128
SUBLANES = 8
FF_TILE = 256
ROW_TILE = 32
GRANT = 53 << 20
SMALL_GRANT = 24 << 20
OTHERS_GRANT = 54 << 20
ROWS_AT_ONCE = 1024


def swap_expert(array, offset):
    size = lax.axis_size("expert")
    return lax.ppermute(array, "expert", [(i, i ^ offset) for i in range(size)])


def swap_group(array, offset):
    size = lax.axis_size("dp")
    return lax.ppermute(array, "dp", [(i, i ^ offset) for i in range(size)])


def contract(left, right, left_dim, right_dim):
    return lax.dot_general(
        left, right, (((left_dim,), (right_dim,)), ((), ())), preferred_element_type=jnp.float32
    )


def balancer_forward_pass(logits):
    densities = [jnp.exp(logits)]
    quotients, column_totals, row_totals = ([], [], [])
    for _ in range(PASSES):
        column_sum = jnp.sum(densities[-1], axis=1, keepdims=True)
        quotient = densities[-1] / column_sum
        row_sum = jnp.sum(quotient, axis=0, keepdims=True)
        densities.append(quotient / row_sum)
        quotients.append(quotient)
        column_totals.append(column_sum)
        row_totals.append(row_sum)
    return (densities, quotients, column_totals, row_totals)


def balancer_adjoint_pass(density_gradient, densities, quotients, column_totals, row_totals):
    for repeat in reversed(range(PASSES)):
        inner = jnp.sum(density_gradient * densities[repeat + 1], axis=0, keepdims=True)
        quotient_grad = (density_gradient - inner) / row_totals[repeat]
        shared = jnp.sum(quotient_grad * quotients[repeat], axis=1, keepdims=True)
        density_gradient = (quotient_grad - shared) / column_totals[repeat]
    return density_gradient * densities[0]


def round_up(value, unit):
    return -(-value // unit) * unit


def pack_kernel(slots, me_ref, ids_ref, tok_ref, router_ref, out, place_ref):
    experts = router_ref.shape[0]
    rows = tok_ref.shape[0]
    at = lax.broadcasted_iota(jnp.int32, place_ref.shape, 1)
    place = jnp.zeros(place_ref.shape, jnp.int32)
    for index, offset in enumerate(slots):
        first = index * rows
        here = (at >= first) & (at < first + rows)
        place = jnp.where(here, (me_ref[0] ^ offset) * rows + at - first, place)
    place_ref[...] = place
    rest = contract(tok_ref[...], router_ref[...], 1, 1)
    lane = lax.broadcasted_iota(jnp.int32, out.shape, 1)
    packed = jnp.zeros(out.shape, jnp.float32)
    for pick in range(ids_ref.shape[1]):
        packed += jnp.where(lane == ids_ref[:, pick : pick + 1], 1.0, 0.0)
    row = lax.broadcasted_iota(jnp.int32, (experts, out.shape[1]), 0)
    column = lax.broadcasted_iota(jnp.int32, (experts, out.shape[1]), 1)
    for term in range(1, 4):
        part = rest.astype(jnp.bfloat16)
        rest = rest - part.astype(jnp.float32)
        place = jnp.where(column == row + term * experts, 1.0, 0.0).astype(jnp.bfloat16)
        packed += contract(part, place, 1, 0)
    out[...] = packed.astype(jnp.bfloat16)


def gate_kernel(parts, experts, me_ref, *refs):
    grad, gate_out, logits_out = (refs[:parts], *refs[parts : parts + 2])
    packed, gate_ref, logits_ref, sems = refs[parts + 2 :]
    copies = Copies(sems)
    extra = packed.shape[1]
    wait(copies.stack(grad, packed, pl.ds(grad[0].shape[1] - extra, extra)))
    turned = jnp.transpose(packed[...].astype(jnp.float32))
    columns = []
    for group in range(logits_ref.shape[1] // packed.shape[0]):
        at = (3 * group + 1) * experts
        terms = [turned[at + i * experts : at + (i + 1) * experts] for i in range(3)]
        columns.append(terms[0] + terms[1] + terms[2])
    logits = jnp.concatenate(columns, axis=1)
    logits_ref[...] = logits
    results = [copies.start(logits_ref, logits_out)]
    gates = experts * balancer_forward_pass(logits)[0][-1]
    row = lax.broadcasted_iota(jnp.int32, gates.shape, 0)
    mine = jnp.sum(jnp.where(row == me_ref[0], gates, 0.0), axis=0, keepdims=True)
    gate_ref[...] = jnp.transpose(jnp.broadcast_to(mine, (LANES, gates.shape[1])))
    wait([*results, copies.start(gate_ref, gate_out)])


def kernel_call(
    kernel, scalars, small, large, out_shape, scratch, copies, large_outs=0, after=(), macs=10**6, grant=GRANT
):
    whole = pl.BlockSpec(memory_space=pltpu.VMEM)
    outside = pl.BlockSpec(memory_space=pltpu.HBM)
    inputs = len(scalars) + len(small) + len(large)

    def body(*refs):
        kernel(*refs[:inputs], *refs[inputs + len(after) :])

    return pl.pallas_call(
        body,
        in_specs=[pl.BlockSpec(memory_space=pltpu.SMEM)] * len(scalars)
        + [whole] * len(small)
        + [outside] * (len(large) + len(after)),
        out_specs=[outside] * large_outs + [whole] * (len(out_shape) - large_outs),
        out_shape=out_shape,
        scratch_shapes=[*scratch] + [pltpu.SemaphoreType.DMA((copies,))] * (copies > 0),
        compiler_params=pltpu.CompilerParams(vmem_limit_bytes=grant),
        cost_estimate=pl.CostEstimate(
            flops=2 * macs, bytes_accessed=macs // 200, transcendentals=macs // 10000
        ),
    )(*scalars, *small, *large, *after)


def shape(rows, columns, dtype=jnp.bfloat16):
    return jax.ShapeDtypeStruct((rows, columns), dtype)


def tiles(extent, tile):
    tile = tile if extent % tile == 0 else extent
    return [slice(at, at + tile) for at in range(0, extent, tile)]


class Copies:
    def __init__(self, sems):
        self.sems, self.count = (sems, 0)

    def start(self, source, target):
        copy = pltpu.make_async_copy(source, target, self.sems.at[self.count])
        self.count += 1
        copy.start()
        return copy

    def stack(self, parts, target, columns=slice(None)):
        started, at = ([], 0)
        for part in parts:
            rows = part.shape[0]
            started.append(self.start(part.at[:, columns], target.at[pl.ds(at, rows), :]))
            at += rows
        return started


def wait(copies):
    for copy in copies:
        copy.wait()


def loop(count, body, rolled=True):
    if not rolled:
        for index in range(count):
            body(index)
        return

    def step(index, carry):
        body(index)
        return carry

    lax.fori_loop(0, count, step, 0)


class Tiles:
    def __init__(self, copies, source, target, dim, tile):
        extent = target.shape[dim]
        self.tile = tile if extent % tile == 0 else extent
        self.count = extent // self.tile
        self.source, self.target, self.dim = (source, target, dim)
        self.sems, self.base = (copies.sems, copies.count)
        copies.count += self.count
        for index in range(self.count):
            self.copy(index).start()

    def here(self, index):
        start = index * self.tile
        if not isinstance(index, int):
            start = pl.multiple_of(start, self.tile)
        cut = pl.ds(start, self.tile)
        return (cut, slice(None)) if self.dim == 0 else (slice(None), cut)

    def copy(self, index):
        here = self.here(index)
        return pltpu.make_async_copy(
            self.source.at[here], self.target.at[here], self.sems.at[self.base + index]
        )


def mask_of(me_ref, picked):
    row = lax.broadcasted_iota(jnp.int32, (LANES, LANES), 0)
    mine = jnp.where(row == me_ref[0], 1.0, 0.0).astype(jnp.bfloat16)
    return contract(picked, mine, 1, 0)


def spread(lanes, width):
    return jnp.concatenate([lanes] * (width // LANES), axis=1)


def rounded(array):
    return array.astype(jnp.bfloat16).astype(jnp.float32)


def inner_terms(gate_pre, up_pre, hidden_grad):
    sigmoid_gate = jax.nn.sigmoid(gate_pre)
    activation = gate_pre * sigmoid_gate
    hidden = activation * up_pre
    gate_grad = hidden_grad * up_pre * sigmoid_gate * (1.0 + gate_pre * (1.0 - sigmoid_gate))
    up_grad = hidden_grad * activation
    half = jnp.bfloat16
    return hidden, gate_grad.astype(half), up_grad.astype(half)


def project_start(copies, tok, rows_in, sources, weights):
    width = rows_in.shape[1]
    tile = 2 * FF_TILE if width % (2 * FF_TILE) == 0 else width
    blocks = []
    for start in range(0, width, tile):
        cut = pl.ds(start, tile)
        here, at = ([], 0)
        for part in tok:
            rows = pl.ds(at, part.shape[0])
            here.append(copies.start(part.at[:, cut], rows_in.at[rows, cut]))
            at += part.shape[0]
        for source, weight in zip(sources, weights):
            here.append(copies.start(source.at[0, cut, :], weight.at[cut, :]))
        blocks.append((slice(start, start + tile), here))
    return blocks


def project(blocks, rows_in, targets, weights):
    for cut, here in blocks:
        wait(here)
        for target, weight in zip(targets, weights):
            value = contract(rows_in[:, cut], weight[cut, :], 1, 0)
            if cut.start == 0:
                target[...] = value
            else:
                target[...] += value


def backward(grad_here, rows_grad, hidden_grad, weight):
    wait(grad_here)

    def body(index):
        weight.copy(index).wait()
        cut = weight.here(index)[0]
        rows = rows_grad[:, : weight.target.shape[1]]
        hidden_grad[:, cut] = contract(rows, weight.target[cut, :], 1, 1)

    loop(weight.count, body)


def row_cut(index):
    start = index * ROW_TILE
    return pl.ds(start if isinstance(index, int) else pl.multiple_of(start, ROW_TILE), ROW_TILE)


def expert_kernel(parts, me_ref, place_ref, gate_all, *refs):
    tok, grad, sources = (refs[:parts], refs[parts : 2 * parts], refs[2 * parts : 2 * parts + 3])
    refs = refs[2 * parts + 3 :]
    sum_outs, scaled_outs = (refs[:parts], refs[parts : parts + 3])
    rows_in, rows_grad, gate_pre, up_pre, hidden_grad, *refs = refs[parts + 3 :]
    wg, wu, wd, gate_grad, up_grad, hs, gs, us, sums, column, gate, sems = refs
    copies = Copies(sems)
    width = wg.shape[0]
    rows = gate_pre.shape[0]
    ff_width = wd.shape[0]
    blocks = project_start(copies, tok, rows_in, sources, (wg, wu))
    grad_here = copies.stack(grad, rows_grad)
    grad_here.append(copies.start(gate_all.at[pl.ds(0, rows), :], gate))
    down = Tiles(copies, sources[2].at[0], wd, 0, FF_TILE)
    project(blocks, rows_in, (gate_pre, up_pre), (wg, wu))
    backward(grad_here, rows_grad, hidden_grad, down)
    column[...] = mask_of(me_ref, rows_grad[:, width : width + LANES])
    gate[...] *= column[...]

    def terms(index):
        cut = row_cut(index)
        values = inner_terms(gate_pre[cut, :], up_pre[cut, :], hidden_grad[cut, :])
        gate_grad[cut, :] = values[1]
        up_grad[cut, :] = values[2]
        sent = spread(rounded(gate[cut, :]), ff_width)
        for value, target in zip(values, (hs, gs, us)):
            target[cut, :] = (sent * value).astype(jnp.bfloat16)
        product = hidden_grad[cut, :] * values[0]
        column[cut, :] *= sum(product[:, at] for at in tiles(ff_width, LANES))

    loop(rows // ROW_TILE, terms)
    results = [copies.start(source, out) for source, out in zip((hs, gs, us), scaled_outs)]
    ones = jnp.ones((SUBLANES, LANES), jnp.bfloat16)
    high = column[...].astype(jnp.bfloat16)
    low = (column[...] - high.astype(jnp.float32)).astype(jnp.bfloat16)
    score = (contract(ones, high, 1, 1) + contract(ones, low, 1, 1)).astype(jnp.bfloat16)
    score = contract(score, order_matrix(place_ref, round_up(rows, LANES)), 1, 1)
    block = placed([score[:1, at] for at in tiles(score.shape[1], LANES)], sums.shape[0])
    sums[:, width:] = block.astype(sums.dtype)
    chunk = sum_outs[0].shape[0]
    for at in range(0, rows, chunk):
        sums[at : at + chunk, width:] = sums[:chunk, width:]

    tile = 2 * FF_TILE if width % (2 * FF_TILE) == 0 else width

    def products(index):
        cut = pl.ds(pl.multiple_of(index * tile, tile), tile)
        part = contract(gate_grad[...], wg[cut, :], 1, 1)
        part += contract(up_grad[...], wu[cut, :], 1, 1)
        sums[:, cut] = (spread(gate[...], tile) * part).astype(jnp.bfloat16)

    loop(width // tile, products)
    at = 0
    for out in sum_outs:
        here = sums.at[pl.ds(at, out.shape[0]), pl.ds(0, out.shape[1])]
        results.append(copies.start(here, out))
        at += out.shape[0]
    wait(results)


def expert_call(me, gate, place, tok, grad, weights, after):
    rows = sum(part.shape[0] for part in tok)
    width, ff_width = weights[0].shape[1:]
    half = jnp.bfloat16
    narrow = pltpu.VMEM((rows, ff_width), half)
    return kernel_call(
        functools.partial(expert_kernel, len(tok)), (me,), (place,),
        (gate, *tok, *grad, *weights),
        [shape(part.shape[0], width + LANES * (at > 1)) for at, part in enumerate(tok)]
        + [shape(rows, ff_width)] * 3,
        [pltpu.VMEM((rows, width), half), pltpu.VMEM((rows, grad[0].shape[1]), half)]
        + [pltpu.VMEM((rows, ff_width), jnp.float32)] * 3
        + [pltpu.VMEM((width, ff_width), half)] * 2 + [pltpu.VMEM((ff_width, width), half)]
        + [narrow] * 5 + [pltpu.VMEM((rows, width + LANES), half)]
        + [pltpu.VMEM((rows, LANES), jnp.float32)] * 2,
        2 * len(tok) + (len(tok) + 2) * len(tiles(width, 2 * FF_TILE))
        + len(tiles(ff_width, FF_TILE)) + 4,
        len(tok) + 3, after, 5 * rows * width * ff_width,
    )


def placed(rows, height):
    index = lax.broadcasted_iota(jnp.int32, (height, LANES), 0)
    block = jnp.zeros((height, LANES), jnp.float32)
    for at, row in enumerate(rows):
        block = jnp.where(index == at, jnp.broadcast_to(row, block.shape), block)
    return block


def first_rows(block, count):
    block = block.astype(jnp.float32)
    return [block[at : at + 1, :] for at in range(count)]


def order_matrix(place_ref, height):
    count = place_ref.shape[1]
    row = lax.broadcasted_iota(jnp.int32, (height, count), 0)
    return jnp.where(row == place_ref[...], 1.0, 0.0).astype(jnp.bfloat16)


def near_kernel(pieces, keep, got, out, score_out, keep_here, got_here, total, sems):
    copies = Copies(sems)
    wait([copies.start(keep, keep_here), copies.start(got, got_here)])
    width = total.shape[1] - LANES
    total[:, :width] = (
        keep_here[:, :width].astype(jnp.float32) + got_here[:, :width].astype(jnp.float32)
    ).astype(total.dtype)
    scores = first_rows(keep_here[: 2 * SUBLANES, width:], pieces)
    scores += first_rows(got_here[: 2 * SUBLANES, width:], pieces)
    block = placed(scores, total.shape[0]).astype(total.dtype)
    total[:, width:] = block
    score_out[...] = block[: score_out.shape[0]]
    wait([copies.start(total, out)])


def ready_kernel(pieces, others, *refs):
    other_scores, (keep, got, near, across, *refs) = (refs[:others], refs[others:])
    outs, refs = (refs[: len(refs) - 6], refs[len(refs) - 6 :])
    keep_here, got_here, near_here, across_here, made, sems = refs
    copies = Copies(sems)
    wait(
        [
            copies.start(keep, keep_here), copies.start(got, got_here),
            copies.start(near, near_here), copies.start(across, across_here),
        ]
    )
    far = made.shape[0]
    rows = made.shape[1]
    width = keep_here.shape[1]
    scores = first_rows(near_here[: 4 * SUBLANES, width:], 2 * pieces)
    scores += first_rows(across_here[: 4 * SUBLANES, width:], 2 * pieces)
    for other in other_scores:
        scores += first_rows(other[...], 2 * pieces)
    blocks = [placed(scores[at : at + rows], rows) for at in range(0, len(scores), rows)]
    block = jnp.concatenate(blocks, axis=1)
    total = keep_here[...].astype(jnp.float32) + got_here[...].astype(jnp.float32)
    total += across_here[:, :width].astype(jnp.float32)
    results = []
    for k in range(far):
        made[k, :, :width] = total[k * rows : (k + 1) * rows, :].astype(made.dtype)
        made[k, :, width:] = block.astype(made.dtype)
        results.append(copies.start(made.at[k], outs[k]))
    wait(results)


def others_kernel(parts, start, me_ref, gate_all, *refs):
    tok, grad, sources = (refs[:parts], refs[parts : 2 * parts], refs[2 * parts : 2 * parts + 3])
    outs, refs = (refs[2 * parts + 3 : 2 * parts + 6], refs[2 * parts + 6 :])
    rows_in, rows_grad, gate_pre, up_pre, hidden_grad, wg, wu, wd, hs, gs, us, gate, sems = refs
    copies = Copies(sems)
    rows, width = rows_in.shape
    ff_width = wd.shape[0]
    blocks = project_start(copies, tok, rows_in, sources, (wg, wu))
    grad_here = copies.stack(grad, rows_grad)
    grad_here.append(copies.start(gate_all.at[pl.ds(start, rows), :], gate))
    down = Tiles(copies, sources[2].at[0], wd, 0, FF_TILE)
    project(blocks, rows_in, (gate_pre, up_pre), (wg, wu))
    backward(grad_here, rows_grad, hidden_grad, down)
    gate[...] *= mask_of(me_ref, rows_grad[:, width : width + LANES])

    def terms(index):
        cut = row_cut(index)
        values = inner_terms(gate_pre[cut, :], up_pre[cut, :], hidden_grad[cut, :])
        sent = spread(rounded(gate[cut, :]), ff_width)
        for value, target in zip(values, (hs, gs, us)):
            target[cut, :] = (sent * value).astype(jnp.bfloat16)

    loop(rows // ROW_TILE, terms)
    wait([copies.start(source, out) for source, out in zip((hs, gs, us), outs)])


def others_call(me, gate, tok, grad, weights, start, after=()):
    rows = sum(part.shape[0] for part in tok)
    width, ff_width = weights[0].shape[1:]
    half = jnp.bfloat16
    return kernel_call(
        functools.partial(others_kernel, len(tok), start), (me,), (),
        (gate, *tok, *grad, *weights),
        [shape(rows, ff_width)] * 3,
        [pltpu.VMEM((rows, width), half), pltpu.VMEM((rows, grad[0].shape[1]), half)]
        + [pltpu.VMEM((rows, ff_width), jnp.float32)] * 3
        + [pltpu.VMEM((width, ff_width), half)] * 2 + [pltpu.VMEM((ff_width, width), half)]
        + [pltpu.VMEM((rows, ff_width), half)] * 3 + [pltpu.VMEM((rows, LANES), jnp.float32)],
        len(tok) + (len(tok) + 2) * len(tiles(width, 2 * FF_TILE))
        + len(tiles(ff_width, FF_TILE)) + 4,
        3, after, rows * width * ff_width, OTHERS_GRANT,
    )


def weights_kernel(parts, given, steps, group_ref, *refs):
    tok, grad, given_refs = (refs[:parts], refs[parts : 2 * parts], refs[2 * parts :][: 3 * given])
    outs, refs = (refs[2 * parts + 3 * given :][:3], refs[2 * parts + 3 * given + 3 :])
    hs, gs, us, tok_half, grad_all, hidden_half, *tile_out, sems = refs
    copies = Copies(sems)
    width = grad_all.shape[1]
    half = outs[0].shape[1]
    half_ff = outs[2].shape[1]
    blocks = [given_refs[kind * given : (kind + 1) * given] for kind in range(3)]
    mine = pl.ds(pl.multiple_of(group_ref[0] * half, LANES), half)
    gate_here = copies.stack(tok, tok_half, mine) + copies.stack(blocks[1], gs)
    up_here = copies.stack(blocks[2], us)
    down_here = copies.stack(blocks[0], hs) + copies.stack(grad, grad_all, pl.ds(0, width))
    base = copies.count

    def result(which, step):
        tile = tile_out[which].shape[1 if which < 2 else 2]
        at = step * tile if isinstance(step, int) else pl.multiple_of(step * tile, tile)
        cut = pl.ds(at, tile)
        target = outs[which].at[0, cut, :] if which < 2 else outs[which].at[0, :, cut]
        return cut, pltpu.make_async_copy(
            tile_out[which].at[step], target, sems.at[base + which * steps + step]
        )

    def form(which, left, right):
        def body(step):
            cut, copy = result(which, step)
            sides = (left[:, cut], right[...]) if which < 2 else (left[...], right[:, cut])
            tile_out[which][step] = contract(*sides, 0, 0).astype(tile_out[which].dtype)
            copy.start()

        loop(steps, body, rolled=False)

    wait(gate_here)
    form(0, tok_half, gs)
    wait(up_here)
    form(1, tok_half, us)
    wait(down_here)
    if half_ff % LANES == 0:
        place = pl.ds(pl.multiple_of(group_ref[0] * half_ff, LANES), half_ff)
        hidden_half[...] = hs[:, place]
    else:
        for index in range(hs.shape[1] // half_ff):

            @pl.when(group_ref[0] == index)
            def _():
                hidden_half[...] = hs[:, index * half_ff : (index + 1) * half_ff]

    form(2, hidden_half, grad_all)
    wait([result(which, step)[1] for which in range(3) for step in range(steps)])


def weights_call(group, groups, tok, grad, given, dtype, after=()):
    width, ff_width = (tok[0].shape[1], given[0][0].shape[1])
    half, half_ff = (width // groups, ff_width // groups)
    rows = sum(part.shape[0] for part in tok)
    steps = max(s for s in (4, 2, 1) if half % (s * LANES) == 0)
    low = jnp.bfloat16
    scratch = [pltpu.VMEM((rows, ff_width), low)] * 3
    scratch += [
        pltpu.VMEM((rows, half), low),
        pltpu.VMEM((rows, width), low),
        pltpu.VMEM((rows, half_ff), low),
        pltpu.VMEM((steps, half // steps, ff_width), dtype),
        pltpu.VMEM((steps, half // steps, ff_width), dtype),
        pltpu.VMEM((steps, half_ff, width // steps), dtype),
    ]
    return kernel_call(
        functools.partial(weights_kernel, len(tok), len(given), steps), (group,), (),
        (*tok, *grad, *(block[kind] for kind in range(3) for block in given)),
        [
            jax.ShapeDtypeStruct((1, half, ff_width), dtype),
            jax.ShapeDtypeStruct((1, half, ff_width), dtype),
            jax.ShapeDtypeStruct((1, half_ff, width), dtype),
        ],
        scratch, 2 * len(tok) + 3 * len(given) + 3 * steps, 3, after, 3 * rows * half * ff_width,
    )


def router_kernel(parts, me_ref, *refs):
    score_ref, place_ref, logits_all, *tok = refs[: 3 + parts]
    grad_ref, router_ref, rows, logits_ref, sems = refs[3 + parts :]
    copies = Copies(sems)
    logits_here = copies.start(logits_all, logits_ref)
    rows_here = copies.stack(tok, rows)
    logits_here.wait()
    logits = logits_ref[...]
    experts = logits.shape[0]
    row = lax.broadcasted_iota(jnp.int32, (experts, experts), 0)
    column = lax.broadcasted_iota(jnp.int32, (experts, experts), 1)
    unswap = jnp.where((row ^ me_ref[0]) == column, 1.0, 0.0).astype(jnp.bfloat16)
    group = score_ref.shape[2]
    order = order_matrix(place_ref, group)
    score = jnp.concatenate(
        [contract(score_ref[at], order, 1, 0) for at in range(score_ref.shape[0])], axis=1
    )
    score = contract(unswap, score.astype(jnp.bfloat16), 1, 0)
    state = balancer_forward_pass(logits)
    grad = balancer_adjoint_pass(experts * score, *state).astype(jnp.bfloat16)
    grad_ref[...] = grad
    wait(rows_here)
    router_ref[...] = contract(grad, rows[...], 1, 0)


def per_device(tokens, out_grad, expert_ids, router_weight, w_gate, w_up, w_down):
    tok_rows, width = tokens.shape
    experts = router_weight.shape[1]
    groups = lax.axis_size("dp")
    far = lax.axis_size("expert") // 4
    chunk = 2 * far * tok_rows
    me = lax.axis_index("expert").astype(jnp.int32)[None]
    group = lax.axis_index("dp").astype(jnp.int32)[None]

    def along(array):
        return jnp.concatenate([array] + [swap_expert(array, 4 * k) for k in range(1, far)], axis=0)

    tok_line = along(tokens)
    slots = [4 * j + 2 * i + k for i in range(2) for k in range(2) for j in range(far)]
    packed, place = kernel_call(
        functools.partial(pack_kernel, slots), (me,), (expert_ids, tokens, router_weight.T), (),
        [shape(tok_rows, round_up(4 * experts, LANES)), shape(1, 2 * chunk, jnp.int32)], (), 0,
    )
    columns = [out_grad, packed[:, : 4 * experts]]
    for offset in range(1, groups):
        columns.append(swap_group(packed, offset)[:, experts : 4 * experts])
    extra = (3 * groups + 1) * experts
    columns.append(jnp.zeros((tok_rows, round_up(extra, LANES) - extra), jnp.bfloat16))
    grad_line = along(jnp.concatenate(columns, axis=1))
    tok_next = swap_expert(tok_line, 2)
    grad_next = swap_expert(grad_line, 2)
    tok_own = [(tok_line, swap_expert(tok_line, 1)), (tok_next, swap_expert(tok_next, 1))]
    grad_own = [(grad_line, swap_expert(grad_line, 1)), (grad_next, swap_expert(grad_next, 1))]

    tok_parts = [rows for pair in tok_own for rows in pair]
    grad_parts = [rows for pair in grad_own for rows in pair]
    weights = (w_gate, w_up, w_down)

    at_once = 2 * groups * chunk <= ROWS_AT_ONCE

    def moved(parts, offset):
        out = []
        for part in parts:
            part = swap_group(part, offset)
            out += [part, swap_expert(part, 1)]
        return out

    moved_tok = moved((tok_line, tok_next), 1) if at_once else []
    moved_grad = moved((grad_line, grad_next), 1) if at_once else []
    early = [part[: 2 * SUBLANES, :LANES] for part in moved_tok[1:2]]
    extra = grad_line.shape[1] - width
    wide = jnp.float32
    all_rows = 2 * chunk * groups
    gate, logits = kernel_call(
        functools.partial(gate_kernel, len(grad_parts), experts), (me,), (), grad_parts,
        [shape(all_rows, LANES, wide), shape(experts, all_rows, wide)],
        [
            pltpu.VMEM((2 * chunk, extra), jnp.bfloat16), pltpu.VMEM((all_rows, LANES), wide),
            pltpu.VMEM((experts, all_rows), wide),
        ],
        len(grad_parts) + 2, 2, early,
    )
    pieces = round_up(2 * chunk, LANES) // LANES

    keep0, send0, keep1, send1, *scaled = expert_call(
        me, gate, place, tok_parts, grad_parts, weights, moved_tok[3:4]
    )
    given = [scaled]
    got1, got0 = (swap_expert(send1, 1), swap_expert(send0, 1))
    near, near_score = kernel_call(
        functools.partial(near_kernel, pieces), (), (), (keep1, got1),
        [shape(*keep1.shape), shape(round_up(2 * pieces, 2 * SUBLANES), LANES)],
        [pltpu.VMEM(keep1.shape, keep1.dtype)] * 3, 3, 1, moved_grad[0::2], grant=SMALL_GRANT,
    )
    other_scores = []
    for offset in range(1, groups):
        moved_score = swap_group(near_score, offset)
        other_scores += [moved_score, swap_expert(moved_score, 2)]
    across = swap_expert(near, 2)
    count = 4 * pieces * groups
    behind = round_up(count, tok_rows) // tok_rows * LANES
    ready = kernel_call(
        functools.partial(ready_kernel, pieces, len(other_scores)), (), other_scores,
        (keep0, got0, near, across), [shape(tok_rows, width + behind)] * far,
        [pltpu.VMEM(keep0.shape, keep0.dtype)] * 2 + [pltpu.VMEM(near.shape, near.dtype)] * 2
        + [pltpu.VMEM((far, tok_rows, width + behind), near.dtype)], 4 + far, far, grant=SMALL_GRANT,
    )
    arrived = [ready[0]] + [swap_expert(ready[k], 4 * k) for k in range(1, far)]
    row_sum = sum(part[:, :width].astype(jnp.float32) for part in arrived)
    score = [
        jnp.concatenate([part[:, at : at + LANES] for at in range(width, width + behind, LANES)])
        for part in arrived
    ]
    score = jnp.stack([part[:count].reshape(groups, 4, pieces * LANES) for part in score], axis=1)
    score = score.reshape(groups, experts, pieces * LANES)
    to_send = ready[1:]

    token_rows = list(tok_parts)
    totals = None
    if not at_once:
        totals = weights_call(group, groups, tok_parts, grad_parts, given, jnp.float32)
        tok_parts, grad_parts, given = ([], [], [])
    for offset in range(1, groups):
        if not at_once:
            (tok_line, tok_next, grad_line, grad_next), totals = lax.optimization_barrier(
                ((tok_line, tok_next, grad_line, grad_next), totals)
            )
            moved_tok = moved((tok_line, tok_next), offset)
            moved_grad = moved((grad_line, grad_next), offset)
        token_rows += moved_tok
        fresh = others_call(me, gate, moved_tok, moved_grad, weights, 2 * chunk * offset)
        terms = weights_call(
            group, groups, tok_parts + moved_tok, grad_parts + moved_grad, given + [fresh],
            jnp.bfloat16 if at_once else jnp.float32, to_send,
        )
        totals = terms if totals is None else [t + u for t, u in zip(totals, terms)]
    final = [t.astype(jnp.bfloat16) for t in totals]

    logit_grad, grad_router = kernel_call(
        functools.partial(router_kernel, len(token_rows)), (me,), (score, place),
        (logits, *token_rows),
        [shape(*logits.shape), shape(experts, width, jnp.float32)],
        [pltpu.VMEM((logits.shape[1], width), jnp.bfloat16), pltpu.VMEM(logits.shape, wide)],
        len(token_rows) + 1,
    )
    row_sum = row_sum + contract(logit_grad[:, :tok_rows], router_weight, 0, 1)
    return (row_sum.astype(jnp.bfloat16), grad_router.T, *final)


def solution(mesh):
    in_specs = (
        P(("dp", "expert"), None),
        P(("dp", "expert"), None),
        P(("dp", "expert"), None),
        P(),
        P("expert", None, None),
        P("expert", None, None),
        P("expert", None, None),
    )
    out_specs = (
        P(("dp", "expert"), None),
        P(),
        P("expert", "dp", None),
        P("expert", "dp", None),
        P("expert", "dp", None),
    )
    return jax.shard_map(
        per_device, mesh=mesh, in_specs=in_specs, out_specs=out_specs, check_vma=False
    )
```

```python
import functools

import jax
import jax.numpy as jnp
from jax import lax
from jax.experimental import pallas as pl
from jax.experimental.pallas import tpu as pltpu
from jax.sharding import PartitionSpec as P

PASSES = 3
LANES = 128
SUBLANES = 8
FF_TILE = 256
ROW_TILE = 32
GRANT = 53 << 20
SMALL_GRANT = 24 << 20
OTHERS_GRANT = 54 << 20
ROWS_AT_ONCE = 1024


def swap_expert(array, offset):
    size = lax.axis_size("expert")
    return lax.ppermute(array, "expert", [(i, i ^ offset) for i in range(size)])


def swap_group(array, offset):
    size = lax.axis_size("dp")
    return lax.ppermute(array, "dp", [(i, i ^ offset) for i in range(size)])


def contract(left, right, left_dim, right_dim):
    return lax.dot_general(
        left, right, (((left_dim,), (right_dim,)), ((), ())), preferred_element_type=jnp.float32
    )


def balancer_forward_pass(logits):
    densities = [jnp.exp(logits)]
    quotients, column_totals, row_totals = ([], [], [])
    for _ in range(PASSES):
        column_sum = jnp.sum(densities[-1], axis=1, keepdims=True)
        quotient = densities[-1] / column_sum
        row_sum = jnp.sum(quotient, axis=0, keepdims=True)
        densities.append(quotient / row_sum)
        quotients.append(quotient)
        column_totals.append(column_sum)
        row_totals.append(row_sum)
    return (densities, quotients, column_totals, row_totals)


def balancer_adjoint_pass(density_gradient, densities, quotients, column_totals, row_totals):
    for repeat in reversed(range(PASSES)):
        inner = jnp.sum(density_gradient * densities[repeat + 1], axis=0, keepdims=True)
        quotient_grad = (density_gradient - inner) / row_totals[repeat]
        shared = jnp.sum(quotient_grad * quotients[repeat], axis=1, keepdims=True)
        density_gradient = (quotient_grad - shared) / column_totals[repeat]
    return density_gradient * densities[0]


def round_up(value, unit):
    return -(-value // unit) * unit


def pack_kernel(slots, me_ref, ids_ref, tok, router, out, place_ref, tok_ref, router_ref, sems):
    copies = Copies(sems)
    operands_here = [copies.start(tok, tok_ref), copies.start(router, router_ref)]
    experts = router_ref.shape[0]
    rows = tok_ref.shape[0]
    at = lax.broadcasted_iota(jnp.int32, place_ref.shape, 1)
    place = jnp.zeros(place_ref.shape, jnp.int32)
    for index, offset in enumerate(slots):
        first = index * rows
        here = (at >= first) & (at < first + rows)
        place = jnp.where(here, (me_ref[0] ^ offset) * rows + at - first, place)
    place_ref[...] = place
    wait(operands_here)
    rest = contract(tok_ref[...], router_ref[...], 1, 1)
    lane = lax.broadcasted_iota(jnp.int32, out.shape, 1)
    packed = jnp.zeros(out.shape, jnp.float32)
    for pick in range(ids_ref.shape[1]):
        packed += jnp.where(lane == ids_ref[:, pick : pick + 1], 1.0, 0.0)
    row = lax.broadcasted_iota(jnp.int32, (experts, out.shape[1]), 0)
    column = lax.broadcasted_iota(jnp.int32, (experts, out.shape[1]), 1)
    for term in range(1, 4):
        part = rest.astype(jnp.bfloat16)
        rest = rest - part.astype(jnp.float32)
        place = jnp.where(column == row + term * experts, 1.0, 0.0).astype(jnp.bfloat16)
        packed += contract(part, place, 1, 0)
    out[...] = packed.astype(jnp.bfloat16)


def gate_kernel(parts, experts, me_ref, *refs):
    grad, gate_out, logits_out = (refs[:parts], *refs[parts : parts + 2])
    packed, gate_ref, logits_ref, sems = refs[parts + 2 :]
    copies = Copies(sems)
    extra = packed.shape[1]
    wait(copies.stack(grad, packed, pl.ds(grad[0].shape[1] - extra, extra)))
    turned = jnp.transpose(packed[...].astype(jnp.float32))
    columns = []
    for group in range(logits_ref.shape[1] // packed.shape[0]):
        at = (3 * group + 1) * experts
        terms = [turned[at + i * experts : at + (i + 1) * experts] for i in range(3)]
        columns.append(terms[0] + terms[1] + terms[2])
    logits = jnp.concatenate(columns, axis=1)
    logits_ref[...] = logits
    results = [copies.start(logits_ref, logits_out)]
    gates = experts * balancer_forward_pass(logits)[0][-1]
    row = lax.broadcasted_iota(jnp.int32, gates.shape, 0)
    mine = jnp.sum(jnp.where(row == me_ref[0], gates, 0.0), axis=0, keepdims=True)
    gate_ref[...] = jnp.transpose(jnp.broadcast_to(mine, (LANES, gates.shape[1])))
    wait([*results, copies.start(gate_ref, gate_out)])


def kernel_call(
    kernel, scalars, small, large, out_shape, scratch, copies, large_outs=0, after=(), macs=10**6, grant=GRANT
):
    whole = pl.BlockSpec(memory_space=pltpu.VMEM)
    outside = pl.BlockSpec(memory_space=pltpu.HBM)
    inputs = len(scalars) + len(small) + len(large)

    def body(*refs):
        kernel(*refs[:inputs], *refs[inputs + len(after) :])

    return pl.pallas_call(
        body,
        in_specs=[pl.BlockSpec(memory_space=pltpu.SMEM)] * len(scalars)
        + [whole] * len(small)
        + [outside] * (len(large) + len(after)),
        out_specs=[outside] * large_outs + [whole] * (len(out_shape) - large_outs),
        out_shape=out_shape,
        scratch_shapes=[*scratch] + [pltpu.SemaphoreType.DMA((copies,))] * (copies > 0),
        compiler_params=pltpu.CompilerParams(vmem_limit_bytes=grant),
        cost_estimate=pl.CostEstimate(
            flops=2 * macs, bytes_accessed=macs // 200, transcendentals=macs // 10000
        ),
    )(*scalars, *small, *large, *after)


def shape(rows, columns, dtype=jnp.bfloat16):
    return jax.ShapeDtypeStruct((rows, columns), dtype)


def tiles(extent, tile):
    tile = tile if extent % tile == 0 else extent
    return [slice(at, at + tile) for at in range(0, extent, tile)]


class Copies:
    def __init__(self, sems):
        self.sems, self.count = (sems, 0)

    def start(self, source, target):
        copy = pltpu.make_async_copy(source, target, self.sems.at[self.count])
        self.count += 1
        copy.start()
        return copy

    def stack(self, parts, target, columns=slice(None)):
        started, at = ([], 0)
        for part in parts:
            rows = part.shape[0]
            started.append(self.start(part.at[:, columns], target.at[pl.ds(at, rows), :]))
            at += rows
        return started


def wait(copies):
    for copy in copies:
        copy.wait()


def loop(count, body, rolled=True):
    if not rolled:
        for index in range(count):
            body(index)
        return

    def step(index, carry):
        body(index)
        return carry

    lax.fori_loop(0, count, step, 0)


class Tiles:
    def __init__(self, copies, source, target, dim, tile):
        extent = target.shape[dim]
        self.tile = tile if extent % tile == 0 else extent
        self.count = extent // self.tile
        self.source, self.target, self.dim = (source, target, dim)
        self.sems, self.base = (copies.sems, copies.count)
        copies.count += self.count
        for index in range(self.count):
            self.copy(index).start()

    def here(self, index):
        start = index * self.tile
        if not isinstance(index, int):
            start = pl.multiple_of(start, self.tile)
        cut = pl.ds(start, self.tile)
        return (cut, slice(None)) if self.dim == 0 else (slice(None), cut)

    def copy(self, index):
        here = self.here(index)
        return pltpu.make_async_copy(
            self.source.at[here], self.target.at[here], self.sems.at[self.base + index]
        )


def mask_of(me_ref, picked):
    row = lax.broadcasted_iota(jnp.int32, (LANES, LANES), 0)
    mine = jnp.where(row == me_ref[0], 1.0, 0.0).astype(jnp.bfloat16)
    return contract(picked, mine, 1, 0)


def spread(lanes, width):
    return jnp.concatenate([lanes] * (width // LANES), axis=1)


def rounded(array):
    return array.astype(jnp.bfloat16).astype(jnp.float32)


def inner_terms(gate_pre, up_pre, hidden_grad):
    sigmoid_gate = jax.nn.sigmoid(gate_pre)
    activation = gate_pre * sigmoid_gate
    hidden = activation * up_pre
    gate_grad = hidden_grad * up_pre * sigmoid_gate * (1.0 + gate_pre * (1.0 - sigmoid_gate))
    up_grad = hidden_grad * activation
    half = jnp.bfloat16
    return hidden, gate_grad.astype(half), up_grad.astype(half)


def project_start(copies, tok, rows_in, sources, weights):
    width = rows_in.shape[1]
    tile = 2 * FF_TILE if width % (2 * FF_TILE) == 0 else width
    blocks = []
    for start in range(0, width, tile):
        cut = pl.ds(start, tile)
        here, at = ([], 0)
        for part in tok:
            rows = pl.ds(at, part.shape[0])
            here.append(copies.start(part.at[:, cut], rows_in.at[rows, cut]))
            at += part.shape[0]
        for source, weight in zip(sources, weights):
            here.append(copies.start(source.at[0, cut, :], weight.at[cut, :]))
        blocks.append((slice(start, start + tile), here))
    return blocks


def project(blocks, rows_in, targets, weights):
    for cut, here in blocks:
        wait(here)
        for target, weight in zip(targets, weights):
            value = contract(rows_in[:, cut], weight[cut, :], 1, 0)
            if cut.start == 0:
                target[...] = value
            else:
                target[...] += value


def backward(grad_here, rows_grad, hidden_grad, weight):
    wait(grad_here)

    def body(index):
        weight.copy(index).wait()
        cut = weight.here(index)[0]
        rows = rows_grad[:, : weight.target.shape[1]]
        hidden_grad[:, cut] = contract(rows, weight.target[cut, :], 1, 1)

    loop(weight.count, body)


def row_cut(index):
    start = index * ROW_TILE
    return pl.ds(start if isinstance(index, int) else pl.multiple_of(start, ROW_TILE), ROW_TILE)


def expert_kernel(parts, me_ref, place_ref, gate_all, *refs):
    tok, grad, sources = (refs[:parts], refs[parts : 2 * parts], refs[2 * parts : 2 * parts + 3])
    refs = refs[2 * parts + 3 :]
    sum_outs, scaled_outs = (refs[:parts], refs[parts : parts + 3])
    rows_in, rows_grad, gate_pre, up_pre, hidden_grad, *refs = refs[parts + 3 :]
    wg, wu, wd, gate_grad, up_grad, hs, gs, us, sums, column, gate, sems = refs
    copies = Copies(sems)
    width = wg.shape[0]
    rows = gate_pre.shape[0]
    ff_width = wd.shape[0]
    blocks = project_start(copies, tok, rows_in, sources, (wg, wu))
    grad_here = copies.stack(grad, rows_grad)
    grad_here.append(copies.start(gate_all.at[pl.ds(0, rows), :], gate))
    down = Tiles(copies, sources[2].at[0], wd, 0, FF_TILE)
    project(blocks, rows_in, (gate_pre, up_pre), (wg, wu))
    backward(grad_here, rows_grad, hidden_grad, down)
    column[...] = mask_of(me_ref, rows_grad[:, width : width + LANES])
    gate[...] *= column[...]

    def terms(index):
        cut = row_cut(index)
        values = inner_terms(gate_pre[cut, :], up_pre[cut, :], hidden_grad[cut, :])
        gate_grad[cut, :] = values[1]
        up_grad[cut, :] = values[2]
        sent = spread(rounded(gate[cut, :]), ff_width)
        for value, target in zip(values, (hs, gs, us)):
            target[cut, :] = (sent * value).astype(jnp.bfloat16)
        product = hidden_grad[cut, :] * values[0]
        column[cut, :] *= sum(product[:, at] for at in tiles(ff_width, LANES))

    loop(rows // ROW_TILE, terms)
    results = [copies.start(source, out) for source, out in zip((hs, gs, us), scaled_outs)]
    ones = jnp.ones((SUBLANES, LANES), jnp.bfloat16)
    high = column[...].astype(jnp.bfloat16)
    low = (column[...] - high.astype(jnp.float32)).astype(jnp.bfloat16)
    score = (contract(ones, high, 1, 1) + contract(ones, low, 1, 1)).astype(jnp.bfloat16)
    score = contract(score, order_matrix(place_ref, round_up(rows, LANES)), 1, 1)
    block = placed([score[:1, at] for at in tiles(score.shape[1], LANES)], sums.shape[0])
    sums[:, width:] = block.astype(sums.dtype)
    chunk = sum_outs[0].shape[0]
    for at in range(0, rows, chunk):
        sums[at : at + chunk, width:] = sums[:chunk, width:]

    tile = 2 * FF_TILE if width % (2 * FF_TILE) == 0 else width

    def products(index):
        cut = pl.ds(pl.multiple_of(index * tile, tile), tile)
        part = contract(gate_grad[...], wg[cut, :], 1, 1)
        part += contract(up_grad[...], wu[cut, :], 1, 1)
        sums[:, cut] = (spread(gate[...], tile) * part).astype(jnp.bfloat16)

    loop(width // tile, products)
    at = 0
    for out in sum_outs:
        here = sums.at[pl.ds(at, out.shape[0]), pl.ds(0, out.shape[1])]
        results.append(copies.start(here, out))
        at += out.shape[0]
    wait(results)


def expert_call(me, gate, place, tok, grad, weights, after):
    rows = sum(part.shape[0] for part in tok)
    width, ff_width = weights[0].shape[1:]
    half = jnp.bfloat16
    narrow = pltpu.VMEM((rows, ff_width), half)
    return kernel_call(
        functools.partial(expert_kernel, len(tok)), (me,), (place,),
        (gate, *tok, *grad, *weights),
        [shape(part.shape[0], width + LANES * (at > 1)) for at, part in enumerate(tok)]
        + [shape(rows, ff_width)] * 3,
        [pltpu.VMEM((rows, width), half), pltpu.VMEM((rows, grad[0].shape[1]), half)]
        + [pltpu.VMEM((rows, ff_width), jnp.float32)] * 3
        + [pltpu.VMEM((width, ff_width), half)] * 2 + [pltpu.VMEM((ff_width, width), half)]
        + [narrow] * 5 + [pltpu.VMEM((rows, width + LANES), half)]
        + [pltpu.VMEM((rows, LANES), jnp.float32)] * 2,
        2 * len(tok) + (len(tok) + 2) * len(tiles(width, 2 * FF_TILE))
        + len(tiles(ff_width, FF_TILE)) + 4,
        len(tok) + 3, after, 5 * rows * width * ff_width,
    )


def placed(rows, height):
    index = lax.broadcasted_iota(jnp.int32, (height, LANES), 0)
    block = jnp.zeros((height, LANES), jnp.float32)
    for at, row in enumerate(rows):
        block = jnp.where(index == at, jnp.broadcast_to(row, block.shape), block)
    return block


def first_rows(block, count):
    block = block.astype(jnp.float32)
    return [block[at : at + 1, :] for at in range(count)]


def order_matrix(place_ref, height):
    count = place_ref.shape[1]
    row = lax.broadcasted_iota(jnp.int32, (height, count), 0)
    return jnp.where(row == place_ref[...], 1.0, 0.0).astype(jnp.bfloat16)


def near_kernel(pieces, keep, got, out, score_out, keep_here, got_here, total, sems):
    copies = Copies(sems)
    wait([copies.start(keep, keep_here), copies.start(got, got_here)])
    width = total.shape[1] - LANES
    total[:, :width] = (
        keep_here[:, :width].astype(jnp.float32) + got_here[:, :width].astype(jnp.float32)
    ).astype(total.dtype)
    scores = first_rows(keep_here[: 2 * SUBLANES, width:], pieces)
    scores += first_rows(got_here[: 2 * SUBLANES, width:], pieces)
    block = placed(scores, total.shape[0]).astype(total.dtype)
    total[:, width:] = block
    score_out[...] = block[: score_out.shape[0]]
    wait([copies.start(total, out)])


def ready_kernel(pieces, others, *refs):
    other_scores, (keep, got, near, across, *refs) = (refs[:others], refs[others:])
    outs, refs = (refs[: len(refs) - 6], refs[len(refs) - 6 :])
    keep_here, got_here, near_here, across_here, made, sems = refs
    copies = Copies(sems)
    wait(
        [
            copies.start(keep, keep_here), copies.start(got, got_here),
            copies.start(near, near_here), copies.start(across, across_here),
        ]
    )
    far = made.shape[0]
    rows = made.shape[1]
    width = keep_here.shape[1]
    scores = first_rows(near_here[: 4 * SUBLANES, width:], 2 * pieces)
    scores += first_rows(across_here[: 4 * SUBLANES, width:], 2 * pieces)
    for other in other_scores:
        scores += first_rows(other[...], 2 * pieces)
    blocks = [placed(scores[at : at + rows], rows) for at in range(0, len(scores), rows)]
    block = jnp.concatenate(blocks, axis=1)
    total = keep_here[...].astype(jnp.float32) + got_here[...].astype(jnp.float32)
    total += across_here[:, :width].astype(jnp.float32)
    results = []
    for k in range(far):
        made[k, :, :width] = total[k * rows : (k + 1) * rows, :].astype(made.dtype)
        made[k, :, width:] = block.astype(made.dtype)
        results.append(copies.start(made.at[k], outs[k]))
    wait(results)


def others_kernel(parts, start, me_ref, gate_all, *refs):
    tok, grad, sources = (refs[:parts], refs[parts : 2 * parts], refs[2 * parts : 2 * parts + 3])
    outs, refs = (refs[2 * parts + 3 : 2 * parts + 6], refs[2 * parts + 6 :])
    rows_in, rows_grad, gate_pre, up_pre, hidden_grad, wg, wu, wd, hs, gs, us, gate, sems = refs
    copies = Copies(sems)
    rows, width = rows_in.shape
    ff_width = wd.shape[0]
    blocks = project_start(copies, tok, rows_in, sources, (wg, wu))
    grad_here = copies.stack(grad, rows_grad)
    grad_here.append(copies.start(gate_all.at[pl.ds(start, rows), :], gate))
    down = Tiles(copies, sources[2].at[0], wd, 0, FF_TILE)
    project(blocks, rows_in, (gate_pre, up_pre), (wg, wu))
    backward(grad_here, rows_grad, hidden_grad, down)
    gate[...] *= mask_of(me_ref, rows_grad[:, width : width + LANES])

    def terms(index):
        cut = row_cut(index)
        values = inner_terms(gate_pre[cut, :], up_pre[cut, :], hidden_grad[cut, :])
        sent = spread(rounded(gate[cut, :]), ff_width)
        for value, target in zip(values, (hs, gs, us)):
            target[cut, :] = (sent * value).astype(jnp.bfloat16)

    loop(rows // ROW_TILE, terms)
    wait([copies.start(source, out) for source, out in zip((hs, gs, us), outs)])


def others_call(me, gate, tok, grad, weights, start, after=()):
    rows = sum(part.shape[0] for part in tok)
    width, ff_width = weights[0].shape[1:]
    half = jnp.bfloat16
    return kernel_call(
        functools.partial(others_kernel, len(tok), start), (me,), (),
        (gate, *tok, *grad, *weights),
        [shape(rows, ff_width)] * 3,
        [pltpu.VMEM((rows, width), half), pltpu.VMEM((rows, grad[0].shape[1]), half)]
        + [pltpu.VMEM((rows, ff_width), jnp.float32)] * 3
        + [pltpu.VMEM((width, ff_width), half)] * 2 + [pltpu.VMEM((ff_width, width), half)]
        + [pltpu.VMEM((rows, ff_width), half)] * 3 + [pltpu.VMEM((rows, LANES), jnp.float32)],
        len(tok) + (len(tok) + 2) * len(tiles(width, 2 * FF_TILE))
        + len(tiles(ff_width, FF_TILE)) + 4,
        3, after, rows * width * ff_width, OTHERS_GRANT,
    )


def weights_kernel(parts, given, steps, group_ref, *refs):
    tok, grad, given_refs = (refs[:parts], refs[parts : 2 * parts], refs[2 * parts :][: 3 * given])
    outs, refs = (refs[2 * parts + 3 * given :][:3], refs[2 * parts + 3 * given + 3 :])
    hs, gs, us, tok_half, grad_all, hidden_half, *tile_out, sems = refs
    copies = Copies(sems)
    width = grad_all.shape[1]
    half = outs[0].shape[1]
    half_ff = outs[2].shape[1]
    blocks = [given_refs[kind * given : (kind + 1) * given] for kind in range(3)]
    mine = pl.ds(pl.multiple_of(group_ref[0] * half, LANES), half)
    gate_here = copies.stack(tok, tok_half, mine) + copies.stack(blocks[1], gs)
    up_here = copies.stack(blocks[2], us)
    down_here = copies.stack(blocks[0], hs) + copies.stack(grad, grad_all, pl.ds(0, width))
    base = copies.count

    def result(which, step):
        tile = tile_out[which].shape[1 if which < 2 else 2]
        at = step * tile if isinstance(step, int) else pl.multiple_of(step * tile, tile)
        cut = pl.ds(at, tile)
        target = outs[which].at[0, cut, :] if which < 2 else outs[which].at[0, :, cut]
        return cut, pltpu.make_async_copy(
            tile_out[which].at[step], target, sems.at[base + which * steps + step]
        )

    def form(which, left, right):
        def body(step):
            cut, copy = result(which, step)
            sides = (left[:, cut], right[...]) if which < 2 else (left[...], right[:, cut])
            tile_out[which][step] = contract(*sides, 0, 0).astype(tile_out[which].dtype)
            copy.start()

        loop(steps, body, rolled=False)

    wait(gate_here)
    form(0, tok_half, gs)
    wait(up_here)
    form(1, tok_half, us)
    wait(down_here)
    if half_ff % LANES == 0:
        place = pl.ds(pl.multiple_of(group_ref[0] * half_ff, LANES), half_ff)
        hidden_half[...] = hs[:, place]
    else:
        for index in range(hs.shape[1] // half_ff):

            @pl.when(group_ref[0] == index)
            def _():
                hidden_half[...] = hs[:, index * half_ff : (index + 1) * half_ff]

    form(2, hidden_half, grad_all)
    wait([result(which, step)[1] for which in range(3) for step in range(steps)])


def weights_call(group, groups, tok, grad, given, dtype, after=()):
    width, ff_width = (tok[0].shape[1], given[0][0].shape[1])
    half, half_ff = (width // groups, ff_width // groups)
    rows = sum(part.shape[0] for part in tok)
    steps = max(s for s in (4, 2, 1) if half % (s * LANES) == 0)
    low = jnp.bfloat16
    scratch = [pltpu.VMEM((rows, ff_width), low)] * 3
    scratch += [
        pltpu.VMEM((rows, half), low),
        pltpu.VMEM((rows, width), low),
        pltpu.VMEM((rows, half_ff), low),
        pltpu.VMEM((steps, half // steps, ff_width), dtype),
        pltpu.VMEM((steps, half // steps, ff_width), dtype),
        pltpu.VMEM((steps, half_ff, width // steps), dtype),
    ]
    return kernel_call(
        functools.partial(weights_kernel, len(tok), len(given), steps), (group,), (),
        (*tok, *grad, *(block[kind] for kind in range(3) for block in given)),
        [
            jax.ShapeDtypeStruct((1, half, ff_width), dtype),
            jax.ShapeDtypeStruct((1, half, ff_width), dtype),
            jax.ShapeDtypeStruct((1, half_ff, width), dtype),
        ],
        scratch, 2 * len(tok) + 3 * len(given) + 3 * steps, 3, after, 3 * rows * half * ff_width,
    )


def router_kernel(parts, me_ref, *refs):
    score_ref, place_ref, logits_all, *tok = refs[: 3 + parts]
    grad_ref, router_ref, rows, logits_ref, sems = refs[3 + parts :]
    copies = Copies(sems)
    logits_here = copies.start(logits_all, logits_ref)
    rows_here = copies.stack(tok, rows)
    logits_here.wait()
    logits = logits_ref[...]
    experts = logits.shape[0]
    row = lax.broadcasted_iota(jnp.int32, (experts, experts), 0)
    column = lax.broadcasted_iota(jnp.int32, (experts, experts), 1)
    unswap = jnp.where((row ^ me_ref[0]) == column, 1.0, 0.0).astype(jnp.bfloat16)
    group = score_ref.shape[2]
    order = order_matrix(place_ref, group)
    score = jnp.concatenate(
        [contract(score_ref[at], order, 1, 0) for at in range(score_ref.shape[0])], axis=1
    )
    score = contract(unswap, score.astype(jnp.bfloat16), 1, 0)
    state = balancer_forward_pass(logits)
    grad = balancer_adjoint_pass(experts * score, *state).astype(jnp.bfloat16)
    grad_ref[...] = grad
    wait(rows_here)
    router_ref[...] = contract(grad, rows[...], 1, 0)


def per_device(tokens, out_grad, expert_ids, router_weight, w_gate, w_up, w_down):
    tok_rows, width = tokens.shape
    experts = router_weight.shape[1]
    groups = lax.axis_size("dp")
    far = lax.axis_size("expert") // 4
    chunk = 2 * far * tok_rows
    me = lax.axis_index("expert").astype(jnp.int32)[None]
    group = lax.axis_index("dp").astype(jnp.int32)[None]

    def along(array):
        return jnp.concatenate([array] + [swap_expert(array, 4 * k) for k in range(1, far)], axis=0)

    tok_line = along(tokens)
    slots = [4 * j + 2 * i + k for i in range(2) for k in range(2) for j in range(far)]
    packed, place = kernel_call(
        functools.partial(pack_kernel, slots), (me,), (expert_ids,),
        (tokens, router_weight.T),
        [shape(tok_rows, round_up(4 * experts, LANES)), shape(1, 2 * chunk, jnp.int32)],
        [pltpu.VMEM(tokens.shape, tokens.dtype), pltpu.VMEM((experts, width), tokens.dtype)], 2,
    )
    columns = [out_grad, packed[:, : 4 * experts]]
    for offset in range(1, groups):
        columns.append(swap_group(packed, offset)[:, experts : 4 * experts])
    extra = (3 * groups + 1) * experts
    columns.append(jnp.zeros((tok_rows, round_up(extra, LANES) - extra), jnp.bfloat16))
    grad_line = along(jnp.concatenate(columns, axis=1))
    tok_next = swap_expert(tok_line, 2)
    grad_next = swap_expert(grad_line, 2)
    tok_own = [(tok_line, swap_expert(tok_line, 1)), (tok_next, swap_expert(tok_next, 1))]
    grad_own = [(grad_line, swap_expert(grad_line, 1)), (grad_next, swap_expert(grad_next, 1))]

    tok_parts = [rows for pair in tok_own for rows in pair]
    grad_parts = [rows for pair in grad_own for rows in pair]
    weights = (w_gate, w_up, w_down)

    at_once = 2 * groups * chunk <= ROWS_AT_ONCE

    def moved(parts, offset):
        out = []
        for part in parts:
            part = swap_group(part, offset)
            out += [part, swap_expert(part, 1)]
        return out

    moved_tok = moved((tok_line, tok_next), 1) if at_once else []
    moved_grad = moved((grad_line, grad_next), 1) if at_once else []
    early = [part[: 2 * SUBLANES, :LANES] for part in moved_tok[1:2]]
    extra = grad_line.shape[1] - width
    wide = jnp.float32
    all_rows = 2 * chunk * groups
    gate, logits = kernel_call(
        functools.partial(gate_kernel, len(grad_parts), experts), (me,), (), grad_parts,
        [shape(all_rows, LANES, wide), shape(experts, all_rows, wide)],
        [
            pltpu.VMEM((2 * chunk, extra), jnp.bfloat16), pltpu.VMEM((all_rows, LANES), wide),
            pltpu.VMEM((experts, all_rows), wide),
        ],
        len(grad_parts) + 2, 2, early,
    )
    pieces = round_up(2 * chunk, LANES) // LANES

    keep0, send0, keep1, send1, *scaled = expert_call(
        me, gate, place, tok_parts, grad_parts, weights, moved_tok[3:4]
    )
    given = [scaled]
    got1, got0 = (swap_expert(send1, 1), swap_expert(send0, 1))
    near, near_score = kernel_call(
        functools.partial(near_kernel, pieces), (), (), (keep1, got1),
        [shape(*keep1.shape), shape(round_up(2 * pieces, 2 * SUBLANES), LANES)],
        [pltpu.VMEM(keep1.shape, keep1.dtype)] * 3, 3, 1, moved_grad[0::2], grant=SMALL_GRANT,
    )
    other_scores = []
    for offset in range(1, groups):
        moved_score = swap_group(near_score, offset)
        other_scores += [moved_score, swap_expert(moved_score, 2)]
    across = swap_expert(near, 2)
    count = 4 * pieces * groups
    behind = round_up(count, tok_rows) // tok_rows * LANES
    ready = kernel_call(
        functools.partial(ready_kernel, pieces, len(other_scores)), (), other_scores,
        (keep0, got0, near, across), [shape(tok_rows, width + behind)] * far,
        [pltpu.VMEM(keep0.shape, keep0.dtype)] * 2 + [pltpu.VMEM(near.shape, near.dtype)] * 2
        + [pltpu.VMEM((far, tok_rows, width + behind), near.dtype)], 4 + far, far, grant=SMALL_GRANT,
    )
    arrived = [ready[0]] + [swap_expert(ready[k], 4 * k) for k in range(1, far)]
    row_sum = sum(part[:, :width].astype(jnp.float32) for part in arrived)
    score = [
        jnp.concatenate([part[:, at : at + LANES] for at in range(width, width + behind, LANES)])
        for part in arrived
    ]
    score = jnp.stack([part[:count].reshape(groups, 4, pieces * LANES) for part in score], axis=1)
    score = score.reshape(groups, experts, pieces * LANES)
    to_send = ready[1:]

    token_rows = list(tok_parts)
    totals = None
    if not at_once:
        totals = weights_call(group, groups, tok_parts, grad_parts, given, jnp.float32)
        tok_parts, grad_parts, given = ([], [], [])
    for offset in range(1, groups):
        if not at_once:
            (tok_line, tok_next, grad_line, grad_next), totals = lax.optimization_barrier(
                ((tok_line, tok_next, grad_line, grad_next), totals)
            )
            moved_tok = moved((tok_line, tok_next), offset)
            moved_grad = moved((grad_line, grad_next), offset)
        token_rows += moved_tok
        fresh = others_call(me, gate, moved_tok, moved_grad, weights, 2 * chunk * offset)
        terms = weights_call(
            group, groups, tok_parts + moved_tok, grad_parts + moved_grad, given + [fresh],
            jnp.bfloat16 if at_once else jnp.float32, to_send,
        )
        totals = terms if totals is None else [t + u for t, u in zip(totals, terms)]
    final = [t.astype(jnp.bfloat16) for t in totals]

    logit_grad, grad_router = kernel_call(
        functools.partial(router_kernel, len(token_rows)), (me,), (score, place),
        (logits, *token_rows),
        [shape(*logits.shape), shape(experts, width, jnp.float32)],
        [pltpu.VMEM((logits.shape[1], width), jnp.bfloat16), pltpu.VMEM(logits.shape, wide)],
        len(token_rows) + 1,
    )
    row_sum = row_sum + contract(logit_grad[:, :tok_rows], router_weight, 0, 1)
    return (row_sum.astype(jnp.bfloat16), grad_router.T, *final)


def solution(mesh):
    in_specs = (
        P(("dp", "expert"), None),
        P(("dp", "expert"), None),
        P(("dp", "expert"), None),
        P(),
        P("expert", None, None),
        P("expert", None, None),
        P("expert", None, None),
    )
    out_specs = (
        P(("dp", "expert"), None),
        P(),
        P("expert", "dp", None),
        P("expert", "dp", None),
        P("expert", "dp", None),
    )
    return jax.shard_map(
        per_device, mesh=mesh, in_specs=in_specs, out_specs=out_specs, check_vma=False
    )
```
